32 devices in a mesh: dp: 4 (over z), seq: 8 (over y, x, core).
Axes of the slice: x: 2, y: 2, z: 4, core: 2. Of those that a mesh axis runs over, the one named last changes fastest.
Arguments:
- hidden_in: bfloat16 [4, 2048, 1152], P('dp', 'seq'), may hold values from -6 to 6
- lengths: int32 [4, 8], P('dp'), may hold values from 64 to 384, as said below
- timesteps: int32 [4, 8], P('dp'), may hold values from 0 to 999
- head_mask: int32 [4, 2, 8, 16], P('dp'), may hold values 0 or 1
- group_mask: int32 [4, 2, 8, 16], P('dp'), may hold values 0 or 1
- skip_mask: int32 [4, 2, 2048], P('dp', None, 'seq'), may hold values 0 or 1
- modulation_weight: bfloat16 [2, 1152, 6912], P(None, 'dp', 'seq'), may hold values from -0.1875 to 0.1875
- joint_weight: bfloat16 [2, 1152, 3456], P(None, 'dp', 'seq'), may hold values from -0.25 to 0.25
- project_weight: bfloat16 [2, 1152, 1152], P(None, 'dp', 'seq'), may hold values from -0.5 to 0.5
- expand_weight: bfloat16 [2, 1152, 4608], P(None, 'dp', 'seq'), may hold values from -0.1875 to 0.1875
- reduce_weight: bfloat16 [2, 4608, 1152], P(None, 'dp', 'seq'), may hold values from -0.09375 to 0.09375
- cotangent: bfloat16 [4, 2048, 1152], P('dp', 'seq'), may hold values from -6 to 6
Outputs:
- final_state: bfloat16 [4, 2048, 1152], P('dp', 'seq')
- input_grad: float32 [4, 2048, 1152], P('dp', 'seq')
- modulation_grad: float32 [2, 1152, 6912], P(None, 'dp', 'seq')
- joint_grad: float32 [2, 1152, 3456], P(None, 'dp', 'seq')
- project_grad: float32 [2, 1152, 1152], P(None, 'dp', 'seq')
- expand_grad: float32 [2, 1152, 4608], P(None, 'dp', 'seq')
- reduce_grad: float32 [2, 4608, 1152], P(None, 'dp', 'seq')
The draws below stay inside these ranges and needn't reach their ends.
Inputs may be any that keep to these rules, and one draw needn't show every extreme that they name: `lengths`: in every row the crops follow one another from the row's start and padding of 1 to 64 tokens fills the rest. Crop c, for c < 7, ends (c + 1) * 256 + u tokens into the row with 64 <= u <= 128, so every boundary between consecutive blocks of 256 tokens lies inside a crop and a crop lies within two such blocks.
All inputs are finite; a program needn't handle non-finite values. No bound on the sum of `head_mask` or of `group_mask` or of `skip_mask` on one device may be relied on, other than what follows from the above.
Results may differ from the reference program's by a relative error of at most 0.04.
Values may be sent and summed in bfloat16 or wider, within the bound.
No kernel may reach another device: no remote copies, remote signals or barrier semaphores. Data moves between devices by JAX's collectives and lax.ppermute only.
A program may use at most 320 MiB of HBM per device.

```python
import math
import jax
import jax.numpy as jnp
from jax import lax

D = 1152
HEADS = 16
HEAD_DIM = 72
FF = 4608
GROUPS = 16
LAYERS = 2
TOK_DEV = 256
CROPS = 8
ROW = 2048
ROWS = 4


def draw_lengths(key, part):
    key = jax.random.fold_in(key, 11)
    first_key, second_key, third_key = jax.random.split(key, 3)
    shifts = jax.random.randint(first_key, (ROWS, CROPS - 1), TOK_DEV // 4, TOK_DEV // 2 + 1)
    chosen = jax.random.randint(second_key, (), 0, ROWS)
    rows_here = jnp.arange(ROWS, dtype=jnp.int32)
    first_shift = jnp.where(rows_here == chosen, TOK_DEV // 2, shifts[:, 0])
    shifts = jnp.concatenate([first_shift[:, None], shifts[:, 1:]], axis=1)
    padding = jax.random.randint(third_key, (ROWS, 1), 1, TOK_DEV // 4 + 1)
    ends = (jnp.arange(1, CROPS, dtype=jnp.int32) * TOK_DEV)[None, :] + shifts
    starts = jnp.concatenate([jnp.zeros((ROWS, 1), jnp.int32), ends], axis=1)
    closes = jnp.concatenate([ends, ROW - padding], axis=1)
    return (closes - starts).astype(jnp.int32)


def place_ends(drawn, rng, low, largest):
    longest = drawn.shape.index(max(drawn.shape))
    spots = []
    for shift in (0, 1):
        where = [jax.random.randint(jax.random.fold_in(rng, axis), (), 0, length) for axis, length in enumerate(drawn.shape)]
        where[longest] = (where[longest] + shift) % drawn.shape[longest]
        spots.append(tuple(where))
    return drawn.at[spots[0]].set(low).at[spots[1]].set(largest)


def level_of(own_key, dims, cuts, low, top_value):
    loudness, own = 1.0, jax.random.fold_in(own_key, 6)
    for position, blocks in cuts:
        heights = jnp.exp(jax.random.uniform(jax.random.fold_in(own, position), (blocks,), jnp.float32, low / len(cuts), top_value / len(cuts)))
        loudness = loudness * jnp.repeat(heights, dims[position] // blocks).reshape([-1 if axis == position else 1 for axis in range(len(dims))])
    return loudness


def normal_values(stream_key, extent, width, limit, cuts=(), held_as=jnp.bfloat16):
    drawn = width * jax.random.normal(stream_key, extent, jnp.float32)
    if cuts:
        drawn = drawn * level_of(stream_key, extent, cuts, -0.22, 0.18)
    return jnp.clip(drawn, -limit, limit).astype(held_as)


def setup_inputs(seed: int = 0) -> dict:
    key_list = jax.random.split(jax.random.key(seed), 13)
    return {
        "hidden_in": normal_values(key_list[0], (ROWS, ROW, D), 1.0, 6.0, ((0, 4), (1, 8))),
        "lengths": draw_lengths(jax.random.fold_in(key_list[12], 71), 0),
        "timesteps": place_ends(jax.random.randint(key_list[2], (ROWS, CROPS), 0, 1000), jax.random.fold_in(key_list[2], 1), 0, 999).astype(jnp.int32),
        "head_mask": place_ends((jax.random.randint(key_list[3], (ROWS, LAYERS, CROPS, HEADS), 0, 4) < 3).astype(jnp.int32), jax.random.fold_in(key_list[3], 1), 0, 1),
        "group_mask": place_ends((jax.random.randint(key_list[4], (ROWS, LAYERS, CROPS, GROUPS), 0, 4) < 3).astype(jnp.int32), jax.random.fold_in(key_list[4], 1), 0, 1),
        "skip_mask": place_ends((jax.random.randint(key_list[5], (ROWS, LAYERS, ROW), 0, 4) < 3).astype(jnp.int32), jax.random.fold_in(key_list[5], 1), 0, 1),
        "modulation_weight": normal_values(key_list[6], (LAYERS, D, 6 * D), D ** -0.5, 0.1875, ((1, 4), (2, 8))),
        "joint_weight": normal_values(key_list[7], (LAYERS, D, 3 * D), (D // 2) ** -0.5, 0.25, ((1, 4), (2, 8))),
        "project_weight": normal_values(key_list[8], (LAYERS, D, D), (D // 8) ** -0.5, 0.5, ((1, 4), (2, 8))),
        "expand_weight": normal_values(key_list[9], (LAYERS, D, FF), D ** -0.5, 0.1875, ((1, 4), (2, 8))),
        "reduce_weight": normal_values(key_list[10], (LAYERS, FF, D), FF ** -0.5, 0.09375, ((1, 4), (2, 8))),
        "cotangent": normal_values(key_list[11], (ROWS, ROW, D), 1.0, 6.0, ((0, 4), (1, 8))),
    }


@jax.custom_vjp
def low(v):
    return lax.optimization_barrier(v.astype(jnp.bfloat16)).astype(jnp.float32)

@jax.custom_vjp
def low_back(v):
    return v

def low_keep(v):
    return (low(v), None)

def low_pass(kept, grad):
    return (grad,)

def back_keep(v):
    return (v, None)

def back_low(kept, grad):
    return (low(grad),)
low.defvjp(low_keep, low_pass)
low_back.defvjp(back_keep, back_low)
EPS = 1e-06
HIGH = lax.Precision.HIGHEST
NEGATIVE = -1e+30

def layer_norm(stream):
    center = stream - lax.optimization_barrier(jnp.mean(stream, axis=-1, keepdims=True))
    spread = lax.optimization_barrier(jnp.mean(center * center, axis=-1, keepdims=True))
    return center * lax.rsqrt(spread + EPS)

def step_embed(stamps):
    halfway = D // 2
    frequency = jnp.exp(-math.log(10000.0) * jnp.arange(halfway, dtype=jnp.float32) / halfway)
    angles = stamps.astype(jnp.float32)[..., None] * frequency
    return jnp.concatenate([jnp.cos(angles), jnp.sin(angles)], axis=-1)

def attend_row(queries, key_rows, value_rows, segment):
    block_rows = math.gcd(512, ROW)
    query_blocks = queries.reshape(ROW // block_rows, block_rows, HEADS, HEAD_DIM)
    segment_blocks = segment.reshape(ROW // block_rows, block_rows)
    factor = HEAD_DIM ** (-0.5)

    def one_block(item):
        query_part, segment_part = item
        scores = jnp.einsum('qhd,khd->hqk', query_part, key_rows, precision=HIGH) * factor
        scores = low_back(scores)
        allowed = (segment_part[:, None] == segment[None, :])[None]
        masked = jnp.where(allowed, scores, NEGATIVE)
        weights = low(jax.nn.softmax(masked, axis=-1))
        return jnp.einsum('hqk,khd->qhd', weights, value_rows, precision=HIGH)
    result = lax.map(jax.checkpoint(one_block), (query_blocks, segment_blocks))
    return result.reshape(ROW, HEADS, HEAD_DIM)

def block_layer(stream, number, cond, onehot, living, segment, heads_on, groups_on, skips, w_mod, w_joint, w_proj, w_exp, w_red):
    modulation = jnp.einsum('rcd,de->rce', cond, w_mod[number], precision=HIGH)
    tokmod = jnp.einsum('rtc,rce->rte', onehot, modulation, precision=HIGH)
    offset_one, stretch_one, gate_one, offset_two, stretch_two, gate_two = jnp.split(tokmod, 6, axis=-1)
    head_tok = jnp.einsum('rtc,rch->rth', onehot, heads_on[:, number], precision=HIGH)
    group_tok = jnp.einsum('rtc,rcg->rtg', onehot, groups_on[:, number], precision=HIGH)
    channel_tok = jnp.repeat(group_tok, FF // GROUPS, axis=-1)
    keeping = skips[:, number] * living
    normed_one = low(layer_norm(stream) * (1.0 + stretch_one) + offset_one)
    joint = low_back(low(jnp.einsum('rtd,de->rte', normed_one, w_joint[number], precision=HIGH)))
    queries, key_rows, value_rows = jnp.split(joint, 3, axis=-1)
    shape = (ROWS, ROW, HEADS, HEAD_DIM)
    attended = lax.map(lambda item: attend_row(item[0], item[1], item[2], item[3]), (queries.reshape(shape), key_rows.reshape(shape), value_rows.reshape(shape), segment))
    attended = low_back(attended)
    mixed = low((attended * head_tok[..., None]).reshape(ROWS, ROW, D))
    branch = low_back(jnp.einsum('rtd,de->rte', mixed, w_proj[number], precision=HIGH))
    middle = stream + gate_one * branch * living[..., None]
    normed_two = low(layer_norm(middle) * (1.0 + stretch_two) + offset_two)
    pre_act = low_back(jnp.einsum('rtd,df->rtf', normed_two, w_exp[number], precision=HIGH))
    activated = low(jax.nn.gelu(pre_act, approximate=True) * channel_tok)
    feedout = low_back(jnp.einsum('rtf,fd->rtd', activated, w_red[number], precision=HIGH))
    return middle + gate_two * feedout * keeping[..., None]

def reference(hidden_in, lengths, timesteps, head_mask, group_mask, skip_mask, modulation_weight, joint_weight, project_weight, expand_weight, reduce_weight, cotangent):
    places = jnp.arange(ROW, dtype=jnp.int32)
    bounds = jnp.cumsum(lengths, axis=-1).astype(jnp.int32)
    segment = lax.optimization_barrier(jnp.sum((places[None, :, None] >= bounds[:, None, :]).astype(jnp.int32), axis=-1)).astype(jnp.int32)
    onehot = (segment[..., None] == jnp.arange(CROPS, dtype=jnp.int32)).astype(jnp.float32)
    living = (segment < CROPS).astype(jnp.float32)
    cond = low(jax.nn.silu(step_embed(timesteps)))
    heads_on = head_mask.astype(jnp.float32)
    groups_on = group_mask.astype(jnp.float32)
    skips = skip_mask.astype(jnp.float32)

    def forward(stream, w_mod, w_joint, w_proj, w_exp, w_red):
        for number in range(LAYERS):
            stream = block_layer(stream, number, cond, onehot, living, segment, heads_on, groups_on, skips, w_mod, w_joint, w_proj, w_exp, w_red)
        return stream
    final, backward = jax.vjp(forward, hidden_in.astype(jnp.float32), modulation_weight.astype(jnp.float32), joint_weight.astype(jnp.float32), project_weight.astype(jnp.float32), expand_weight.astype(jnp.float32), reduce_weight.astype(jnp.float32))
    grads = backward(cotangent.astype(jnp.float32))
    return (final.astype(jnp.bfloat16), grads[0], grads[1], grads[2], grads[3], grads[4], grads[5])
```

```python
import functools
import math

import jax
import jax.numpy as jnp
import numpy as np
from jax import lax
from jax.experimental import pallas as pl
from jax.experimental.pallas import tpu as pltpu
from jax.sharding import PartitionSpec as P

D = 1152
HEADS = 16
HEAD_DIM = 72
FF = 4608
GROUPS = 16
LAYERS = 2

TP = 4
LANES = 128
LOCAL_HEADS = HEADS // TP
WIDTH = -(-LOCAL_HEADS * HEAD_DIM // LANES) * LANES
AFTER = 128

EPS = 1e-06
HIGH = lax.Precision.HIGHEST
NEGATIVE = -1e30
FACTOR = HEAD_DIM ** (-0.5)
F32 = jnp.float32
BF16 = jnp.bfloat16


def sizes():
    seq = lax.axis_size("seq")
    return seq, seq // TP, lax.axis_size("dp")


def place():
    s = lax.axis_index("seq")
    return s // TP, s % TP


def device_of(unit, groups):
    return (unit % groups) * TP + unit // groups


def unit_table(seq, groups):
    return np.array([(s % TP) * groups + s // TP for s in range(seq)])


def my_unit():
    seq, groups, _ = sizes()
    group, member = place()
    return member * groups + group


def exchange(value, mask):
    seq = lax.axis_size("seq")
    return lax.ppermute(value, "seq", [(i, i ^ mask) for i in range(seq)])


def shifted(value, steps):
    count = lax.axis_size("seq")
    return lax.ppermute(
        value, "seq", [(i, i + steps) for i in range(count) if 0 <= i + steps < count]
    )


def dot(left, right):
    return jnp.dot(left, right, preferred_element_type=F32)


def through_rows(left, right):
    return lax.dot_general(left, right, (((0,), (0,)), ((), ())), preferred_element_type=F32)


def against_cols(left, right):
    return lax.dot_general(left, right, (((1,), (1,)), ((), ())), preferred_element_type=F32)


def spread(mine):
    _, member = place()
    got = {0: mine}
    for mask in range(2, TP, 2):
        got[mask] = exchange(mine, mask)
    for mask in range(0, TP, 2):
        got[mask + 1] = exchange(got[mask], 1)
    whole = jnp.zeros((TP,) + mine.shape, mine.dtype)
    for mask in range(TP):
        whole = lax.dynamic_update_index_in_dim(whole, got[mask], member ^ mask, 0)
    return whole.reshape((TP * mine.shape[0],) + mine.shape[1:])


def collect(parts):
    _, member = place()
    parts = parts.reshape((TP, parts.shape[0] // TP) + parts.shape[1:])

    def pick(mask):
        return lax.dynamic_index_in_dim(parts, member ^ mask, 0, keepdims=False)

    total = None
    for mask in reversed(range(0, TP, 2)):
        pair = pick(mask).astype(F32) + exchange(pick(mask + 1), 1).astype(F32)
        if mask:
            pair = exchange(pair.astype(BF16), mask).astype(F32)
        total = pair if total is None else total + pair
    return total


def kinds_of():
    seq, groups, _ = sizes()
    units = unit_table(seq, groups)
    pairs, kinds = [], np.zeros((3, seq), np.int32)
    for r in range(3):
        targets = [device_of((3 * s + r) % seq, groups) for s in range(seq)]
        pairs.append(list(enumerate(targets)))
        for s in range(seq):
            kinds[r, targets[s]] = (3 * s + r) // seq
    return pairs, jnp.asarray(kinds)[:, lax.axis_index("seq")]


def deal_joint(part):
    pairs, kinds = kinds_of()
    cols = part.shape[-1] // 3
    got = [
        lax.ppermute(part[..., r * cols : (r + 1) * cols], "seq", pairs[r]) for r in range(3)
    ]
    out = []
    for kind in range(3):
        out.append(
            jnp.where(kinds[0] == kind, got[0], jnp.where(kinds[1] == kind, got[1], got[2]))
        )
    return jnp.concatenate(out, axis=-1)


def return_joint(grad):
    pairs, kinds = kinds_of()
    cols = grad.shape[-1] // 3
    own = [grad[..., k * cols : (k + 1) * cols] for k in range(3)]
    back = []
    for r in range(3):
        piece = jnp.where(kinds[r] == 0, own[0], jnp.where(kinds[r] == 1, own[1], own[2]))
        back.append(lax.ppermute(piece, "seq", [(b, a) for a, b in pairs[r]]))
    return jnp.concatenate(back, axis=-1)


def expand_pairs(step):
    seq, groups, planes = sizes()
    ways = seq // planes
    pairs = []
    for s in range(seq):
        q = (s // ways + step) % planes
        pairs.append((s, device_of(planes * (s % ways) + q, groups)))
    return pairs


def deal_expand(part):
    seq, _, planes = sizes()
    ways = seq // planes
    cols = part.shape[-1] // planes
    s = lax.axis_index("seq")
    q_mine = my_unit() % planes
    out = jnp.zeros((planes,) + part.shape[:-1] + (cols,), part.dtype)
    blocks = jnp.stack([part[..., q * cols : (q + 1) * cols] for q in range(planes)])
    for step in range(planes):
        piece = lax.dynamic_index_in_dim(blocks, (s // ways + step) % planes, 0, keepdims=False)
        piece = lax.ppermute(piece, "seq", expand_pairs(step))
        out = lax.dynamic_update_index_in_dim(out, piece, (q_mine - step) % planes, 0)
    return jnp.concatenate([out[d] for d in range(planes)], axis=-1)


def return_expand(grad):
    seq, _, planes = sizes()
    ways = seq // planes
    cols = grad.shape[-1] // planes
    s = lax.axis_index("seq")
    q_mine = my_unit() % planes
    blocks = jnp.stack([grad[..., d * cols : (d + 1) * cols] for d in range(planes)])
    out = jnp.zeros_like(blocks)
    for step in range(planes):
        piece = lax.dynamic_index_in_dim(blocks, (q_mine - step) % planes, 0, keepdims=False)
        piece = lax.ppermute(piece, "seq", [(b, a) for a, b in expand_pairs(step)])
        out = lax.dynamic_update_index_in_dim(out, piece, (s // ways + step) % planes, 0)
    return jnp.concatenate([out[q] for q in range(planes)], axis=-1)


def deal_rows(part):
    seq, groups, _ = sizes()
    rows = part.shape[0] // seq
    chunks = part.reshape(TP, groups, rows, part.shape[1]).transpose(1, 0, 2, 3)
    chunks = lax.all_to_all(
        chunks.reshape(seq, rows, part.shape[1]), "seq", 0, 0, tiled=True
    )
    return jnp.concatenate([chunks[s] for s in range(seq)], axis=-1)


def return_rows(grad):
    seq, groups, _ = sizes()
    rows, cols = grad.shape[0], grad.shape[1] // seq
    chunks = jnp.stack([grad[:, s * cols : (s + 1) * cols] for s in range(seq)])
    chunks = lax.all_to_all(chunks, "seq", 0, 0, tiled=True)
    chunks = chunks.reshape(groups, TP, rows, cols).transpose(1, 0, 2, 3)
    return chunks.reshape(seq * rows, cols)


def fold(part, cols):
    return jnp.concatenate(
        [part[:, k * cols : (k + 1) * cols] for k in range(part.shape[1] // cols)], axis=0
    )


def unfold(part, rows):
    return jnp.concatenate(
        [part[k * rows : (k + 1) * rows] for k in range(part.shape[0] // rows)], axis=1
    )


def ordered(pieces):
    if len(pieces) != 2:
        return pieces
    group, _ = place()
    first, second = pieces
    return [jnp.where(group == 0, first, second), jnp.where(group == 0, second, first)]


def over_groups(part):
    seq, groups, _ = sizes()
    if groups == 1:
        return [part]
    if groups == 2:
        return [part, exchange(part, TP)]
    teams = [[g * TP + t for g in range(groups)] for t in range(TP)]
    every = lax.all_gather(part, "seq", axis_index_groups=teams)
    return [every[g] for g in range(groups)]


def group_sum(pieces):
    seq, groups, _ = sizes()
    if groups == 1:
        return pieces[0]
    if groups == 2:
        return pieces[0] + exchange(pieces[1].astype(BF16), TP).astype(F32)
    teams = [[g * TP + t for g in range(groups)] for t in range(TP)]
    stacked = jnp.stack([piece.astype(BF16) for piece in pieces])
    return lax.psum_scatter(
        stacked, "seq", scatter_dimension=0, axis_index_groups=teams, tiled=False
    ).astype(F32)


def slot_units():
    seq, groups, _ = sizes()
    group, member = place()
    if groups == 2:
        return [member * 2 + group, member * 2 + 1 - group]
    return [member * groups + g for g in range(groups)]


def over_planes(part):
    return lax.all_gather(part, "dp", axis=0, tiled=False)


def attention_weights(packed):
    seq, _, planes = sizes()
    cols = D // seq
    joint = ordered(over_groups(packed[:, :, : 3 * cols].reshape(D, 3 * cols)))
    project = ordered(over_groups(deal_rows(packed[:, :, 3 * cols :].reshape(D, cols))))
    blank = jnp.zeros((D, WIDTH - LOCAL_HEADS * HEAD_DIM), BF16)
    columns = []
    for kind in range(3):
        columns += [piece[:, kind * cols : (kind + 1) * cols] for piece in joint] + [blank]
    return (
        jnp.concatenate(columns, axis=1),
        jnp.concatenate(project + [blank.T], axis=0),
    )


def forward_weights(packed):
    seq, _, planes = sizes()
    height, width = D // planes, FF // seq
    expand = over_groups(packed[:, :height].reshape(D, width))
    rows = FF // (planes * seq)
    reduce = jnp.concatenate([unfold(packed[d, height:], rows) for d in range(planes)], axis=0)
    reduce = over_groups(reduce)
    return jnp.concatenate(expand, axis=1), jnp.concatenate(reduce, axis=0)


def head_tiles(head):
    low = head * HEAD_DIM // LANES * LANES
    high = -(-(head + 1) * HEAD_DIM // LANES) * LANES
    return low, high


def lanes_of(head, shape):
    low, high = head_tiles(head)
    lane = lax.broadcasted_iota(jnp.int32, shape, 1) + low
    return (lane >= head * HEAD_DIM) & (lane < (head + 1) * HEAD_DIM)


def attend_kernel(block, span, q_ref, kv_ref, segq_ref, segk_ref, head_ref, mixed_ref, lse_ref):
    window = pl.ds(pl.multiple_of(pl.program_id(0) * block, block), span)
    allowed = segq_ref[...] == segk_ref[0]
    tiles = [jnp.zeros((block, LANES), F32) for _ in range(WIDTH // LANES)]
    total = jnp.zeros((block, LANES), F32)
    lane = lax.broadcasted_iota(jnp.int32, (block, LANES), 1)
    for head in range(LOCAL_HEADS):
        low, high = head_tiles(head)
        mine = lanes_of(head, (block, high - low))
        query = jnp.where(mine, q_ref[:, low:high], 0)
        scores = against_cols(query, kv_ref[window, low:high]) * FACTOR
        scores = jnp.where(allowed, scores, NEGATIVE)
        highest = jnp.max(scores, axis=-1, keepdims=True)
        weights = jnp.exp(scores - highest)
        sums = jnp.sum(weights, axis=-1, keepdims=True)
        probs = (weights / sums).astype(BF16)
        out = dot(probs, kv_ref[window, WIDTH + low : WIDTH + high])
        out = jnp.where(mine, out, 0.0) * head_ref[:, head : head + 1]
        for k in range(low // LANES, high // LANES):
            at = k * LANES - low
            tiles[k] = tiles[k] + out[:, at : at + LANES]
        total = jnp.where(lane == head, highest + jnp.log(sums), total)
    for k, tile in enumerate(tiles):
        mixed_ref[:, k * LANES : (k + 1) * LANES] = tile.astype(BF16)
    lse_ref[...] = total


def attend_back_kernel(
    block,
    span,
    q_ref,
    kv_ref,
    grad_ref,
    mixed_ref,
    lse_ref,
    segq_ref,
    segk_ref,
    head_ref,
    dq_ref,
    dkv_ref,
    sum_ref,
):
    step = pl.program_id(0)

    @pl.when(step == 0)
    def _():
        sum_ref[...] = jnp.zeros_like(sum_ref)

    window = pl.ds(pl.multiple_of(step * block, block), span)
    allowed = segq_ref[...] == segk_ref[0]
    tiles = [jnp.zeros((block, LANES), F32) for _ in range(WIDTH // LANES)]
    for head in range(LOCAL_HEADS):
        low, high = head_tiles(head)
        mine = lanes_of(head, (block, high - low))
        query = jnp.where(mine, q_ref[:, low:high], 0)
        key = kv_ref[window, low:high]
        value = kv_ref[window, WIDTH + low : WIDTH + high]
        active = head_ref[:, head : head + 1]
        grad = jnp.where(mine, grad_ref[:, low:high].astype(F32) * active, 0.0)
        balance = jnp.sum(grad * mixed_ref[:, low:high].astype(F32), axis=-1, keepdims=True)
        grad = grad.astype(BF16)
        scores = against_cols(query, key) * FACTOR
        probs = jnp.where(allowed, jnp.exp(scores - lse_ref[:, head : head + 1]), 0.0)
        d_value = through_rows(probs.astype(BF16), grad)
        d_probs = against_cols(grad, value)
        d_scores = (probs * (d_probs - balance)).astype(BF16)
        d_query = jnp.where(mine, dot(d_scores, key), 0.0)
        d_key = through_rows(d_scores, query) * FACTOR
        sum_ref[window, low:high] += d_key
        sum_ref[window, WIDTH + low : WIDTH + high] += d_value
        for k in range(low // LANES, high // LANES):
            at = k * LANES - low
            tiles[k] = tiles[k] + d_query[:, at : at + LANES]
    for k, tile in enumerate(tiles):
        dq_ref[:, k * LANES : (k + 1) * LANES] = (tile * FACTOR).astype(BF16)

    @pl.when(step == pl.num_programs(0) - 1)
    def _():
        dkv_ref[...] = sum_ref[...].astype(BF16)


def kernel_params():
    return pltpu.CompilerParams(
        dimension_semantics=("arbitrary",), vmem_limit_bytes=48 * 1024 * 1024
    )


def attend(joint, pairs, segq, segk, heads):
    span = segk.shape[2]
    count = joint.shape[0]
    block = count // segk.shape[0]
    rows = lambda width: pl.BlockSpec((block, width), lambda b: (b, 0))
    whole = lambda array: pl.BlockSpec(array.shape, lambda b: (0, 0))
    return pl.pallas_call(
        functools.partial(attend_kernel, block, span),
        grid=(count // block,),
        in_specs=[
            rows(WIDTH),
            whole(pairs),
            rows(1),
            pl.BlockSpec((1, 1, span), lambda b: (b, 0, 0)),
            rows(LANES),
        ],
        out_specs=[rows(WIDTH), rows(LANES)],
        out_shape=[
            jax.ShapeDtypeStruct((count, WIDTH), BF16),
            jax.ShapeDtypeStruct((count, LANES), F32),
        ],
        compiler_params=kernel_params(),
        cost_estimate=pl.CostEstimate(
            flops=4 * count * span * LANES * LOCAL_HEADS,
            bytes_accessed=count * WIDTH * 8,
            transcendentals=count * span * LOCAL_HEADS,
        ),
        name="attend",
    )(joint, pairs, segq, segk, heads)


def attend_back(joint, pairs, grad, mixed, log_total, segq, segk, heads):
    span = segk.shape[2]
    count = joint.shape[0]
    block = count // segk.shape[0]
    rows = lambda width: pl.BlockSpec((block, width), lambda b: (b, 0))
    whole = lambda shape: pl.BlockSpec(shape, lambda b: (0, 0))
    return pl.pallas_call(
        functools.partial(attend_back_kernel, block, span),
        grid=(count // block,),
        in_specs=[
            rows(WIDTH),
            whole(pairs.shape),
            rows(WIDTH),
            rows(WIDTH),
            rows(LANES),
            rows(1),
            pl.BlockSpec((1, 1, span), lambda b: (b, 0, 0)),
            rows(LANES),
        ],
        out_specs=[rows(WIDTH), whole(pairs.shape)],
        out_shape=[
            jax.ShapeDtypeStruct((count, WIDTH), BF16),
            jax.ShapeDtypeStruct(pairs.shape, BF16),
        ],
        scratch_shapes=[pltpu.VMEM(pairs.shape, F32)],
        compiler_params=kernel_params(),
        cost_estimate=pl.CostEstimate(
            flops=10 * count * span * LANES * LOCAL_HEADS,
            bytes_accessed=count * WIDTH * 20,
            transcendentals=count * span * LOCAL_HEADS,
        ),
        name="attend_back",
    )(joint, pairs, grad, mixed, log_total, segq, segk, heads)


def with_halo(pairs, block):
    _, groups, _ = sizes()
    if groups == 1:
        before = jnp.zeros((block, pairs.shape[1]), pairs.dtype)
        after = jnp.zeros((AFTER, pairs.shape[1]), pairs.dtype)
    else:
        before = shifted(pairs[-block:], TP)
        after = shifted(pairs[:AFTER], -TP)
    return jnp.concatenate([before, pairs, after], axis=0)


def halo_back(d_pairs, block):
    _, groups, _ = sizes()
    own = d_pairs[block:-AFTER]
    if groups == 1:
        return own
    from_above = shifted(d_pairs[:block], -TP).astype(F32)
    from_below = shifted(d_pairs[-AFTER:], TP).astype(F32)
    count = own.shape[0]
    top = (own[:AFTER].astype(F32) + from_below).astype(BF16)
    bottom = (own[-block:].astype(F32) + from_above).astype(BF16)
    return jnp.concatenate([top, own[AFTER : count - block], bottom], axis=0)


def normed(stream):
    center = stream - jnp.mean(stream, axis=-1, keepdims=True)
    scale = lax.rsqrt(jnp.mean(center * center, axis=-1, keepdims=True) + EPS)
    return center * scale, scale


def norm_back(grad, unit, scale):
    mean = jnp.mean(grad, axis=-1, keepdims=True)
    slope = jnp.mean(grad * unit, axis=-1, keepdims=True)
    return scale * (grad - mean - unit * slope)


def per_token(vectors, sides):
    return sides[0] * vectors[0][None, :] + sides[1] * vectors[1][None, :]


def per_crop(value, sides):
    return jnp.stack([jnp.sum(value * sides[0], axis=0), jnp.sum(value * sides[1], axis=0)])


def step_embed(stamps, breadth):
    halfway = breadth // 2
    frequency = jnp.exp(-math.log(10000.0) * jnp.arange(halfway, dtype=F32) / halfway)
    angles = stamps.astype(F32)[..., None] * frequency
    return jnp.concatenate([jnp.cos(angles), jnp.sin(angles)], axis=-1)


def segment_of(places, bounds):
    return jnp.sum((places[:, None] >= bounds[None, :]).astype(jnp.int32), axis=-1)


def gelu_slope(value):
    root = math.sqrt(2.0 / math.pi)
    inner = root * (value + 0.044715 * value * value * value)
    curve = jnp.tanh(inner)
    slope = root * (1.0 + 3 * 0.044715 * value * value)
    return 0.5 * (1.0 + curve) + 0.5 * value * (1.0 - curve * curve) * slope


def layer_forward(stream, mod, weights, masks, context):
    w_joint, w_project, w_expand, w_reduce = weights
    head_tok, channel_tok, keeping = masks
    sides, living, segq, segk, block = context
    offset_one, stretch_one, gate_one, offset_two, stretch_two, gate_two = [
        per_token(mod[:, i], sides) for i in range(6)
    ]
    unit_one, _ = normed(stream)
    normed_one = spread((unit_one * (1.0 + stretch_one) + offset_one).astype(BF16))
    joint = dot(normed_one, w_joint).astype(BF16)
    pairs = with_halo(joint[:, WIDTH:], block)
    mixed, log_total = attend(joint, pairs, segq, segk, head_tok)
    branch = collect(dot(mixed, w_project).astype(BF16))
    middle = stream + gate_one * branch * living
    unit_two, _ = normed(middle)
    normed_two = spread((unit_two * (1.0 + stretch_two) + offset_two).astype(BF16))
    pre_act = dot(normed_two, w_expand)
    activated = (jax.nn.gelu(pre_act, approximate=True) * channel_tok).astype(BF16)
    feedout = collect(dot(activated, w_reduce).astype(BF16))
    result = middle + gate_two * feedout * keeping
    record = (
        stream,
        normed_one,
        joint,
        pairs,
        mixed,
        log_total,
        branch,
        middle,
        normed_two,
        pre_act.astype(BF16),
        activated,
        feedout,
    )
    return result, record


def layer_backward(adjoint, record, mod, weights, masks, context):
    (
        stream,
        normed_one,
        joint,
        pairs,
        mixed,
        log_total,
        branch,
        middle,
        normed_two,
        pre_act,
        activated,
        feedout,
    ) = record
    w_joint, w_project, w_expand, w_reduce = weights
    head_tok, channel_tok, keeping = masks
    sides, living, segq, segk, block = context
    offset_one, stretch_one, gate_one, offset_two, stretch_two, gate_two = [
        per_token(mod[:, i], sides) for i in range(6)
    ]
    d_feed = spread((adjoint * gate_two * keeping).astype(BF16))
    d_gate_two = per_crop(adjoint * feedout * keeping, sides)
    d_active = against_cols(d_feed, w_reduce)
    d_pre = (gelu_slope(pre_act.astype(F32)) * channel_tok * d_active).astype(BF16)
    d_normed_two = collect(against_cols(d_pre, w_expand).astype(BF16))
    g_reduce = through_rows(activated, d_feed)
    g_expand = through_rows(normed_two, d_pre)
    unit_two, scale_two = normed(middle)
    d_middle = adjoint + norm_back(d_normed_two * (1.0 + stretch_two), unit_two, scale_two)
    d_offset_two = per_crop(d_normed_two, sides)
    d_stretch_two = per_crop(d_normed_two * unit_two, sides)
    d_branch = spread((d_middle * gate_one * living).astype(BF16))
    d_gate_one = per_crop(d_middle * branch * living, sides)
    d_mixed = against_cols(d_branch, w_project).astype(BF16)
    g_project = through_rows(mixed, d_branch)
    d_query, d_pairs = attend_back(joint, pairs, d_mixed, mixed, log_total, segq, segk, head_tok)
    d_joint = jnp.concatenate([d_query, halo_back(d_pairs, block)], axis=-1)
    d_normed_one = collect(against_cols(d_joint, w_joint).astype(BF16))
    g_joint = through_rows(normed_one, d_joint)
    unit_one, scale_one = normed(stream)
    d_stream = d_middle + norm_back(d_normed_one * (1.0 + stretch_one), unit_one, scale_one)
    d_offset_one = per_crop(d_normed_one, sides)
    d_stretch_one = per_crop(d_normed_one * unit_one, sides)
    d_mod = jnp.stack(
        [d_offset_one, d_stretch_one, d_gate_one, d_offset_two, d_stretch_two, d_gate_two], axis=1
    )
    return d_stream, d_mod, (g_joint, g_project, g_expand, g_reduce)


def attention_grads(g_joint, g_project):
    seq, groups, planes = sizes()
    cols = D // seq
    joint = [
        jnp.concatenate(
            [
                g_joint[:, kind * WIDTH + slot * cols : kind * WIDTH + (slot + 1) * cols]
                for kind in range(3)
            ],
            axis=1,
        )
        for slot in range(groups)
    ]
    project = [g_project[slot * cols : (slot + 1) * cols] for slot in range(groups)]
    joint, project = group_sum(ordered(joint)), group_sum(ordered(project))
    project = return_rows(project.astype(BF16))
    packed = jnp.concatenate([joint.astype(BF16), project], axis=1)
    owned = lax.psum_scatter(packed, "dp", scatter_dimension=0, tiled=True)
    return return_joint(owned[:, : 3 * cols]).astype(F32), owned[:, 3 * cols :].astype(F32)


def forward_grads(g_expand, g_reduce):
    seq, groups, planes = sizes()
    width = FF // seq
    expand = group_sum([g_expand[:, slot * width : (slot + 1) * width] for slot in range(groups)])
    reduce = group_sum([g_reduce[slot * width : (slot + 1) * width] for slot in range(groups)])
    height, rows = D // planes, width // planes
    expand = expand.astype(BF16).reshape(planes, height, width)
    reduce = reduce.astype(BF16)
    reduce = jnp.stack([fold(reduce[d * rows : (d + 1) * rows], width) for d in range(planes)])
    packed = jnp.concatenate([expand, reduce], axis=1)
    owned = lax.psum_scatter(packed, "dp", scatter_dimension=0, tiled=False)
    return (
        return_expand(owned[:height]).astype(F32),
        return_rows(unfold(owned[height:], rows)).astype(F32),
    )


def shards(
    hidden_in,
    lengths,
    timesteps,
    head_mask,
    group_mask,
    skip_mask,
    modulation_weight,
    joint_weight,
    project_weight,
    expand_weight,
    reduce_weight,
    cotangent,
):
    seq, groups, planes = sizes()
    block = hidden_in.shape[1]
    crops = lengths.shape[1]
    mine = lax.axis_index("seq")
    plane = lax.axis_index("dp")
    group, member = place()
    both = ("dp", "seq")

    attention_packs = [
        jnp.concatenate([deal_joint(joint_weight[l]), project_weight[l]], axis=1)
        for l in range(LAYERS)
    ]
    forward_packs = [
        jnp.concatenate(
            [deal_expand(expand_weight[l]), fold(deal_rows(reduce_weight[l]), FF // seq)], axis=0
        )
        for l in range(LAYERS)
    ]
    height = D // planes
    gathered = [
        over_planes(attention_packs[0]),
        over_planes(forward_packs[0]),
        over_planes(jnp.concatenate([attention_packs[1], forward_packs[1]], axis=0)),
    ]
    weights = [
        attention_weights(gathered[0]) + forward_weights(gathered[1]),
        attention_weights(gathered[2][:, :height]) + forward_weights(gathered[2][:, height:]),
    ]

    stamps = lax.all_gather(timesteps[0], "dp", axis=0, tiled=True)
    embedded = jax.nn.silu(step_embed(stamps, D)).astype(BF16)
    condition = lax.dynamic_slice_in_dim(embedded, plane * height, height, axis=1)
    part = jnp.stack([dot(condition, modulation_weight[l]) for l in range(LAYERS)], axis=1)
    part = lax.all_to_all(part, both, 0, 0, tiled=True)
    part = jnp.sum(part.reshape((planes, seq) + part.shape[1:]), axis=0)
    mod_here = jnp.transpose(part, (1, 0, 2)).reshape(LAYERS, 6, D)
    mod_before = shifted(mod_here, 1)
    mods = jnp.stack([mod_before, mod_here], axis=1)

    bounds = jnp.cumsum(lengths[0])
    first = group * TP * block
    span = 2 * block + AFTER
    places = first - block + jnp.arange((TP + 1) * block + AFTER, dtype=jnp.int32)
    inside = (places >= 0) & (places < seq * block)
    segment = jnp.where(inside, segment_of(places, bounds), -1)
    segq = segment[block : (TP + 1) * block][:, None]
    segk = jnp.stack([segment[b * block : b * block + span] for b in range(TP)])[:, None, :]
    own = segment_of(mine * block + jnp.arange(block, dtype=jnp.int32), bounds)[:, None]
    sides = [(own == mine - 1).astype(F32), ((own == mine) & (own < crops)).astype(F32)]
    living = (own < crops).astype(F32)
    onehot = (segq == jnp.arange(crops, dtype=jnp.int32)[None, :]).astype(BF16)
    units = slot_units()
    heads_here = member * LOCAL_HEADS + jnp.arange(LOCAL_HEADS, dtype=jnp.int32)
    rows = FF // (planes * seq)
    within = jnp.arange(rows, dtype=jnp.int32)
    hidden_here = jnp.concatenate(
        [(FF // planes) * d + rows * unit + within for unit in units for d in range(planes)]
    )
    groups_here = hidden_here // (FF // GROUPS)
    context = (sides, living, segq, segk, block)
    masks = []
    for l in range(LAYERS):
        heads_on = jnp.take(head_mask[0, l], heads_here, axis=1).astype(BF16)
        heads_on = jnp.pad(heads_on, ((0, 0), (0, LANES - LOCAL_HEADS)))
        groups_on = jnp.take(group_mask[0, l], groups_here, axis=1).astype(BF16)
        masks.append(
            (
                dot(onehot, heads_on),
                dot(onehot, groups_on).astype(BF16),
                skip_mask[0, l].astype(F32)[:, None] * living,
            )
        )

    stream = hidden_in[0].astype(F32)
    records = []
    for l in range(LAYERS):
        stream, record = layer_forward(stream, mods[l], weights[l], masks[l], context)
        records.append(record)
    final_state = stream.astype(BF16)[None]
    adjoint = cotangent[0].astype(F32)
    owned, d_mods = [None] * LAYERS, [None] * LAYERS
    for l in reversed(range(LAYERS)):
        adjoint, d_mods[l], grads = layer_backward(
            adjoint, records[l], mods[l], weights[l], masks[l], context
        )
        owned[l] = attention_grads(*grads[:2]) + forward_grads(*grads[2:])

    d_mod = jnp.stack(d_mods, axis=1)
    d_mod = d_mod[1] + shifted(d_mod[0], -1)
    d_mod = jnp.transpose(d_mod.reshape(LAYERS, seq, 6 * D // seq), (1, 0, 2))
    d_mod = jnp.broadcast_to(d_mod[None], (planes,) + d_mod.shape)
    d_mod = d_mod.reshape((planes * seq,) + d_mod.shape[2:])
    d_mod = lax.all_to_all(d_mod, both, 0, 0, tiled=True)
    modulation_grad = jnp.stack(
        [
            lax.dot_general(
                condition.astype(F32),
                d_mod[:, l],
                (((0,), (0,)), ((), ())),
                precision=HIGH,
                preferred_element_type=F32,
            )
            for l in range(LAYERS)
        ]
    )
    joint_grad, project_grad, expand_grad, reduce_grad = [
        jnp.stack([owned[l][i] for l in range(LAYERS)]) for i in range(4)
    ]
    return (
        final_state,
        adjoint[None],
        modulation_grad,
        joint_grad,
        project_grad,
        expand_grad,
        reduce_grad,
    )


def solution(mesh):
    in_specs = (
        P("dp", "seq", None),
        P("dp", None),
        P("dp", None),
        P("dp", None, None, None),
        P("dp", None, None, None),
        P("dp", None, "seq"),
        P(None, "dp", "seq"),
        P(None, "dp", "seq"),
        P(None, "dp", "seq"),
        P(None, "dp", "seq"),
        P(None, "dp", "seq"),
        P("dp", "seq", None),
    )
    out_specs = (
        P("dp", "seq", None),
        P("dp", "seq", None),
        P(None, "dp", "seq"),
        P(None, "dp", "seq"),
        P(None, "dp", "seq"),
        P(None, "dp", "seq"),
        P(None, "dp", "seq"),
    )
    return jax.shard_map(shards, mesh=mesh, in_specs=in_specs, out_specs=out_specs, check_vma=False)
```

```python
import functools
import math

import jax
import jax.numpy as jnp
import numpy as np
from jax import lax
from jax.experimental import pallas as pl
from jax.experimental.pallas import tpu as pltpu
from jax.sharding import Mesh
from jax.sharding import PartitionSpec as P

D = 1152
HEADS = 16
HEAD_DIM = 72
FF = 4608
GROUPS = 16
LAYERS = 2

TP = 4
LANES = 128
LOCAL_HEADS = HEADS // TP
LOCAL_FF = FF // TP
WIDTH = -(-LOCAL_HEADS * HEAD_DIM // LANES) * LANES
AFTER = 128
CHUNK = 256

SEQ = ("group", "member")
EVERY = ("dp", "group", "member")
OWNERS = ("dp", "group")

EPS = 1e-06
HIGH = lax.Precision.HIGHEST
NEGATIVE = -1e30
FACTOR = HEAD_DIM ** (-0.5)
F32 = jnp.float32
BF16 = jnp.bfloat16


def sizes():
    groups, planes = lax.axis_size("group"), lax.axis_size("dp")
    return groups * TP, groups, planes


def place():
    return lax.axis_index("group"), lax.axis_index("member")


def here():
    return jnp.stack([lax.axis_index("dp"), *place()])


def device_of(unit, groups):
    return (unit % groups) * TP + unit // groups


def unit_table(seq, groups):
    return np.array([(s % TP) * groups + s // TP for s in range(seq)])


def my_unit():
    _, groups, _ = sizes()
    group, member = place()
    return member * groups + group


def exchange(value, mask):
    seq, _, _ = sizes()
    return lax.ppermute(value, SEQ, [(i, i ^ mask) for i in range(seq)])


def shifted(value, steps):
    count, _, _ = sizes()
    return lax.ppermute(
        value, SEQ, [(i, i + steps) for i in range(count) if 0 <= i + steps < count]
    )


def from_plane(value, back):
    planes = lax.axis_size("dp")
    return lax.ppermute(value, "dp", [(d, (d + back) % planes) for d in range(planes)])


def after(value, *events):
    return lax.optimization_barrier((value,) + events)[0]


def dot(left, right):
    return jnp.dot(left, right, preferred_element_type=F32)


def through_rows(left, right):
    return lax.dot_general(left, right, (((0,), (0,)), ((), ())), preferred_element_type=F32)


def against_cols(left, right):
    return lax.dot_general(left, right, (((1,), (1,)), ((), ())), preferred_element_type=F32)


def near(mine):
    return [mine, exchange(mine, 1)]


def far(theirs):
    return [theirs, exchange(theirs, 1)]


def pair_sum(parts):
    return parts[0].astype(F32) + exchange(parts[1], 1).astype(F32)


def far_sum(pair):
    return exchange(pair.astype(BF16), 2).astype(F32)


def kinds_table(seq, groups):
    pairs, kinds = [], np.zeros((3, seq), np.int32)
    for r in range(3):
        targets = [device_of((3 * s + r) % seq, groups) for s in range(seq)]
        pairs.append(list(enumerate(targets)))
        for s in range(seq):
            kinds[r, targets[s]] = (3 * s + r) // seq
    return pairs, kinds


def my_kinds():
    seq, groups, _ = sizes()
    return jnp.asarray(kinds_table(seq, groups)[1])[:, lax.axis_index(SEQ)]


def deal_joint(joint):
    seq, groups, _ = sizes()
    pairs, _ = kinds_table(seq, groups)
    cols = joint.shape[1] // 3
    return [
        lax.ppermute(joint[:, r * cols : (r + 1) * cols], SEQ, pairs[r]) for r in range(3)
    ]


def return_joint(parts):
    seq, groups, _ = sizes()
    pairs, _ = kinds_table(seq, groups)
    back = [lax.ppermute(part, SEQ, [(b, a) for a, b in pairs[r]]) for r, part in enumerate(parts)]
    return jnp.concatenate(back, axis=1).astype(F32)


def choose(which, options):
    first, second, third = options
    return jnp.where(which == 0, first, jnp.where(which == 1, second, third))


def pack_attention_any(got, project):
    kinds = my_kinds()
    sent = [jnp.where(kinds[0] == k, got[0], jnp.where(kinds[1] == k, got[1], got[2])) for k in range(3)]
    return jnp.concatenate(sent + [project], axis=1)


def open_attention_any(stack):
    _, groups, planes = sizes()
    height, cols = stack.shape[1], stack.shape[2] // 4
    stack = stack.reshape(planes, groups, height, 4, cols)
    kinds = jnp.transpose(stack, (3, 0, 2, 1, 4)).reshape(4, D, groups * cols)
    blank = jnp.zeros((D, WIDTH - groups * cols), BF16)
    joint = jnp.concatenate([part for k in range(3) for part in (kinds[k], blank)], axis=1)
    return joint, kinds[3].reshape(TP, D // TP, groups * cols)


def join_project_any(got):
    _, groups, _ = sizes()
    rows = got.reshape(TP, D // TP, groups, -1).transpose(1, 2, 0, 3).reshape(D // TP, D)
    return jnp.concatenate([rows, jnp.zeros((WIDTH - D // TP, D), BF16)], axis=0)


def split_project_any(grad):
    _, groups, _ = sizes()
    chunks = grad[: D // TP].reshape(D // TP, groups, TP, -1).transpose(2, 0, 1, 3)
    return chunks.reshape(TP, D // TP, -1)


def split_attention_any(g_joint, got):
    _, groups, planes = sizes()
    cols = D // TP // groups
    parts = [g_joint[:, k * WIDTH : k * WIDTH + groups * cols] for k in range(3)]
    parts = jnp.stack(parts + [got.reshape(D, groups * cols)])
    parts = parts.reshape(4, planes, D // planes, groups, cols).transpose(1, 3, 2, 0, 4)
    return parts.reshape(planes * groups, D // planes, 4 * cols)


def unpack_attention_any(owned):
    kinds = my_kinds()
    cols = owned.shape[1] // 4
    own = [owned[:, k * cols : (k + 1) * cols] for k in range(4)]
    return [choose(kinds[r], own[:3]).astype(BF16) for r in range(3)] + [own[3].astype(F32)]


def pack_forward_any(expand, reduce):
    seq, groups, planes = sizes()
    cols, rows = expand.shape[1] // planes, reduce.shape[0] // seq
    chunks = []
    for unit in unit_table(seq, groups):
        q = unit % planes
        chunks += [expand[:, q * cols : (q + 1) * cols], reduce[unit * rows : (unit + 1) * rows]]
    chunks = jnp.concatenate([chunk.reshape(-1, cols) for chunk in chunks], axis=0)
    return chunks.reshape(seq, -1, cols)


def unpack_forward_any(got):
    seq, _, planes = sizes()
    ways, cols = seq // planes, got.shape[2]
    height, width = D // planes, got.shape[2] * planes
    mine = got.reshape((planes, ways) + got.shape[1:])
    mine = lax.dynamic_index_in_dim(mine, my_unit() // planes, 1, keepdims=False)
    expand = jnp.concatenate([mine[d, :height] for d in range(planes)], axis=1)
    reduce = got[:, height:].reshape(seq, cols, D // seq)
    reduce = jnp.concatenate([reduce[s] for s in range(seq)], axis=1)
    blocks = [reduce[:, k * width : (k + 1) * width] for k in range(D // width)]
    return jnp.concatenate([expand] + blocks, axis=0)


def open_forward_any(stack):
    _, groups, planes = sizes()
    height, width = D // planes, stack.shape[2]
    rows = width // planes
    stack = stack.reshape((planes, groups) + stack.shape[1:])
    expand = jnp.transpose(stack[:, :, :height], (0, 2, 1, 3)).reshape(D, groups * width)
    reduce = stack[:, :, height:].reshape(planes, groups, D // width, rows, width)
    reduce = jnp.transpose(reduce, (1, 0, 3, 2, 4)).reshape(groups * planes * rows, D)
    return expand, reduce


def split_forward_any(g_expand, g_reduce):
    _, groups, planes = sizes()
    height, width = D // planes, LOCAL_FF // groups
    rows = width // planes
    expand = g_expand.reshape(planes, height, groups, width).transpose(0, 2, 1, 3)
    reduce = g_reduce.reshape(groups, planes, rows, D // width, width).transpose(1, 0, 3, 2, 4)
    reduce = reduce.reshape(planes, groups, rows * D // width, width)
    stack = jnp.concatenate([expand, reduce], axis=2)
    return stack.reshape((planes * groups,) + stack.shape[2:])


def pack_return_any(owned):
    seq, _, planes = sizes()
    ways, height, width = seq // planes, D // planes, owned.shape[1]
    rows, cols = width // planes, width // planes
    blocks = owned[height:].reshape(D // width, rows, width)
    reduce = jnp.concatenate([blocks[k] for k in range(D // width)], axis=1)
    chunks = []
    for s in range(seq):
        d = s // ways
        chunks.append(owned[:height, d * cols : (d + 1) * cols])
        chunks.append(reduce[:, s * (D // seq) : (s + 1) * (D // seq)].reshape(-1, cols))
    return jnp.concatenate(chunks, axis=0).reshape(seq, -1, cols)


def unpack_return_any(got):
    seq, groups, planes = sizes()
    ways, cols, height = seq // planes, got.shape[2], D // planes
    got = jnp.swapaxes(got.reshape((groups, TP) + got.shape[1:]), 0, 1).reshape(got.shape)
    first = planes * (lax.axis_index(SEQ) % ways)
    mine = lax.dynamic_slice_in_dim(got[:, :height], first, planes)
    expand = jnp.concatenate([mine[q] for q in range(planes)], axis=1)
    return expand.astype(F32), got[:, height:].reshape(-1, D // seq).astype(F32)


def compact():
    seq, groups, planes = sizes()
    return groups == 2 and planes == 4 and D // seq % 16 == 0


def rearrange(body, arrays, outs, name):
    return pl.pallas_call(
        body,
        in_specs=[pl.BlockSpec(memory_space=pltpu.SMEM)]
        + [pl.BlockSpec(memory_space=pltpu.VMEM)] * len(arrays),
        out_specs=[pl.BlockSpec(memory_space=pltpu.VMEM)] * len(outs),
        out_shape=[jax.ShapeDtypeStruct(shape, dtype) for shape, dtype in outs],
        compiler_params=pltpu.CompilerParams(vmem_limit_bytes=48 * 1024 * 1024),
        cost_estimate=pl.CostEstimate(
            flops=0,
            bytes_accessed=sum(math.prod(shape) * 4 for shape, _ in outs),
            transcendentals=0,
        ),
        name=name,
    )(here(), *arrays)


def side_by_side(parts):
    return jnp.concatenate(parts, axis=1)


def kind_sent(me_ref, r):
    unit = me_ref[2] * 2 + me_ref[1]
    source = (3 * (unit + 8 - r)) % 8
    return (3 * source + r) // 8


def pack_attention_kernel(me_ref, a_ref, b_ref, c_ref, project_ref, out_ref):
    cols = a_ref.shape[1]
    first, second = kind_sent(me_ref, 0), kind_sent(me_ref, 1)
    for half in range(2):
        rows = slice(half * cols, (half + 1) * cols)
        a, b, c = a_ref[rows], b_ref[rows], c_ref[rows]
        parts = [jnp.where(first == k, a, jnp.where(second == k, b, c)) for k in range(3)]
        out_ref[:, half * 4 * cols : (half + 1) * 4 * cols] = side_by_side(
            parts + [project_ref[rows]]
        )


def by_plane(me_ref, refs):
    if len(refs) == 1:
        return [(d, refs[0][2 * d], refs[0][2 * d + 1]) for d in range(4)]
    got = []
    for step in range(4):
        own, other = refs[step][...], refs[4 + step][...]
        first = jnp.where(me_ref[1] == 0, own, other)
        second = jnp.where(me_ref[1] == 0, other, own)
        got.append(((me_ref[0] + 4 - step) % 4, first, second))
    return got


def rows_at(start, count):
    if isinstance(start, int):
        return slice(start, start + count)
    return pl.ds(pl.multiple_of(start, 16), count)


def open_attention_kernel(me_ref, *refs):
    *refs, joint_ref, project_ref = refs
    cols = refs[0].shape[-2]
    blank = jnp.zeros((cols, WIDTH - 2 * cols), BF16)
    for plane, first, second in by_plane(me_ref, refs):
        for half in range(2):
            pieces = [
                [piece[:, (4 * half + k) * cols : (4 * half + k + 1) * cols] for k in range(4)]
                for piece in (first, second)
            ]
            parts = []
            for kind in range(3):
                parts += [pieces[0][kind], pieces[1][kind], blank]
            joint_ref[rows_at(plane * 2 * cols + half * cols, cols)] = side_by_side(parts)
            project_ref[plane, half * cols : (half + 1) * cols] = side_by_side(
                [pieces[0][3], pieces[1][3]]
            )


def join_project_kernel(me_ref, got_ref, out_ref):
    cols = got_ref.shape[2] // 2
    rows = got_ref.shape[1]
    out_ref[:rows] = side_by_side(
        [got_ref[t][:, g * cols : (g + 1) * cols] for g in range(2) for t in range(4)]
    )
    out_ref[rows:] = jnp.zeros((out_ref.shape[0] - rows, out_ref.shape[1]), BF16)


def split_project_kernel(me_ref, grad_ref, out_ref):
    rows, cols = out_ref.shape[1], out_ref.shape[2] // 2
    for t in range(4):
        out_ref[t] = side_by_side(
            [grad_ref[:rows, (g * 4 + t) * cols : (g * 4 + t + 1) * cols] for g in range(2)]
        )


def pack_forward_kernel(me_ref, expand_ref, reduce_ref, out_ref):
    cols = reduce_ref.shape[1]
    for s, unit in enumerate(unit_table(8, 2)):
        at = slice(unit % 4 * cols, (unit % 4 + 1) * cols)
        out_ref[s] = side_by_side(
            [
                expand_ref[:cols, at],
                expand_ref[cols:, at],
                reduce_ref[unit * cols : (unit + 1) * cols],
            ]
        )


def unpack_forward_kernel(me_ref, got_ref, out_ref):
    cols = got_ref.shape[1]
    unit = me_ref[2] * 2 + me_ref[1]
    for half in range(2):
        parts = []
        for d in range(4):
            parts.append(got_ref[2 * d + unit // 4][:, half * cols : (half + 1) * cols])
        for s in range(4):
            parts.append(got_ref[4 * half + s][:, 2 * cols :])
        out_ref[half * cols : (half + 1) * cols] = side_by_side(parts)


def open_forward_kernel(me_ref, *refs):
    *refs, expand_ref, reduce_ref = refs
    height = refs[0].shape[-2]
    rows, width = height // 2, D // 2
    for plane, first, second in by_plane(me_ref, refs):
        expand_ref[rows_at(plane * height, height)] = side_by_side(
            [first[:, :width], second[:, :width]]
        )
        for group, piece in enumerate((first, second)):
            reduce_ref[rows_at(group * width + plane * rows, rows)] = side_by_side(
                [piece[:rows, width:], piece[rows:, width:]]
            )


def put_pieces(me_ref, outs, step, pair):
    if len(outs) == 1:
        outs[0][2 * step], outs[0][2 * step + 1] = pair
    else:
        outs[step][...] = jnp.where(me_ref[1] == 0, pair[0], pair[1])
        outs[4 + step][...] = jnp.where(me_ref[1] == 0, pair[1], pair[0])


def split_forward_kernel(me_ref, expand_ref, reduce_ref, *outs):
    height = outs[0].shape[-2]
    rows, width = height // 2, D // 2
    for step in range(4):
        plane = step if len(outs) == 1 else (me_ref[0] + 3 - step) % 4
        expand = expand_ref[rows_at(plane * height, height)]
        pair = []
        for group in range(2):
            reduce = reduce_ref[rows_at(group * width + plane * rows, rows)]
            part = expand[:, group * width : (group + 1) * width]
            upper = side_by_side([part[:rows], reduce[:, :width]])
            lower = side_by_side([part[rows:], reduce[:, width:]])
            pair.append(jnp.concatenate([upper, lower], axis=0))
        put_pieces(me_ref, outs, step, pair)


def pack_return_kernel(me_ref, whole_ref, out_ref):
    cols = out_ref.shape[1]
    for s in range(8):
        at = slice(s // 2 * cols, (s // 2 + 1) * cols)
        right = slice((4 + s % 4) * cols, (5 + s % 4) * cols)
        out_ref[s] = side_by_side(
            [
                whole_ref[:cols, at],
                whole_ref[cols:, at],
                whole_ref[s // 4 * cols : (s // 4 + 1) * cols, right],
            ]
        )


def unpack_return_kernel(me_ref, got_ref, expand_ref, reduce_ref):
    cols = got_ref.shape[1]
    for half in range(2):
        parts = []
        for q in range(4):
            device = q % 2 * 4 + 2 * (me_ref[2] % 2) + q // 2
            parts.append(got_ref[device][:, half * cols : (half + 1) * cols])
        expand_ref[half * cols : (half + 1) * cols] = side_by_side(parts).astype(F32)
    for s, unit in enumerate(unit_table(8, 2)):
        reduce_ref[unit * cols : (unit + 1) * cols] = got_ref[s][:, 2 * cols :].astype(F32)


def split_attention_kernel(me_ref, joint_ref, project_ref, *outs):
    cols = outs[0].shape[-2]
    for step in range(4):
        plane = step if len(outs) == 1 else (me_ref[0] + 3 - step) % 4
        parts = [[], []]
        for half in range(2):
            rows = joint_ref[rows_at(plane * 2 * cols + half * cols, cols)]
            project = project_ref[plane, half * cols : (half + 1) * cols]
            for group in range(2):
                for kind in range(3):
                    at = kind * WIDTH + group * cols
                    parts[group].append(rows[:, at : at + cols])
                parts[group].append(project[:, group * cols : (group + 1) * cols])
        put_pieces(me_ref, outs, step, [side_by_side(part) for part in parts])


def unpack_attention_kernel(me_ref, whole_ref, a_ref, b_ref, c_ref, project_ref):
    cols = whole_ref.shape[0]
    for half in range(2):
        rows = slice(half * cols, (half + 1) * cols)
        parts = []
        for k in range(4):
            at = (half * 4 + k) * cols
            parts.append(whole_ref[:, at : at + cols])
        for r, ref in enumerate((a_ref, b_ref, c_ref)):
            ref[rows] = choose(kind_sent(me_ref, r), parts[:3]).astype(BF16)
        project_ref[rows] = parts[3].astype(F32)


def pack_attention(joint, project):
    got = deal_joint(joint)
    if not compact():
        return pack_attention_any(got, project)
    cols = project.shape[1]
    outs = [((cols, 8 * cols), BF16)]
    return rearrange(pack_attention_kernel, [*got, project], outs, "pack_attention")[0]


def pack_forward(expand, reduce, *events):
    cols = reduce.shape[1]
    if compact():
        outs = [((8, cols, 3 * cols), BF16)]
        (chunks,) = rearrange(pack_forward_kernel, [expand, reduce], outs, "pack_forward")
    else:
        chunks = pack_forward_any(expand, reduce)
    got = after(lax.all_to_all(chunks, SEQ, 0, 0, tiled=True), *events)
    if not compact():
        return unpack_forward_any(got)
    return rearrange(
        unpack_forward_kernel, [got], [((2 * cols, 8 * cols), BF16)], "unpack_forward"
    )[0]


def gather_slow(pack):
    return [lax.all_gather(pack, OWNERS, axis=0, tiled=False)]


def gather_planes(pack):
    return [pack] + [from_plane(pack, back) for back in range(1, 4)]


def open_attention(pieces):
    if not compact():
        return open_attention_any(pieces[0])
    cols = D // 8
    outs = [((D, 3 * WIDTH), BF16), ((TP, 2 * cols, 2 * cols), BF16)]
    return rearrange(open_attention_kernel, pieces, outs, "open_attention")


def project_matrix(columns):
    got = lax.all_to_all(columns, "member", 0, 0, tiled=True)
    if not compact():
        return join_project_any(got)
    return rearrange(join_project_kernel, [got], [((WIDTH, D), BF16)], "join_project")[0]


def open_forward(pieces):
    if not compact():
        return open_forward_any(pieces[0])
    outs = [((D, D), BF16), ((D, D), BF16)]
    return rearrange(open_forward_kernel, pieces, outs, "open_forward")


def piece_outs(shape, fast):
    return [(shape, BF16)] * 8 if fast else [((8,) + shape, BF16)]


def split_project(g_project):
    if compact():
        outs = [((TP, D // TP, D // TP), BF16)]
        (chunks,) = rearrange(split_project_kernel, [g_project], outs, "split_project")
    else:
        chunks = split_project_any(g_project)
    return lax.all_to_all(chunks, "member", 0, 0, tiled=True)


def split_attention(g_joint, project, fast):
    if not compact():
        return [split_attention_any(g_joint, project)]
    outs = piece_outs((D // 8, D), fast)
    return rearrange(split_attention_kernel, [g_joint, project], outs, "split_attention")


def split_forward(g_expand, g_reduce, fast):
    if not compact():
        return [split_forward_any(g_expand, g_reduce)]
    outs = piece_outs((D // 4, D), fast)
    return rearrange(split_forward_kernel, [g_expand, g_reduce], outs, "split_forward")


def owner_sum(pieces, step, carried, *events):
    own, other = pieces[step], after(pieces[4 + step], *events)
    total = own.astype(F32) + exchange(other, TP).astype(F32)
    if step:
        total = total + from_plane(carried, 1).astype(F32)
    return total.astype(BF16)


def owner_sum_slow(pieces):
    return lax.psum_scatter(pieces[0], OWNERS, scatter_dimension=0, tiled=False)


def return_attention(owned):
    if compact():
        cols = D // 8
        outs = [((2 * cols, cols), BF16)] * 3 + [((2 * cols, cols), F32)]
        *parts, project = rearrange(unpack_attention_kernel, [owned], outs, "unpack_attention")
    else:
        *parts, project = unpack_attention_any(owned)
    return return_joint(parts), project


def return_forward(owned):
    cols = D // 8
    if compact():
        outs = [((8, cols, 3 * cols), BF16)]
        (chunks,) = rearrange(pack_return_kernel, [owned], outs, "pack_return")
    else:
        chunks = pack_return_any(owned)
    got = lax.all_to_all(chunks, SEQ, 0, 0, tiled=True)
    if not compact():
        return unpack_return_any(got)
    outs = [((2 * cols, 4 * cols), F32), ((8 * cols, cols), F32)]
    return rearrange(unpack_return_kernel, [got], outs, "unpack_return")


def half_call(body, half, chunks, matrices, tokens, into, partial, name):
    count = chunks[0].shape[0]

    def whole(array):
        return pl.BlockSpec(array.shape, lambda i: (0,) * array.ndim)

    def slot(shape):
        return pl.BlockSpec(shape, lambda i: (2 * half + i,) + (0,) * (len(shape) - 1))

    kept = [array for _, array in into if array is not None]
    operands = [*chunks, *matrices, *tokens]
    specs = [whole(array) for array in (*chunks, *matrices)]
    specs += [slot((array.shape[0] // TP,) + array.shape[1:]) for array in tokens]
    out_specs = [slot((count, width)) for width, _ in into]
    shapes = [jax.ShapeDtypeStruct((TP * count, width), BF16) for width, _ in into]
    if partial:
        out_specs += [pl.BlockSpec((count, D), lambda i: (0, 0))] * 2
        shapes += [jax.ShapeDtypeStruct((count, D), BF16)] * 2
    aliases = {len(operands) + k: k for k in range(len(kept))}
    work = sum(2 * 2 * count * math.prod(matrix.shape) for matrix in matrices)

    def kernel(a_ref, b_ref, *refs):
        n = len(matrices) + len(tokens)
        mine = pl.program_id(0) == 0
        rows = jnp.where(mine, a_ref[...], b_ref[...])
        body(rows, mine, refs[:n], refs[n + len(kept) :])

    return pl.pallas_call(
        kernel,
        grid=(2,),
        in_specs=specs + [pl.BlockSpec(memory_space=pl.ANY)] * len(kept),
        out_specs=out_specs,
        out_shape=shapes,
        input_output_aliases=aliases,
        compiler_params=kernel_params(),
        cost_estimate=pl.CostEstimate(
            flops=work, bytes_accessed=work // 512, transcendentals=2 * count * D
        ),
        name=name,
    )(*operands, *kept)


def put_partial(mine, value, a_ref, b_ref):
    value = value.astype(BF16)

    @pl.when(mine)
    def _():
        a_ref[...] = value

    @pl.when(jnp.logical_not(mine))
    def _():
        b_ref[...] = value


def chunks_of(width):
    return [slice(at, min(at + CHUNK, width)) for at in range(0, width, CHUNK)]


def joint_body(rows, mine, refs, outs):
    outs[0][...] = dot(rows, refs[0][...]).astype(BF16)


def forward_body(rows, mine, refs, outs):
    expand_ref, reduce_ref, sides_ref, active_ref = refs
    activated_ref, slope_ref, a_ref, b_ref = outs
    root = math.sqrt(2.0 / math.pi)
    before, now = sides_ref[:, 0:1], sides_ref[:, 1:2]
    for at in chunks_of(LOCAL_FF):
        pre = dot(rows, expand_ref[:, at])
        square = pre * pre
        curve = jnp.tanh(root * pre * (1.0 + 0.044715 * square))
        half = 0.5 + 0.5 * curve
        mask = before * active_ref[0, 0:1, at] + now * active_ref[0, 1:2, at]
        slope = half + pre * (half - half * half) * (2.0 * root * (1.0 + 0.134145 * square))
        activated_ref[:, at] = (pre * half * mask).astype(BF16)
        slope_ref[:, at] = (slope * mask).astype(BF16)
    put_partial(mine, dot(activated_ref[...], reduce_ref[...]), a_ref, b_ref)


def backward_body(rows, mine, refs, outs):
    expand_ref, reduce_ref, slope_ref = refs
    d_pre_ref, a_ref, b_ref = outs
    for at in chunks_of(LOCAL_FF):
        d_active = against_cols(rows, reduce_ref[at])
        d_pre_ref[:, at] = (d_active * slope_ref[:, at].astype(F32)).astype(BF16)
    put_partial(mine, against_cols(d_pre_ref[...], expand_ref[...]), a_ref, b_ref)


def head_tiles(head):
    low = head * HEAD_DIM // LANES * LANES
    high = -(-(head + 1) * HEAD_DIM // LANES) * LANES
    return low, high


def lanes_of(head, shape):
    low, high = head_tiles(head)
    lane = lax.broadcasted_iota(jnp.int32, shape, 1) + low
    return (lane >= head * HEAD_DIM) & (lane < (head + 1) * HEAD_DIM)


def key_tiles(refs, halos, block, base, low, high):
    before_ref, after_ref = halos
    prev_ref, here_ref, next_ref = refs
    prev = jnp.where(block == 0, before_ref[:, base + low : base + high], prev_ref[:, low:high])
    following = jnp.where(
        block == TP - 1, after_ref[:, base + low : base + high], next_ref[:, low:high]
    )
    return prev, here_ref[:, low:high], following


def attend_kernel(
    me_ref,
    q_ref,
    *refs,
):
    keys, values, halos = refs[0:3], refs[3:6], refs[6:8]
    segq_ref, segk_ref, head_ref, mixed_ref, lse_ref = refs[8:]
    block = pl.program_id(0) ^ me_ref[2]
    count = q_ref.shape[0]
    allowed = segq_ref[...] == segk_ref[0]
    tiles = [jnp.zeros((count, LANES), F32) for _ in range(WIDTH // LANES)]
    total = jnp.zeros((count, LANES), F32)
    lane = lax.broadcasted_iota(jnp.int32, (count, LANES), 1)
    for head in range(LOCAL_HEADS):
        low, high = head_tiles(head)
        mine = lanes_of(head, (count, high - low))
        query = jnp.where(mine, q_ref[:, low:high], 0)
        key = key_tiles(keys, halos, block, 0, low, high)
        scores = jnp.concatenate([against_cols(query, part) for part in key], axis=1) * FACTOR
        scores = jnp.where(allowed, scores, NEGATIVE)
        highest = jnp.max(scores, axis=-1, keepdims=True)
        weights = jnp.exp(scores - highest)
        sums = jnp.sum(weights, axis=-1, keepdims=True)
        probs = (weights / sums).astype(BF16)
        out, at = 0.0, 0
        for part in key_tiles(values, halos, block, WIDTH, low, high):
            out = out + dot(probs[:, at : at + part.shape[0]], part)
            at += part.shape[0]
        out = jnp.where(mine, out, 0.0) * head_ref[:, head : head + 1]
        for k in range(low // LANES, high // LANES):
            at = k * LANES - low
            tiles[k] = tiles[k] + out[:, at : at + LANES]
        total = jnp.where(lane == head, highest + jnp.log(sums), total)
    for k, tile in enumerate(tiles):
        mixed_ref[:, k * LANES : (k + 1) * LANES] = tile.astype(BF16)
    lse_ref[...] = total


def attend_back_kernel(me_ref, q_ref, *refs):
    keys, values, halos = refs[0:3], refs[3:6], refs[6:8]
    grad_ref, mixed_ref, lse_ref, segq_ref, segk_ref, head_ref = refs[8:14]
    d_joint_ref, d_before_ref, d_after_ref, sum_ref = refs[14:]
    step = pl.program_id(0)
    block = step ^ me_ref[2]
    count = q_ref.shape[0]

    @pl.when(step == 0)
    def _():
        sum_ref[...] = jnp.zeros_like(sum_ref)

    prev = jnp.where(block == 0, TP, jnp.maximum(block - 1, 0) ^ me_ref[2])
    following = jnp.where(block == TP - 1, TP + 1, jnp.minimum(block + 1, TP - 1) ^ me_ref[2])
    windows = [
        (pl.ds(pl.multiple_of(prev * count, count), count), 0),
        (pl.ds(pl.multiple_of(step * count, count), count), count),
        (pl.ds(pl.multiple_of(following * count, count), AFTER), 2 * count),
    ]
    rows = pl.ds(pl.multiple_of(step * count, count), count)
    allowed = segq_ref[...] == segk_ref[0]
    tiles = [jnp.zeros((count, LANES), F32) for _ in range(WIDTH // LANES)]
    for head in range(LOCAL_HEADS):
        low, high = head_tiles(head)
        mine = lanes_of(head, (count, high - low))
        query = jnp.where(mine, q_ref[:, low:high], 0)
        key = key_tiles(keys, halos, block, 0, low, high)
        value = key_tiles(values, halos, block, WIDTH, low, high)
        active = head_ref[:, head : head + 1]
        grad = jnp.where(mine, grad_ref[:, low:high].astype(F32) * active, 0.0)
        balance = jnp.sum(grad * mixed_ref[:, low:high].astype(F32), axis=-1, keepdims=True)
        grad = grad.astype(BF16)
        scores = jnp.concatenate([against_cols(query, part) for part in key], axis=1) * FACTOR
        probs = jnp.where(allowed, jnp.exp(scores - lse_ref[:, head : head + 1]), 0.0)
        d_probs = jnp.concatenate([against_cols(grad, part) for part in value], axis=1)
        d_scores = (probs * (d_probs - balance)).astype(BF16)
        probs = probs.astype(BF16)
        d_query = 0.0
        for (window, at), part in zip(windows, key):
            piece = d_scores[:, at : at + part.shape[0]]
            d_query = d_query + dot(piece, part)
            sum_ref[window, low:high] += through_rows(piece, query) * FACTOR
            sum_ref[window, WIDTH + low : WIDTH + high] += through_rows(
                probs[:, at : at + part.shape[0]], grad
            )
        d_query = jnp.where(mine, d_query, 0.0)
        for k in range(low // LANES, high // LANES):
            at = k * LANES - low
            tiles[k] = tiles[k] + d_query[:, at : at + LANES]
    for k, tile in enumerate(tiles):
        d_joint_ref[rows, k * LANES : (k + 1) * LANES] = (tile * FACTOR).astype(BF16)

    @pl.when(step == pl.num_programs(0) - 1)
    def _():
        d_joint_ref[:, WIDTH:] = sum_ref[: TP * count].astype(BF16)
        d_before_ref[...] = sum_ref[TP * count : (TP + 1) * count].astype(BF16)
        d_after_ref[...] = sum_ref[(TP + 1) * count : (TP + 1) * count + AFTER].astype(BF16)


def kernel_params():
    return pltpu.CompilerParams(
        dimension_semantics=("arbitrary",), vmem_limit_bytes=48 * 1024 * 1024
    )


def block_specs(count):
    def rows(width):
        return pl.BlockSpec((count, width), lambda j, me: (j, 0))

    def whole(shape):
        return pl.BlockSpec(shape, lambda j, me: (0,) * len(shape))

    def around(kind):
        def before(j, me):
            return (jnp.maximum((j ^ me[2]) - 1, 0) ^ me[2], kind)

        def following(j, me):
            return ((jnp.minimum((j ^ me[2]) + 1, TP - 1) ^ me[2]) * (count // AFTER), kind)

        return [
            pl.BlockSpec((count, WIDTH), before),
            pl.BlockSpec((count, WIDTH), lambda j, me: (j, kind)),
            pl.BlockSpec((AFTER, WIDTH), following),
        ]

    fixed = [rows(WIDTH)] + around(1) + around(2)
    return rows, whole, fixed + [whole((count, 2 * WIDTH)), whole((AFTER, 2 * WIDTH))]


def attend(joint, halos, segq, segk, heads):
    span = segk.shape[2]
    count = joint.shape[0] // TP
    rows, whole, specs = block_specs(count)
    return pl.pallas_call(
        attend_kernel,
        grid_spec=pltpu.PrefetchScalarGridSpec(
            num_scalar_prefetch=1,
            grid=(TP,),
            in_specs=specs
            + [
                rows(1),
                pl.BlockSpec((1, 1, span), lambda j, me: (j, 0, 0)),
                rows(LANES),
            ],
            out_specs=[rows(WIDTH), rows(LANES)],
        ),
        out_shape=[
            jax.ShapeDtypeStruct((TP * count, WIDTH), BF16),
            jax.ShapeDtypeStruct((TP * count, LANES), F32),
        ],
        compiler_params=kernel_params(),
        cost_estimate=pl.CostEstimate(
            flops=8 * TP * count * span * LANES * LOCAL_HEADS,
            bytes_accessed=TP * count * WIDTH * 8,
            transcendentals=TP * count * span * LOCAL_HEADS,
        ),
        name="attend",
    )(here(), *[joint] * 7, *halos, segq, segk, heads)


def attend_back(joint, halos, grad, mixed, log_total, segq, segk, heads):
    span = segk.shape[2]
    count = joint.shape[0] // TP
    rows, whole, specs = block_specs(count)
    shapes = [(TP * count, 3 * WIDTH), (count, 2 * WIDTH), (AFTER, 2 * WIDTH)]
    return pl.pallas_call(
        attend_back_kernel,
        grid_spec=pltpu.PrefetchScalarGridSpec(
            num_scalar_prefetch=1,
            grid=(TP,),
            in_specs=specs
            + [
                rows(WIDTH),
                rows(WIDTH),
                rows(LANES),
                rows(1),
                pl.BlockSpec((1, 1, span), lambda j, me: (j, 0, 0)),
                rows(LANES),
            ],
            out_specs=[whole(shape) for shape in shapes],
            scratch_shapes=[pltpu.VMEM(((TP + 2) * count, 2 * WIDTH), F32)],
        ),
        out_shape=[jax.ShapeDtypeStruct(shape, BF16) for shape in shapes],
        compiler_params=kernel_params(),
        cost_estimate=pl.CostEstimate(
            flops=20 * TP * count * span * LANES * LOCAL_HEADS,
            bytes_accessed=TP * count * WIDTH * 20,
            transcendentals=TP * count * span * LOCAL_HEADS,
        ),
        name="attend_back",
    )(here(), *[joint] * 7, *halos, grad, mixed, log_total, segq, segk, heads)


def halos_of(joint):
    _, groups, _ = sizes()
    count = joint.shape[0] // TP
    if groups == 1:
        return [jnp.zeros((rows, 2 * WIDTH), joint.dtype) for rows in (count, AFTER)]
    group, member = place()
    column = jnp.int32(WIDTH)
    last = ((member ^ (TP - 1)) * count, column)
    if groups == 2:
        first = (member * count, column)
        start = [jnp.where(group == 0, x, y) for x, y in zip(last, first)]
        got = exchange(lax.dynamic_slice(joint, start, (count, 2 * WIDTH)), TP)
        return [got, got]
    last = lax.dynamic_slice(joint, last, (count, 2 * WIDTH))
    first = lax.dynamic_slice(joint, (member * count, column), (AFTER, 2 * WIDTH))
    return [shifted(last, TP), shifted(first, -TP)]


def halos_back(d_joint, d_before, d_after):
    _, groups, _ = sizes()
    if groups == 1:
        return d_joint
    group, member = place()
    count = d_joint.shape[0] // TP
    last, first = (member ^ (TP - 1)) * count, member * count
    if groups == 2:
        d_after = jnp.pad(d_after, ((0, count - AFTER), (0, 0)))
        got = exchange(jnp.where(group == 0, d_after, d_before), TP)
        pieces = [(got, jnp.where(group == 0, last, first))]
    else:
        pieces = [(shifted(d_before, -TP), last), (shifted(d_after, TP), first)]
    for piece, at in pieces:
        start = (at, jnp.int32(WIDTH))
        sums = lax.dynamic_slice(d_joint, start, piece.shape)
        sums = (sums.astype(F32) + piece.astype(F32)).astype(BF16)
        d_joint = lax.dynamic_update_slice(d_joint, sums, start)
    return d_joint


def normed(stream):
    center = stream - jnp.mean(stream, axis=-1, keepdims=True)
    scale = lax.rsqrt(jnp.mean(center * center, axis=-1, keepdims=True) + EPS)
    return center * scale, scale


def norm_back(grad, unit, scale):
    mean = jnp.mean(grad, axis=-1, keepdims=True)
    slope = jnp.mean(grad * unit, axis=-1, keepdims=True)
    return scale * (grad - mean - unit * slope)


def per_token(vectors, sides):
    return sides[0] * vectors[0][None, :] + sides[1] * vectors[1][None, :]


def per_crop(value, sides):
    return jnp.stack([jnp.sum(value * sides[0], axis=0), jnp.sum(value * sides[1], axis=0)])


def step_embed(stamps, breadth):
    halfway = breadth // 2
    frequency = jnp.exp(-math.log(10000.0) * jnp.arange(halfway, dtype=F32) / halfway)
    angles = stamps.astype(F32)[..., None] * frequency
    return jnp.concatenate([jnp.cos(angles), jnp.sin(angles)], axis=-1)


def segment_of(places, bounds):
    return jnp.sum((places[:, None] >= bounds[None, :]).astype(jnp.int32), axis=-1)


def layer_forward(stream, mod, w_joint, project_columns, open_reduce, masks, context, hold):
    head_tok, active, keeping = masks
    sides, living, segq, segk, slot_sides = context
    offset_one, stretch_one, gate_one, offset_two, stretch_two, gate_two = [
        per_token(mod[:, i], sides) for i in range(6)
    ]
    count = stream.shape[0]
    unit_one, _ = normed(stream)
    mine = (unit_one * (1.0 + stretch_one) + offset_one).astype(BF16)
    mine = hold("normed_one", mine)
    theirs, ours = exchange(mine, 2), near(mine)
    (joint,) = half_call(
        joint_body, 0, ours, [w_joint], [], [(3 * WIDTH, None)], False, "joint_near"
    )
    theirs = far(after(theirs, joint))
    (joint,) = half_call(
        joint_body, 1, theirs, [w_joint], [], [(3 * WIDTH, joint)], False, "joint_far"
    )
    normed_one = ours + theirs
    halos = halos_of(joint)
    w_project = project_matrix(after(project_columns, joint))
    halos = hold("halos", halos)
    mixed, log_total = attend(joint, halos, segq, segk, head_tok)
    mixed = hold("mixed", mixed)

    def branch_parts(rows, slots):
        return [dot(rows[j * count : (j + 1) * count], w_project).astype(BF16) for j in slots]

    away = pair_sum(branch_parts(mixed, (2, 3)))
    close = pair_sum(branch_parts(after(mixed, away), (0, 1)))
    branch = after(hold("branch", far_sum(away)), close) + close
    middle = stream + gate_one * branch * living
    unit_two, _ = normed(middle)
    mine = (unit_two * (1.0 + stretch_two) + offset_two).astype(BF16)
    theirs, ours = exchange(mine, 2), near(mine)
    w_expand, w_reduce = open_reduce(mine)
    matrices, tokens = [w_expand, w_reduce], [slot_sides, active]
    activated, slope, *parts = half_call(
        forward_body, 0, ours, matrices, tokens, [(LOCAL_FF, None)] * 2, True, "forward_near"
    )
    close = pair_sum(parts)
    theirs = far(after(theirs, activated))
    activated, slope, *parts = half_call(
        forward_body,
        1,
        theirs,
        matrices,
        tokens,
        [(LOCAL_FF, activated), (LOCAL_FF, slope)],
        True,
        "forward_far",
    )
    away = pair_sum(parts)
    feedout = hold("feedout", far_sum(away), away) + close
    result = middle + gate_two * feedout * keeping
    record = (
        stream,
        normed_one,
        joint,
        halos,
        mixed,
        log_total,
        branch,
        middle,
        ours + theirs,
        slope,
        activated,
        feedout,
    )
    return result, record, (w_joint, w_project, w_expand, w_reduce)


def layer_backward(adjoint, record, mod, weights, masks, context, last, hold):
    (
        stream,
        normed_one,
        joint,
        halos,
        mixed,
        log_total,
        branch,
        middle,
        normed_two,
        slope,
        activated,
        feedout,
    ) = record
    w_joint, w_project, w_expand, w_reduce = weights
    head_tok, active, keeping = masks
    sides, living, segq, segk, slot_sides = context
    offset_one, stretch_one, gate_one, offset_two, stretch_two, gate_two = [
        per_token(mod[:, i], sides) for i in range(6)
    ]
    count = stream.shape[0]
    fast = last and compact()
    mine = (adjoint * gate_two * keeping).astype(BF16)
    theirs, ours = exchange(mine, 2), near(mine)
    matrices = [w_expand, w_reduce]
    d_pre, *parts = half_call(
        backward_body, 0, ours, matrices, [slope], [(LOCAL_FF, None)], True, "backward_near"
    )
    close = pair_sum(parts)
    theirs = far(after(theirs, d_pre))
    d_pre, *parts = half_call(
        backward_body, 1, theirs, matrices, [slope], [(LOCAL_FF, d_pre)], True, "backward_far"
    )
    away = pair_sum(parts)
    d_feed = jnp.concatenate(ours + theirs, axis=0)
    g_reduce = through_rows(activated, after(d_feed, away)).astype(BF16)
    d_gate_two = per_crop(after(adjoint, away) * feedout * keeping, sides)
    unit_two, scale_two = normed(middle)
    d_normed_two = after(far_sum(away), g_reduce, d_gate_two) + close
    d_middle = adjoint + norm_back(d_normed_two * (1.0 + stretch_two), unit_two, scale_two)
    mine = (d_middle * gate_one * living).astype(BF16)
    theirs, ours = exchange(mine, 2), near(mine)
    rows = after(jnp.concatenate(normed_two, axis=0), mine)
    g_expand = through_rows(rows, d_pre).astype(BF16)
    forward_pieces = split_forward(g_expand, g_reduce, fast)
    d_offset_two = per_crop(after(d_normed_two, mine), sides)
    d_stretch_two = per_crop(after(d_normed_two, mine) * unit_two, sides)
    theirs = after(theirs, forward_pieces, d_offset_two, d_stretch_two)
    if fast:
        forward_sum = owner_sum(forward_pieces, 0, None)
    else:
        forward_sum = owner_sum_slow(forward_pieces)
    d_branch = jnp.concatenate(ours + far(theirs), axis=0)
    d_mixed = against_cols(d_branch, w_project).astype(BF16)
    g_project = split_project(through_rows(mixed, d_branch).astype(BF16))
    if fast:
        d_mixed = after(d_mixed, forward_sum)
        forward_sum = owner_sum(forward_pieces, 1, forward_sum)
    d_joint = halos_back(
        *attend_back(joint, halos, d_mixed, mixed, log_total, segq, segk, head_tok)
    )
    d_joint = hold("d_joint", d_joint)
    if fast:
        d_joint = after(d_joint, forward_sum)

    def normed_parts(rows, slots):
        return [against_cols(rows[j * count : (j + 1) * count], w_joint).astype(BF16) for j in slots]

    if last:
        g_joint = through_rows(jnp.concatenate(normed_one, axis=0), d_joint).astype(BF16)
        attention_pieces = split_attention(g_joint, g_project, fast)
        away = pair_sum(normed_parts(after(d_joint, attention_pieces), (2, 3)))
    else:
        away = pair_sum(normed_parts(d_joint, (2, 3)))
        rows = after(jnp.concatenate(normed_one, axis=0), away)
        g_joint = through_rows(rows, d_joint).astype(BF16)
        attention_pieces = split_attention(g_joint, g_project, fast)
    close = pair_sum(normed_parts(after(d_joint, away), (0, 1)))
    d_normed_one = after(far_sum(away), close, attention_pieces) + close
    if fast:
        attention_sum = None
        for step in range(4):
            attention_sum = owner_sum(attention_pieces, step, attention_sum)
        for step in (2, 3):
            forward_sum = owner_sum(forward_pieces, step, forward_sum, attention_pieces)
    else:
        attention_sum = owner_sum_slow(attention_pieces)
    unit_one, scale_one = normed(stream)
    d_stream = d_middle + norm_back(d_normed_one * (1.0 + stretch_one), unit_one, scale_one)
    d_gate_one = per_crop(d_middle * branch * living, sides)
    d_offset_one = per_crop(d_normed_one, sides)
    d_stretch_one = per_crop(d_normed_one * unit_one, sides)
    d_mod = jnp.stack(
        [d_offset_one, d_stretch_one, d_gate_one, d_offset_two, d_stretch_two, d_gate_two], axis=1
    )
    return d_stream, d_mod, attention_sum, forward_sum


def shards(
    hidden_in,
    lengths,
    timesteps,
    head_mask,
    group_mask,
    skip_mask,
    modulation_weight,
    joint_weight,
    project_weight,
    expand_weight,
    reduce_weight,
    cotangent,
):
    seq, groups, planes = sizes()
    block = hidden_in.shape[1]
    crops = lengths.shape[1]
    mine = lax.axis_index(SEQ)
    plane = lax.axis_index("dp")
    group, member = place()
    height = D // planes

    pack = pack_attention(joint_weight[0], project_weight[0])
    if compact():
        first = gather_planes(pack)
        forward_first = gather_planes(
            pack_forward(*after((expand_weight[0], reduce_weight[0]), pack), first)
        )
        first = first + [exchange(piece, TP) for piece in first]
    else:
        first = gather_slow(pack)
        forward_first = gather_slow(pack_forward(expand_weight[0], reduce_weight[0]))
    opened = [open_attention(first)]
    packs = []
    held = first[:4]
    for l in range(1, LAYERS):
        attention = pack_attention(*after((joint_weight[l], project_weight[l]), held))
        held = after((expand_weight[l], reduce_weight[l]), attention)
        packs.append((attention, pack_forward(*held)))
        held = packs[-1]

    stamps = jnp.zeros((planes, crops), jnp.int32)
    for step in range(planes):
        row = from_plane(timesteps[0], step) if step else timesteps[0]
        stamps = jnp.where(
            (jnp.arange(planes) == (plane - step) % planes)[:, None], row[None, :], stamps
        )
    stamps = stamps.reshape(planes * crops)
    embedded = jax.nn.silu(step_embed(stamps, D)).astype(BF16)
    condition = lax.dynamic_slice_in_dim(embedded, plane * height, height, axis=1)
    part = jnp.stack([dot(condition, modulation_weight[l]) for l in range(LAYERS)], axis=1)
    before = jnp.concatenate([jnp.zeros_like(part[:1]), part[:-1]])
    part = jnp.stack([before, part], axis=1)
    part = after(lax.all_to_all(part, EVERY, 0, 0, tiled=True), first[:4])
    part = jnp.sum(part.reshape((planes, seq) + part.shape[1:]), axis=0)
    mods = jnp.transpose(part, (2, 1, 0, 3)).reshape(LAYERS, 2, 6, D)

    bounds = jnp.cumsum(lengths[0])
    span = 2 * block + AFTER
    places = (group * TP - 1) * block + jnp.arange((TP + 1) * block + AFTER, dtype=jnp.int32)
    inside = (places >= 0) & (places < seq * block)
    segment = jnp.where(inside, segment_of(places, bounds), -1)
    segk = jnp.stack(
        [lax.dynamic_slice_in_dim(segment, (member ^ j) * block, span) for j in range(TP)]
    )[:, None, :]
    segq = segk[:, 0, block : 2 * block].reshape(TP * block, 1)
    own = segment_of(mine * block + jnp.arange(block, dtype=jnp.int32), bounds)[:, None]
    sides = [(own == mine - 1).astype(F32), ((own == mine) & (own < crops)).astype(F32)]
    living = (own < crops).astype(F32)
    onehot = (segq == jnp.arange(crops, dtype=jnp.int32)[None, :]).astype(BF16)
    blocks = jnp.stack([group * TP + (member ^ j) for j in range(TP)])
    firsts = jnp.repeat(blocks, block)[:, None]
    slot_sides = jnp.concatenate([segq == firsts - 1, (segq == firsts) & (segq < crops)], axis=1)
    context = (sides, living, segq, segk, slot_sides.astype(F32))
    rows = FF // (planes * seq)
    units = member * groups + jnp.arange(groups, dtype=jnp.int32)
    starts = (FF // planes) * jnp.arange(planes, dtype=jnp.int32)[None, :] + rows * units[:, None]
    hidden_here = (starts[:, :, None] + jnp.arange(rows, dtype=jnp.int32)).reshape(LOCAL_FF)
    spread = (hidden_here // (FF // GROUPS))[None, :] == jnp.arange(GROUPS)[:, None]
    masks = []
    for l in range(LAYERS):
        heads_on = lax.dynamic_slice_in_dim(head_mask[0, l], member * LOCAL_HEADS, LOCAL_HEADS, 1)
        heads_on = jnp.pad(heads_on.astype(BF16), ((0, 0), (0, LANES - LOCAL_HEADS)))
        groups_on = dot(group_mask[0, l].astype(BF16), spread.astype(BF16))
        groups_on = jnp.pad(groups_on, ((1, 0), (0, 0)))
        active = jnp.stack(
            [lax.dynamic_slice_in_dim(groups_on, blocks[j], 2) for j in range(TP)]
        )
        keeping = skip_mask[0, l].astype(F32)[:, None] * living
        masks.append((dot(onehot, heads_on), active, keeping))

    stream = hidden_in[0].astype(F32)
    records, weights, gathered = [], [], []
    for attention, forward in packs:
        gathered.append((gather_slow(attention), gather_slow(forward)))
    w_joint, project_columns = opened[0]
    for l in range(LAYERS):
        events, following = {}, None
        if l + 1 < LAYERS:
            following = open_attention(gathered[l][0])
            events["feedout"] = [following]
        if l == 0 and compact():
            others = [exchange(after(forward_first[0], w_joint), TP)]
            events["normed_one"] = [forward_first[0]]
            events["halos"] = [packs[0][0]]
            events["mixed"] = [others[0], packs[0][1]]

        def hold(name, value, *more, events=events, l=l):
            if l == 0 and compact() and name == "halos":
                others.extend(exchange(after(p, value), TP) for p in forward_first[1:])
                events["branch"] = others[1:3]
            return after(value, *more, *events.get(name, []))

        def open_here(mine, l=l):
            if l == 0:
                return open_forward(forward_first + others if compact() else forward_first)
            return open_forward(gathered[l - 1][1])

        stream, record, used = layer_forward(
            stream, mods[l], w_joint, project_columns, open_here, masks[l], context, hold
        )
        records.append(record)
        weights.append(used)
        if following is not None:
            w_joint, project_columns = following
    final_state = stream.astype(BF16)[None]
    adjoint = cotangent[0].astype(F32)
    grads, d_mods = [None] * LAYERS, [None] * LAYERS
    returned = []
    for l in reversed(range(LAYERS)):

        def hold(name, value, returned=tuple(returned)):
            return after(value, *returned)

        adjoint, d_mods[l], attention, forward = layer_backward(
            adjoint, records[l], mods[l], weights[l], masks[l], context, l == 0, hold
        )
        forward = tuple(return_forward(forward))
        grads[l] = return_attention(attention) + forward
        returned.append(forward)

    d_mod = jnp.stack(d_mods, axis=1)
    d_mod = d_mod[1] + shifted(d_mod[0], -1)
    d_mod = jnp.transpose(d_mod.reshape(LAYERS, seq, 6 * D // seq), (1, 0, 2))
    d_mod = jnp.broadcast_to(d_mod[None], (planes,) + d_mod.shape)
    d_mod = d_mod.reshape((planes * seq,) + d_mod.shape[2:])
    d_mod = lax.all_to_all(d_mod, EVERY, 0, 0, tiled=True)
    modulation_grad = jnp.stack(
        [
            lax.dot_general(
                condition.astype(F32),
                d_mod[:, l],
                (((0,), (0,)), ((), ())),
                precision=HIGH,
                preferred_element_type=F32,
            )
            for l in range(LAYERS)
        ]
    )
    joint_grad, project_grad, expand_grad, reduce_grad = [
        jnp.stack([grads[l][i] for l in range(LAYERS)]) for i in range(4)
    ]
    return (
        final_state,
        adjoint[None],
        modulation_grad,
        joint_grad,
        project_grad,
        expand_grad,
        reduce_grad,
    )


def solution(mesh):
    planes, seq = mesh.shape["dp"], mesh.shape["seq"]
    mesh = Mesh(mesh.devices.reshape(planes, seq // TP, TP), EVERY)
    in_specs = (
        P("dp", SEQ, None),
        P("dp", None),
        P("dp", None),
        P("dp", None, None, None),
        P("dp", None, None, None),
        P("dp", None, SEQ),
        P(None, "dp", SEQ),
        P(None, "dp", SEQ),
        P(None, "dp", SEQ),
        P(None, "dp", SEQ),
        P(None, "dp", SEQ),
        P("dp", SEQ, None),
    )
    out_specs = (
        P("dp", SEQ, None),
        P("dp", SEQ, None),
        P(None, "dp", SEQ),
        P(None, "dp", SEQ),
        P(None, "dp", SEQ),
        P(None, "dp", SEQ),
        P(None, "dp", SEQ),
    )
    return jax.shard_map(shards, mesh=mesh, in_specs=in_specs, out_specs=out_specs, check_vma=False)
```

```python
import functools
import math

import jax
import jax.numpy as jnp
import numpy as np
from jax import lax
from jax.experimental import pallas as pl
from jax.experimental.pallas import tpu as pltpu
from jax.sharding import Mesh
from jax.sharding import PartitionSpec as P

D = 1152
HEADS = 16
HEAD_DIM = 72
FF = 4608
GROUPS = 16
LAYERS = 2

TP = 4
LANES = 128
LOCAL_HEADS = HEADS // TP
LOCAL_FF = FF // TP
WIDTH = -(-LOCAL_HEADS * HEAD_DIM // LANES) * LANES
AFTER = 128
CHUNK = 256

SEQ = ("group", "member")
EVERY = ("dp", "group", "member")
OWNERS = ("dp", "group")

EPS = 1e-06
HIGH = lax.Precision.HIGHEST
NEGATIVE = -1e30
FACTOR = HEAD_DIM ** (-0.5)
F32 = jnp.float32
BF16 = jnp.bfloat16


def sizes():
    groups, planes = lax.axis_size("group"), lax.axis_size("dp")
    return groups * TP, groups, planes


def place():
    return lax.axis_index("group"), lax.axis_index("member")


def here():
    return jnp.stack([lax.axis_index("dp"), *place()])


def device_of(unit, groups):
    return (unit % groups) * TP + unit // groups


def unit_table(seq, groups):
    return np.array([(s % TP) * groups + s // TP for s in range(seq)])


def my_unit():
    _, groups, _ = sizes()
    group, member = place()
    return member * groups + group


def exchange(value, mask):
    seq, _, _ = sizes()
    return lax.ppermute(value, SEQ, [(i, i ^ mask) for i in range(seq)])


def shifted(value, steps):
    count, _, _ = sizes()
    return lax.ppermute(
        value, SEQ, [(i, i + steps) for i in range(count) if 0 <= i + steps < count]
    )


def from_plane(value, back):
    planes = lax.axis_size("dp")
    return lax.ppermute(value, "dp", [(d, (d + back) % planes) for d in range(planes)])


def after(value, *events):
    return lax.optimization_barrier((value,) + events)[0]


def dot(left, right):
    return jnp.dot(left, right, preferred_element_type=F32)


def through_rows(left, right):
    return lax.dot_general(left, right, (((0,), (0,)), ((), ())), preferred_element_type=F32)


def against_cols(left, right):
    return lax.dot_general(left, right, (((1,), (1,)), ((), ())), preferred_element_type=F32)


def near(mine):
    return [mine, exchange(mine, 1)]


def far(theirs):
    return [theirs, exchange(theirs, 1)]


def pair_sum(parts):
    return parts[0].astype(F32) + exchange(parts[1], 1).astype(F32)


def far_sum(pair):
    return exchange(pair.astype(BF16), 2).astype(F32)


def kinds_table(seq, groups):
    pairs, kinds = [], np.zeros((3, seq), np.int32)
    for r in range(3):
        targets = [device_of((3 * s + r) % seq, groups) for s in range(seq)]
        pairs.append(list(enumerate(targets)))
        for s in range(seq):
            kinds[r, targets[s]] = (3 * s + r) // seq
    return pairs, kinds


def my_kinds():
    seq, groups, _ = sizes()
    return jnp.asarray(kinds_table(seq, groups)[1])[:, lax.axis_index(SEQ)]


def deal_joint(joint):
    seq, groups, _ = sizes()
    pairs, _ = kinds_table(seq, groups)
    cols = joint.shape[1] // 3
    return [
        lax.ppermute(joint[:, r * cols : (r + 1) * cols], SEQ, pairs[r]) for r in range(3)
    ]


def return_joint(parts):
    seq, groups, _ = sizes()
    pairs, _ = kinds_table(seq, groups)
    back = [lax.ppermute(part, SEQ, [(b, a) for a, b in pairs[r]]) for r, part in enumerate(parts)]
    return jnp.concatenate(back, axis=1).astype(F32)


def choose(which, options):
    first, second, third = options
    return jnp.where(which == 0, first, jnp.where(which == 1, second, third))


def pack_attention_any(got, project):
    kinds = my_kinds()
    sent = [jnp.where(kinds[0] == k, got[0], jnp.where(kinds[1] == k, got[1], got[2])) for k in range(3)]
    return jnp.concatenate(sent + [project], axis=1)


def open_attention_any(stack):
    _, groups, planes = sizes()
    height, cols = stack.shape[1], stack.shape[2] // 4
    stack = stack.reshape(planes, groups, height, 4, cols)
    kinds = jnp.transpose(stack, (3, 0, 2, 1, 4)).reshape(4, D, groups * cols)
    blank = jnp.zeros((D, WIDTH - groups * cols), BF16)
    joint = jnp.concatenate([part for k in range(3) for part in (kinds[k], blank)], axis=1)
    return joint, kinds[3].reshape(TP, D // TP, groups * cols)


def join_project_any(got):
    _, groups, _ = sizes()
    rows = got.reshape(TP, D // TP, groups, -1).transpose(1, 2, 0, 3).reshape(D // TP, D)
    return jnp.concatenate([rows, jnp.zeros((WIDTH - D // TP, D), BF16)], axis=0)


def split_project_any(grad):
    _, groups, _ = sizes()
    chunks = grad[: D // TP].reshape(D // TP, groups, TP, -1).transpose(2, 0, 1, 3)
    return chunks.reshape(TP, D // TP, -1)


def split_attention_any(g_joint, got):
    _, groups, planes = sizes()
    cols = D // TP // groups
    parts = [g_joint[:, k * WIDTH : k * WIDTH + groups * cols] for k in range(3)]
    parts = jnp.stack(parts + [got.reshape(D, groups * cols)])
    parts = parts.reshape(4, planes, D // planes, groups, cols).transpose(1, 3, 2, 0, 4)
    return parts.reshape(planes * groups, D // planes, 4 * cols)


def unpack_attention_any(owned):
    kinds = my_kinds()
    cols = owned.shape[1] // 4
    own = [owned[:, k * cols : (k + 1) * cols] for k in range(4)]
    return [choose(kinds[r], own[:3]).astype(BF16) for r in range(3)] + [own[3].astype(F32)]


def pack_forward_any(expand, reduce):
    seq, groups, planes = sizes()
    cols, rows = expand.shape[1] // planes, reduce.shape[0] // seq
    chunks = []
    for unit in unit_table(seq, groups):
        q = unit % planes
        chunks += [expand[:, q * cols : (q + 1) * cols], reduce[unit * rows : (unit + 1) * rows]]
    chunks = jnp.concatenate([chunk.reshape(-1, cols) for chunk in chunks], axis=0)
    return chunks.reshape(seq, -1, cols)


def unpack_forward_any(got):
    seq, _, planes = sizes()
    ways, cols = seq // planes, got.shape[2]
    height, width = D // planes, got.shape[2] * planes
    mine = got.reshape((planes, ways) + got.shape[1:])
    mine = lax.dynamic_index_in_dim(mine, my_unit() // planes, 1, keepdims=False)
    expand = jnp.concatenate([mine[d, :height] for d in range(planes)], axis=1)
    reduce = got[:, height:].reshape(seq, cols, D // seq)
    reduce = jnp.concatenate([reduce[s] for s in range(seq)], axis=1)
    blocks = [reduce[:, k * width : (k + 1) * width] for k in range(D // width)]
    return jnp.concatenate([expand] + blocks, axis=0)


def open_forward_any(stack):
    _, groups, planes = sizes()
    height, width = D // planes, stack.shape[2]
    rows = width // planes
    stack = stack.reshape((planes, groups) + stack.shape[1:])
    expand = jnp.transpose(stack[:, :, :height], (0, 2, 1, 3)).reshape(D, groups * width)
    reduce = stack[:, :, height:].reshape(planes, groups, D // width, rows, width)
    reduce = jnp.transpose(reduce, (1, 0, 3, 2, 4)).reshape(groups * planes * rows, D)
    return expand, reduce


def split_forward_any(g_expand, g_reduce):
    _, groups, planes = sizes()
    height, width = D // planes, LOCAL_FF // groups
    rows = width // planes
    expand = g_expand.reshape(planes, height, groups, width).transpose(0, 2, 1, 3)
    reduce = g_reduce.reshape(groups, planes, rows, D // width, width).transpose(1, 0, 3, 2, 4)
    reduce = reduce.reshape(planes, groups, rows * D // width, width)
    stack = jnp.concatenate([expand, reduce], axis=2)
    return stack.reshape((planes * groups,) + stack.shape[2:])


def pack_return_any(owned):
    seq, _, planes = sizes()
    ways, height, width = seq // planes, D // planes, owned.shape[1]
    rows, cols = width // planes, width // planes
    blocks = owned[height:].reshape(D // width, rows, width)
    reduce = jnp.concatenate([blocks[k] for k in range(D // width)], axis=1)
    chunks = []
    for s in range(seq):
        d = s // ways
        chunks.append(owned[:height, d * cols : (d + 1) * cols])
        chunks.append(reduce[:, s * (D // seq) : (s + 1) * (D // seq)].reshape(-1, cols))
    return jnp.concatenate(chunks, axis=0).reshape(seq, -1, cols)


def unpack_return_any(got):
    seq, groups, planes = sizes()
    ways, cols, height = seq // planes, got.shape[2], D // planes
    got = jnp.swapaxes(got.reshape((groups, TP) + got.shape[1:]), 0, 1).reshape(got.shape)
    first = planes * (lax.axis_index(SEQ) % ways)
    mine = lax.dynamic_slice_in_dim(got[:, :height], first, planes)
    expand = jnp.concatenate([mine[q] for q in range(planes)], axis=1)
    return expand.astype(F32), got[:, height:].reshape(-1, D // seq).astype(F32)


def compact():
    seq, groups, planes = sizes()
    return groups == 2 and planes == 4 and D // seq % 16 == 0


def rearrange(body, arrays, outs, name):
    return pl.pallas_call(
        body,
        in_specs=[pl.BlockSpec(memory_space=pltpu.SMEM)]
        + [pl.BlockSpec(memory_space=pltpu.VMEM)] * len(arrays),
        out_specs=[pl.BlockSpec(memory_space=pltpu.VMEM)] * len(outs),
        out_shape=[jax.ShapeDtypeStruct(shape, dtype) for shape, dtype in outs],
        compiler_params=pltpu.CompilerParams(vmem_limit_bytes=48 * 1024 * 1024),
        cost_estimate=pl.CostEstimate(
            flops=0,
            bytes_accessed=sum(math.prod(shape) * 4 for shape, _ in outs),
            transcendentals=0,
        ),
        name=name,
    )(here(), *arrays)


def side_by_side(parts):
    return jnp.concatenate(parts, axis=1)


def kind_sent(me_ref, r):
    unit = me_ref[2] * 2 + me_ref[1]
    source = (3 * (unit + 8 - r)) % 8
    return (3 * source + r) // 8


def pack_attention_kernel(me_ref, a_ref, b_ref, c_ref, project_ref, out_ref):
    cols = a_ref.shape[1]
    first, second = kind_sent(me_ref, 0), kind_sent(me_ref, 1)
    for half in range(2):
        rows = slice(half * cols, (half + 1) * cols)
        a, b, c = a_ref[rows], b_ref[rows], c_ref[rows]
        parts = [jnp.where(first == k, a, jnp.where(second == k, b, c)) for k in range(3)]
        out_ref[:, half * 4 * cols : (half + 1) * 4 * cols] = side_by_side(
            parts + [project_ref[rows]]
        )


def by_plane(me_ref, refs):
    if len(refs) == 1:
        return [(d, refs[0][2 * d], refs[0][2 * d + 1]) for d in range(4)]
    got = []
    for step in range(4):
        own, other = refs[step][...], refs[4 + step][...]
        first = jnp.where(me_ref[1] == 0, own, other)
        second = jnp.where(me_ref[1] == 0, other, own)
        got.append(((me_ref[0] + 4 - step) % 4, first, second))
    return got


def rows_at(start, count):
    if isinstance(start, int):
        return slice(start, start + count)
    return pl.ds(pl.multiple_of(start, 16), count)


def open_attention_kernel(me_ref, *refs):
    *refs, joint_ref, project_ref = refs
    cols = refs[0].shape[-2]
    blank = jnp.zeros((cols, WIDTH - 2 * cols), BF16)
    for plane, first, second in by_plane(me_ref, refs):
        for half in range(2):
            pieces = [
                [piece[:, (4 * half + k) * cols : (4 * half + k + 1) * cols] for k in range(4)]
                for piece in (first, second)
            ]
            parts = []
            for kind in range(3):
                parts += [pieces[0][kind], pieces[1][kind], blank]
            joint_ref[rows_at(plane * 2 * cols + half * cols, cols)] = side_by_side(parts)
            project_ref[plane, half * cols : (half + 1) * cols] = side_by_side(
                [pieces[0][3], pieces[1][3]]
            )


def join_project_kernel(me_ref, got_ref, out_ref):
    cols = got_ref.shape[2] // 2
    rows = got_ref.shape[1]
    out_ref[:rows] = side_by_side(
        [got_ref[t][:, g * cols : (g + 1) * cols] for g in range(2) for t in range(4)]
    )
    out_ref[rows:] = jnp.zeros((out_ref.shape[0] - rows, out_ref.shape[1]), BF16)


def split_project_kernel(me_ref, grad_ref, out_ref):
    rows, cols = out_ref.shape[1], out_ref.shape[2] // 2
    for t in range(4):
        out_ref[t] = side_by_side(
            [grad_ref[:rows, (g * 4 + t) * cols : (g * 4 + t + 1) * cols] for g in range(2)]
        )


def pack_forward_kernel(me_ref, expand_ref, reduce_ref, out_ref):
    cols = reduce_ref.shape[1]
    for s, unit in enumerate(unit_table(8, 2)):
        at = slice(unit % 4 * cols, (unit % 4 + 1) * cols)
        out_ref[s] = side_by_side(
            [
                expand_ref[:cols, at],
                expand_ref[cols:, at],
                reduce_ref[unit * cols : (unit + 1) * cols],
            ]
        )


def unpack_forward_kernel(me_ref, got_ref, out_ref):
    cols = got_ref.shape[1]
    unit = me_ref[2] * 2 + me_ref[1]
    for half in range(2):
        parts = []
        for d in range(4):
            parts.append(got_ref[2 * d + unit // 4][:, half * cols : (half + 1) * cols])
        for s in range(4):
            parts.append(got_ref[4 * half + s][:, 2 * cols :])
        out_ref[half * cols : (half + 1) * cols] = side_by_side(parts)


def open_forward_kernel(me_ref, *refs):
    *refs, expand_ref, reduce_ref = refs
    height = refs[0].shape[-2]
    rows, width = height // 2, D // 2
    for plane, first, second in by_plane(me_ref, refs):
        expand_ref[rows_at(plane * height, height)] = side_by_side(
            [first[:, :width], second[:, :width]]
        )
        for group, piece in enumerate((first, second)):
            reduce_ref[rows_at(group * width + plane * rows, rows)] = side_by_side(
                [piece[:rows, width:], piece[rows:, width:]]
            )


def put_pieces(me_ref, outs, step, pair):
    if len(outs) == 1:
        outs[0][2 * step], outs[0][2 * step + 1] = pair
    else:
        outs[step][...] = jnp.where(me_ref[1] == 0, pair[0], pair[1])
        outs[4 + step][...] = jnp.where(me_ref[1] == 0, pair[1], pair[0])


def split_forward_kernel(me_ref, expand_ref, reduce_ref, *outs):
    height = outs[0].shape[-2]
    rows, width = height // 2, D // 2
    for step in range(4):
        plane = step if len(outs) == 1 else (me_ref[0] + 3 - step) % 4
        expand = expand_ref[rows_at(plane * height, height)]
        pair = []
        for group in range(2):
            reduce = reduce_ref[rows_at(group * width + plane * rows, rows)]
            part = expand[:, group * width : (group + 1) * width]
            upper = side_by_side([part[:rows], reduce[:, :width]])
            lower = side_by_side([part[rows:], reduce[:, width:]])
            pair.append(jnp.concatenate([upper, lower], axis=0))
        put_pieces(me_ref, outs, step, pair)


def pack_return_kernel(me_ref, whole_ref, out_ref):
    cols = out_ref.shape[1]
    for s in range(8):
        at = slice(s // 2 * cols, (s // 2 + 1) * cols)
        right = slice((4 + s % 4) * cols, (5 + s % 4) * cols)
        out_ref[s] = side_by_side(
            [
                whole_ref[:cols, at],
                whole_ref[cols:, at],
                whole_ref[s // 4 * cols : (s // 4 + 1) * cols, right],
            ]
        )


def unpack_return_kernel(me_ref, got_ref, expand_ref, reduce_ref):
    cols = got_ref.shape[1]
    for half in range(2):
        parts = []
        for q in range(4):
            device = q % 2 * 4 + 2 * (me_ref[2] % 2) + q // 2
            parts.append(got_ref[device][:, half * cols : (half + 1) * cols])
        expand_ref[half * cols : (half + 1) * cols] = side_by_side(parts).astype(F32)
    for s, unit in enumerate(unit_table(8, 2)):
        reduce_ref[unit * cols : (unit + 1) * cols] = got_ref[s][:, 2 * cols :].astype(F32)


def split_attention_kernel(me_ref, joint_ref, project_ref, *outs):
    cols = outs[0].shape[-2]
    for step in range(4):
        plane = step if len(outs) == 1 else (me_ref[0] + 3 - step) % 4
        parts = [[], []]
        for half in range(2):
            rows = joint_ref[rows_at(plane * 2 * cols + half * cols, cols)]
            project = project_ref[plane, half * cols : (half + 1) * cols]
            for group in range(2):
                for kind in range(3):
                    at = kind * WIDTH + group * cols
                    parts[group].append(rows[:, at : at + cols])
                parts[group].append(project[:, group * cols : (group + 1) * cols])
        put_pieces(me_ref, outs, step, [side_by_side(part) for part in parts])


def unpack_attention_kernel(me_ref, whole_ref, a_ref, b_ref, c_ref, project_ref):
    cols = whole_ref.shape[0]
    for half in range(2):
        rows = slice(half * cols, (half + 1) * cols)
        parts = []
        for k in range(4):
            at = (half * 4 + k) * cols
            parts.append(whole_ref[:, at : at + cols])
        for r, ref in enumerate((a_ref, b_ref, c_ref)):
            ref[rows] = choose(kind_sent(me_ref, r), parts[:3]).astype(BF16)
        project_ref[rows] = parts[3].astype(F32)


def pack_attention(joint, project):
    got = deal_joint(joint)
    if not compact():
        return pack_attention_any(got, project)
    cols = project.shape[1]
    outs = [((cols, 8 * cols), BF16)]
    return rearrange(pack_attention_kernel, [*got, project], outs, "pack_attention")[0]


def pack_forward(expand, reduce, *events):
    cols = reduce.shape[1]
    if compact():
        outs = [((8, cols, 3 * cols), BF16)]
        (chunks,) = rearrange(pack_forward_kernel, [expand, reduce], outs, "pack_forward")
    else:
        chunks = pack_forward_any(expand, reduce)
    got = after(lax.all_to_all(chunks, SEQ, 0, 0, tiled=True), *events)
    if not compact():
        return unpack_forward_any(got)
    return rearrange(
        unpack_forward_kernel, [got], [((2 * cols, 8 * cols), BF16)], "unpack_forward"
    )[0]


def gather_slow(pack):
    return [lax.all_gather(pack, OWNERS, axis=0, tiled=False)]


def gather_planes(pack):
    return [pack] + [from_plane(pack, back) for back in range(1, 4)]


def open_attention(pieces):
    if not compact():
        return open_attention_any(pieces[0])
    cols = D // 8
    outs = [((D, 3 * WIDTH), BF16), ((TP, 2 * cols, 2 * cols), BF16)]
    return rearrange(open_attention_kernel, pieces, outs, "open_attention")


def project_matrix(columns):
    got = lax.all_to_all(columns, "member", 0, 0, tiled=True)
    if not compact():
        return join_project_any(got)
    return rearrange(join_project_kernel, [got], [((WIDTH, D), BF16)], "join_project")[0]


def open_forward(pieces):
    if not compact():
        return open_forward_any(pieces[0])
    outs = [((D, D), BF16), ((D, D), BF16)]
    return rearrange(open_forward_kernel, pieces, outs, "open_forward")


def piece_outs(shape, fast):
    return [(shape, BF16)] * 8 if fast else [((8,) + shape, BF16)]


def split_project(g_project):
    if compact():
        outs = [((TP, D // TP, D // TP), BF16)]
        (chunks,) = rearrange(split_project_kernel, [g_project], outs, "split_project")
    else:
        chunks = split_project_any(g_project)
    return lax.all_to_all(chunks, "member", 0, 0, tiled=True)


def split_attention(g_joint, project, fast):
    if not compact():
        return [split_attention_any(g_joint, project)]
    outs = piece_outs((D // 8, D), fast)
    return rearrange(split_attention_kernel, [g_joint, project], outs, "split_attention")


def split_forward(g_expand, g_reduce, fast):
    if not compact():
        return [split_forward_any(g_expand, g_reduce)]
    outs = piece_outs((D // 4, D), fast)
    return rearrange(split_forward_kernel, [g_expand, g_reduce], outs, "split_forward")


def owner_sum(pieces, step, carried, *events):
    own, other = pieces[step], after(pieces[4 + step], *events)
    total = own.astype(F32) + exchange(other, TP).astype(F32)
    if step:
        total = total + from_plane(carried, 1).astype(F32)
    return total.astype(BF16)


def owner_sum_slow(pieces):
    return lax.psum_scatter(pieces[0], OWNERS, scatter_dimension=0, tiled=False)


def return_attention(owned):
    if compact():
        cols = D // 8
        outs = [((2 * cols, cols), BF16)] * 3 + [((2 * cols, cols), F32)]
        *parts, project = rearrange(unpack_attention_kernel, [owned], outs, "unpack_attention")
    else:
        *parts, project = unpack_attention_any(owned)
    return return_joint(parts), project


def return_forward(owned):
    cols = D // 8
    if compact():
        outs = [((8, cols, 3 * cols), BF16)]
        (chunks,) = rearrange(pack_return_kernel, [owned], outs, "pack_return")
    else:
        chunks = pack_return_any(owned)
    got = lax.all_to_all(chunks, SEQ, 0, 0, tiled=True)
    if not compact():
        return unpack_return_any(got)
    outs = [((2 * cols, 4 * cols), F32), ((8 * cols, cols), F32)]
    return rearrange(unpack_return_kernel, [got], outs, "unpack_return")


def half_call(body, half, chunks, matrices, tokens, into, partial, name):
    count = chunks[0].shape[0]

    def whole(array):
        return pl.BlockSpec(array.shape, lambda i: (0,) * array.ndim)

    def slot(shape):
        return pl.BlockSpec(shape, lambda i: (2 * half + i,) + (0,) * (len(shape) - 1))

    kept = [array for _, array in into if array is not None]
    operands = [*chunks, *matrices, *tokens]
    specs = [whole(array) for array in (*chunks, *matrices)]
    specs += [slot((array.shape[0] // TP,) + array.shape[1:]) for array in tokens]
    out_specs = [slot((count, width)) for width, _ in into]
    shapes = [jax.ShapeDtypeStruct((TP * count, width), BF16) for width, _ in into]
    if partial:
        out_specs += [pl.BlockSpec((count, D), lambda i: (0, 0))] * 2
        shapes += [jax.ShapeDtypeStruct((count, D), BF16)] * 2
    aliases = {len(operands) + k: k for k in range(len(kept))}
    work = sum(2 * 2 * count * math.prod(matrix.shape) for matrix in matrices)

    def kernel(a_ref, b_ref, *refs):
        n = len(matrices) + len(tokens)
        mine = pl.program_id(0) == 0
        rows = jnp.where(mine, a_ref[...], b_ref[...])
        body(rows, mine, refs[:n], refs[n + len(kept) :])

    return pl.pallas_call(
        kernel,
        grid=(2,),
        in_specs=specs + [pl.BlockSpec(memory_space=pl.ANY)] * len(kept),
        out_specs=out_specs,
        out_shape=shapes,
        input_output_aliases=aliases,
        compiler_params=kernel_params(),
        cost_estimate=pl.CostEstimate(
            flops=work, bytes_accessed=work // 512, transcendentals=2 * count * D
        ),
        name=name,
    )(*operands, *kept)


def put_partial(mine, value, a_ref, b_ref):
    value = value.astype(BF16)

    @pl.when(mine)
    def _():
        a_ref[...] = value

    @pl.when(jnp.logical_not(mine))
    def _():
        b_ref[...] = value


def chunks_of(width):
    return [slice(at, min(at + CHUNK, width)) for at in range(0, width, CHUNK)]


def joint_body(rows, mine, refs, outs):
    outs[0][...] = dot(rows, refs[0][...]).astype(BF16)


def forward_body(rows, mine, refs, outs):
    expand_ref, reduce_ref, sides_ref, active_ref = refs
    activated_ref, slope_ref, a_ref, b_ref = outs
    root = math.sqrt(2.0 / math.pi)
    before, now = sides_ref[:, 0:1], sides_ref[:, 1:2]
    for at in chunks_of(LOCAL_FF):
        pre = dot(rows, expand_ref[:, at])
        square = pre * pre
        curve = jnp.tanh(root * pre * (1.0 + 0.044715 * square))
        half = 0.5 + 0.5 * curve
        mask = before * active_ref[0, 0:1, at] + now * active_ref[0, 1:2, at]
        slope = half + pre * (half - half * half) * (2.0 * root * (1.0 + 0.134145 * square))
        activated_ref[:, at] = (pre * half * mask).astype(BF16)
        slope_ref[:, at] = (slope * mask).astype(BF16)
    put_partial(mine, dot(activated_ref[...], reduce_ref[...]), a_ref, b_ref)


def backward_body(rows, mine, refs, outs):
    expand_ref, reduce_ref, slope_ref = refs
    d_pre_ref, a_ref, b_ref = outs
    for at in chunks_of(LOCAL_FF):
        d_active = against_cols(rows, reduce_ref[at])
        d_pre_ref[:, at] = (d_active * slope_ref[:, at].astype(F32)).astype(BF16)
    put_partial(mine, against_cols(d_pre_ref[...], expand_ref[...]), a_ref, b_ref)


def head_tiles(head):
    low = head * HEAD_DIM // LANES * LANES
    high = -(-(head + 1) * HEAD_DIM // LANES) * LANES
    return low, high


def lanes_of(head, shape):
    low, high = head_tiles(head)
    lane = lax.broadcasted_iota(jnp.int32, shape, 1) + low
    return (lane >= head * HEAD_DIM) & (lane < (head + 1) * HEAD_DIM)


def key_tiles(refs, halos, block, base, low, high):
    before_ref, after_ref = halos
    prev_ref, here_ref, next_ref = refs
    prev = jnp.where(block == 0, before_ref[:, base + low : base + high], prev_ref[:, low:high])
    following = jnp.where(
        block == TP - 1, after_ref[:, base + low : base + high], next_ref[:, low:high]
    )
    return prev, here_ref[:, low:high], following


def attend_kernel(
    me_ref,
    q_ref,
    *refs,
):
    keys, values, halos = refs[0:3], refs[3:6], refs[6:8]
    segq_ref, segk_ref, head_ref, mixed_ref, lse_ref = refs[8:]
    block = pl.program_id(0) ^ me_ref[2]
    count = q_ref.shape[0]
    allowed = segq_ref[...] == segk_ref[0]
    tiles = [jnp.zeros((count, LANES), F32) for _ in range(WIDTH // LANES)]
    total = jnp.zeros((count, LANES), F32)
    lane = lax.broadcasted_iota(jnp.int32, (count, LANES), 1)
    for head in range(LOCAL_HEADS):
        low, high = head_tiles(head)
        mine = lanes_of(head, (count, high - low))
        query = jnp.where(mine, q_ref[:, low:high], 0)
        key = key_tiles(keys, halos, block, 0, low, high)
        scores = jnp.concatenate([against_cols(query, part) for part in key], axis=1) * FACTOR
        scores = jnp.where(allowed, scores, NEGATIVE)
        highest = jnp.max(scores, axis=-1, keepdims=True)
        weights = jnp.exp(scores - highest)
        sums = jnp.sum(weights, axis=-1, keepdims=True)
        probs = (weights / sums).astype(BF16)
        out, at = 0.0, 0
        for part in key_tiles(values, halos, block, WIDTH, low, high):
            out = out + dot(probs[:, at : at + part.shape[0]], part)
            at += part.shape[0]
        out = jnp.where(mine, out, 0.0) * head_ref[:, head : head + 1]
        for k in range(low // LANES, high // LANES):
            at = k * LANES - low
            tiles[k] = tiles[k] + out[:, at : at + LANES]
        total = jnp.where(lane == head, highest + jnp.log(sums), total)
    for k, tile in enumerate(tiles):
        mixed_ref[:, k * LANES : (k + 1) * LANES] = tile.astype(BF16)
    lse_ref[...] = total


def attend_back_kernel(me_ref, q_ref, *refs):
    keys, values, halos = refs[0:3], refs[3:6], refs[6:8]
    grad_ref, mixed_ref, lse_ref, segq_ref, segk_ref, head_ref = refs[8:14]
    d_joint_ref, d_before_ref, d_after_ref, sum_ref = refs[14:]
    step = pl.program_id(0)
    block = step ^ me_ref[2]
    count = q_ref.shape[0]

    @pl.when(step == 0)
    def _():
        sum_ref[...] = jnp.zeros_like(sum_ref)

    prev = jnp.where(block == 0, TP, jnp.maximum(block - 1, 0) ^ me_ref[2])
    following = jnp.where(block == TP - 1, TP + 1, jnp.minimum(block + 1, TP - 1) ^ me_ref[2])
    windows = [
        (pl.ds(pl.multiple_of(prev * count, count), count), 0),
        (pl.ds(pl.multiple_of(step * count, count), count), count),
        (pl.ds(pl.multiple_of(following * count, count), AFTER), 2 * count),
    ]
    rows = pl.ds(pl.multiple_of(step * count, count), count)
    allowed = segq_ref[...] == segk_ref[0]
    tiles = [jnp.zeros((count, LANES), F32) for _ in range(WIDTH // LANES)]
    for head in range(LOCAL_HEADS):
        low, high = head_tiles(head)
        mine = lanes_of(head, (count, high - low))
        query = jnp.where(mine, q_ref[:, low:high], 0)
        key = key_tiles(keys, halos, block, 0, low, high)
        value = key_tiles(values, halos, block, WIDTH, low, high)
        active = head_ref[:, head : head + 1]
        grad = jnp.where(mine, grad_ref[:, low:high].astype(F32) * active, 0.0)
        balance = jnp.sum(grad * mixed_ref[:, low:high].astype(F32), axis=-1, keepdims=True)
        grad = grad.astype(BF16)
        scores = jnp.concatenate([against_cols(query, part) for part in key], axis=1) * FACTOR
        probs = jnp.where(allowed, jnp.exp(scores - lse_ref[:, head : head + 1]), 0.0)
        d_probs = jnp.concatenate([against_cols(grad, part) for part in value], axis=1)
        d_scores = (probs * (d_probs - balance)).astype(BF16)
        probs = probs.astype(BF16)
        d_query = 0.0
        for (window, at), part in zip(windows, key):
            piece = d_scores[:, at : at + part.shape[0]]
            d_query = d_query + dot(piece, part)
            sum_ref[window, low:high] += through_rows(piece, query) * FACTOR
            sum_ref[window, WIDTH + low : WIDTH + high] += through_rows(
                probs[:, at : at + part.shape[0]], grad
            )
        d_query = jnp.where(mine, d_query, 0.0)
        for k in range(low // LANES, high // LANES):
            at = k * LANES - low
            tiles[k] = tiles[k] + d_query[:, at : at + LANES]
    for k, tile in enumerate(tiles):
        d_joint_ref[rows, k * LANES : (k + 1) * LANES] = (tile * FACTOR).astype(BF16)

    @pl.when(step == pl.num_programs(0) - 1)
    def _():
        d_joint_ref[:, WIDTH:] = sum_ref[: TP * count].astype(BF16)
        d_before_ref[...] = sum_ref[TP * count : (TP + 1) * count].astype(BF16)
        d_after_ref[...] = sum_ref[(TP + 1) * count : (TP + 1) * count + AFTER].astype(BF16)


def kernel_params():
    return pltpu.CompilerParams(
        dimension_semantics=("arbitrary",), vmem_limit_bytes=48 * 1024 * 1024
    )


def block_specs(count):
    def rows(width):
        return pl.BlockSpec((count, width), lambda j, me: (j, 0))

    def whole(shape):
        return pl.BlockSpec(shape, lambda j, me: (0,) * len(shape))

    def around(kind):
        def before(j, me):
            return (jnp.maximum((j ^ me[2]) - 1, 0) ^ me[2], kind)

        def following(j, me):
            return ((jnp.minimum((j ^ me[2]) + 1, TP - 1) ^ me[2]) * (count // AFTER), kind)

        return [
            pl.BlockSpec((count, WIDTH), before),
            pl.BlockSpec((count, WIDTH), lambda j, me: (j, kind)),
            pl.BlockSpec((AFTER, WIDTH), following),
        ]

    fixed = [rows(WIDTH)] + around(1) + around(2)
    return rows, whole, fixed + [whole((count, 2 * WIDTH)), whole((AFTER, 2 * WIDTH))]


def attend(joint, halos, segq, segk, heads):
    span = segk.shape[2]
    count = joint.shape[0] // TP
    rows, whole, specs = block_specs(count)
    return pl.pallas_call(
        attend_kernel,
        grid_spec=pltpu.PrefetchScalarGridSpec(
            num_scalar_prefetch=1,
            grid=(TP,),
            in_specs=specs
            + [
                rows(1),
                pl.BlockSpec((1, 1, span), lambda j, me: (j, 0, 0)),
                rows(LANES),
            ],
            out_specs=[rows(WIDTH), rows(LANES)],
        ),
        out_shape=[
            jax.ShapeDtypeStruct((TP * count, WIDTH), BF16),
            jax.ShapeDtypeStruct((TP * count, LANES), F32),
        ],
        compiler_params=kernel_params(),
        cost_estimate=pl.CostEstimate(
            flops=8 * TP * count * span * LANES * LOCAL_HEADS,
            bytes_accessed=TP * count * WIDTH * 8,
            transcendentals=TP * count * span * LOCAL_HEADS,
        ),
        name="attend",
    )(here(), *[joint] * 7, *halos, segq, segk, heads)


def attend_back(joint, halos, grad, mixed, log_total, segq, segk, heads):
    span = segk.shape[2]
    count = joint.shape[0] // TP
    rows, whole, specs = block_specs(count)
    shapes = [(TP * count, 3 * WIDTH), (count, 2 * WIDTH), (AFTER, 2 * WIDTH)]
    return pl.pallas_call(
        attend_back_kernel,
        grid_spec=pltpu.PrefetchScalarGridSpec(
            num_scalar_prefetch=1,
            grid=(TP,),
            in_specs=specs
            + [
                rows(WIDTH),
                rows(WIDTH),
                rows(LANES),
                rows(1),
                pl.BlockSpec((1, 1, span), lambda j, me: (j, 0, 0)),
                rows(LANES),
            ],
            out_specs=[whole(shape) for shape in shapes],
            scratch_shapes=[pltpu.VMEM(((TP + 2) * count, 2 * WIDTH), F32)],
        ),
        out_shape=[jax.ShapeDtypeStruct(shape, BF16) for shape in shapes],
        compiler_params=kernel_params(),
        cost_estimate=pl.CostEstimate(
            flops=20 * TP * count * span * LANES * LOCAL_HEADS,
            bytes_accessed=TP * count * WIDTH * 20,
            transcendentals=TP * count * span * LOCAL_HEADS,
        ),
        name="attend_back",
    )(here(), *[joint] * 7, *halos, grad, mixed, log_total, segq, segk, heads)


def halos_of(joint):
    _, groups, _ = sizes()
    count = joint.shape[0] // TP
    if groups == 1:
        return [jnp.zeros((rows, 2 * WIDTH), joint.dtype) for rows in (count, AFTER)]
    group, member = place()
    column = jnp.int32(WIDTH)
    last = ((member ^ (TP - 1)) * count, column)
    if groups == 2:
        first = (member * count, column)
        start = [jnp.where(group == 0, x, y) for x, y in zip(last, first)]
        got = exchange(lax.dynamic_slice(joint, start, (count, 2 * WIDTH)), TP)
        return [got, got]
    last = lax.dynamic_slice(joint, last, (count, 2 * WIDTH))
    first = lax.dynamic_slice(joint, (member * count, column), (AFTER, 2 * WIDTH))
    return [shifted(last, TP), shifted(first, -TP)]


def halos_back(d_joint, d_before, d_after):
    _, groups, _ = sizes()
    if groups == 1:
        return d_joint
    group, member = place()
    count = d_joint.shape[0] // TP
    last, first = (member ^ (TP - 1)) * count, member * count
    if groups == 2:
        d_after = jnp.pad(d_after, ((0, count - AFTER), (0, 0)))
        got = exchange(jnp.where(group == 0, d_after, d_before), TP)
        pieces = [(got, jnp.where(group == 0, last, first))]
    else:
        pieces = [(shifted(d_before, -TP), last), (shifted(d_after, TP), first)]
    for piece, at in pieces:
        start = (at, jnp.int32(WIDTH))
        sums = lax.dynamic_slice(d_joint, start, piece.shape)
        sums = (sums.astype(F32) + piece.astype(F32)).astype(BF16)
        d_joint = lax.dynamic_update_slice(d_joint, sums, start)
    return d_joint


def normed(stream):
    center = stream - jnp.mean(stream, axis=-1, keepdims=True)
    scale = lax.rsqrt(jnp.mean(center * center, axis=-1, keepdims=True) + EPS)
    return center * scale, scale


def norm_back(grad, unit, scale):
    mean = jnp.mean(grad, axis=-1, keepdims=True)
    slope = jnp.mean(grad * unit, axis=-1, keepdims=True)
    return scale * (grad - mean - unit * slope)


def per_token(vectors, sides):
    return sides[0] * vectors[0][None, :] + sides[1] * vectors[1][None, :]


def per_crop(value, sides):
    return jnp.stack([jnp.sum(value * sides[0], axis=0), jnp.sum(value * sides[1], axis=0)])


def step_embed(stamps, breadth):
    halfway = breadth // 2
    frequency = jnp.exp(-math.log(10000.0) * jnp.arange(halfway, dtype=F32) / halfway)
    angles = stamps.astype(F32)[..., None] * frequency
    return jnp.concatenate([jnp.cos(angles), jnp.sin(angles)], axis=-1)


def segment_of(places, bounds):
    return jnp.sum((places[:, None] >= bounds[None, :]).astype(jnp.int32), axis=-1)


def layer_forward(stream, mod, w_joint, project_columns, open_reduce, masks, context, hold):
    head_tok, active, keeping = masks
    sides, living, segq, segk, slot_sides = context
    offset_one, stretch_one, gate_one, offset_two, stretch_two, gate_two = [
        per_token(mod[:, i], sides) for i in range(6)
    ]
    count = stream.shape[0]
    unit_one, _ = normed(stream)
    mine = (unit_one * (1.0 + stretch_one) + offset_one).astype(BF16)
    mine = hold("normed_one", mine)
    theirs, ours = exchange(mine, 2), near(mine)
    (joint,) = half_call(
        joint_body, 0, ours, [w_joint], [], [(3 * WIDTH, None)], False, "joint_near"
    )
    theirs = far(hold("far_one", theirs, joint))
    (joint,) = half_call(
        joint_body, 1, theirs, [w_joint], [], [(3 * WIDTH, joint)], False, "joint_far"
    )
    normed_one = ours + theirs
    halos = halos_of(joint)
    w_project = project_matrix(after(project_columns, joint))
    halos = hold("halos", halos)
    mixed, log_total = attend(joint, halos, segq, segk, head_tok)
    mixed = hold("mixed", mixed)

    def branch_parts(rows, slots):
        return [dot(rows[j * count : (j + 1) * count], w_project).astype(BF16) for j in slots]

    away = pair_sum(branch_parts(mixed, (2, 3)))
    close = pair_sum(branch_parts(after(mixed, away), (0, 1)))
    branch = after(hold("branch", far_sum(away)), close) + close
    middle = stream + gate_one * branch * living
    unit_two, _ = normed(middle)
    mine = (unit_two * (1.0 + stretch_two) + offset_two).astype(BF16)
    theirs, ours = exchange(mine, 2), near(mine)
    w_expand, w_reduce = open_reduce(mine)
    matrices, tokens = [w_expand, w_reduce], [slot_sides, active]
    activated, slope, *parts = half_call(
        forward_body, 0, ours, matrices, tokens, [(LOCAL_FF, None)] * 2, True, "forward_near"
    )
    close = pair_sum(parts)
    theirs = far(hold("far_two", theirs, activated))
    activated, slope, *parts = half_call(
        forward_body,
        1,
        theirs,
        matrices,
        tokens,
        [(LOCAL_FF, activated), (LOCAL_FF, slope)],
        True,
        "forward_far",
    )
    away = pair_sum(parts)
    feedout = hold("feedout", far_sum(away), away) + close
    result = middle + gate_two * feedout * keeping
    record = (
        stream,
        normed_one,
        joint,
        halos,
        mixed,
        log_total,
        branch,
        middle,
        ours + theirs,
        slope,
        activated,
        feedout,
    )
    return result, record, (w_joint, w_project, w_expand, w_reduce)


def layer_backward(adjoint, record, mod, weights, masks, context, last, hold):
    (
        stream,
        normed_one,
        joint,
        halos,
        mixed,
        log_total,
        branch,
        middle,
        normed_two,
        slope,
        activated,
        feedout,
    ) = record
    w_joint, w_project, w_expand, w_reduce = weights
    head_tok, active, keeping = masks
    sides, living, segq, segk, slot_sides = context
    offset_one, stretch_one, gate_one, offset_two, stretch_two, gate_two = [
        per_token(mod[:, i], sides) for i in range(6)
    ]
    count = stream.shape[0]
    fast = compact()
    mine = (adjoint * gate_two * keeping).astype(BF16)
    theirs, ours = exchange(mine, 2), near(mine)
    matrices = [w_expand, w_reduce]
    d_pre, *parts = half_call(
        backward_body, 0, ours, matrices, [slope], [(LOCAL_FF, None)], True, "backward_near"
    )
    close = pair_sum(parts)
    theirs = far(hold("far_feed", theirs, d_pre))
    d_pre, *parts = half_call(
        backward_body, 1, theirs, matrices, [slope], [(LOCAL_FF, d_pre)], True, "backward_far"
    )
    away = pair_sum(parts)
    d_feed = jnp.concatenate(ours + theirs, axis=0)
    g_reduce = through_rows(activated, after(d_feed, away)).astype(BF16)
    d_gate_two = per_crop(after(adjoint, away) * feedout * keeping, sides)
    unit_two, scale_two = normed(middle)
    d_normed_two = hold("d_normed_two", far_sum(away), g_reduce, d_gate_two) + close
    d_middle = adjoint + norm_back(d_normed_two * (1.0 + stretch_two), unit_two, scale_two)
    mine = (d_middle * gate_one * living).astype(BF16)
    theirs, ours = exchange(mine, 2), near(mine)
    rows = after(jnp.concatenate(normed_two, axis=0), ours)
    g_expand = through_rows(rows, d_pre).astype(BF16)
    forward_pieces = split_forward(g_expand, g_reduce, False)
    d_offset_two = per_crop(after(d_normed_two, mine), sides)
    d_stretch_two = per_crop(after(d_normed_two, mine) * unit_two, sides)
    theirs = hold("d_branch", theirs, forward_pieces, d_offset_two, d_stretch_two)
    forward_sum = owner_sum_slow(forward_pieces)
    d_branch = jnp.concatenate(ours + far(theirs), axis=0)
    d_mixed = against_cols(d_branch, w_project).astype(BF16)
    g_project = split_project(through_rows(mixed, d_branch).astype(BF16))
    d_mixed = hold("d_mixed", d_mixed)
    d_joint = halos_back(
        *attend_back(joint, halos, d_mixed, mixed, log_total, segq, segk, head_tok)
    )
    d_joint = hold("d_joint", d_joint)

    def normed_parts(rows, slots):
        return [against_cols(rows[j * count : (j + 1) * count], w_joint).astype(BF16) for j in slots]

    if last:
        g_joint = through_rows(jnp.concatenate(normed_one, axis=0), d_joint).astype(BF16)
        attention_pieces = split_attention(g_joint, g_project, fast)
        away = pair_sum(normed_parts(after(d_joint, attention_pieces), (2, 3)))
    else:
        away = pair_sum(normed_parts(d_joint, (2, 3)))
        rows = after(jnp.concatenate(normed_one, axis=0), away)
        g_joint = through_rows(rows, d_joint).astype(BF16)
        attention_pieces = split_attention(g_joint, g_project, fast)
    close = pair_sum(normed_parts(after(d_joint, away), (0, 1)))
    d_normed_one = after(far_sum(away), close, attention_pieces) + close
    unit_one, scale_one = normed(stream)
    d_stream = d_middle + norm_back(d_normed_one * (1.0 + stretch_one), unit_one, scale_one)
    d_gate_one = per_crop(d_middle * branch * living, sides)
    d_offset_one = per_crop(d_normed_one, sides)
    d_stretch_one = per_crop(d_normed_one * unit_one, sides)
    d_mod = jnp.stack(
        [d_offset_one, d_stretch_one, d_gate_one, d_offset_two, d_stretch_two, d_gate_two], axis=1
    )
    return d_stream, d_mod, attention_pieces, forward_sum


def shards(
    hidden_in,
    lengths,
    timesteps,
    head_mask,
    group_mask,
    skip_mask,
    modulation_weight,
    joint_weight,
    project_weight,
    expand_weight,
    reduce_weight,
    cotangent,
):
    seq, groups, planes = sizes()
    block = hidden_in.shape[1]
    crops = lengths.shape[1]
    mine = lax.axis_index(SEQ)
    plane = lax.axis_index("dp")
    group, member = place()
    height = D // planes

    pack = pack_attention(joint_weight[0], project_weight[0])
    if compact():
        first = gather_planes(pack)
        forward_first = gather_planes(
            pack_forward(*after((expand_weight[0], reduce_weight[0]), pack), first)
        )
        for k in range(4):
            first.append(exchange(after(first[k], first[-1]) if k else first[0], TP))
        mod_events, normed_events = [first[1], first[4]], [forward_first[0], first[5]]
    else:
        first = gather_slow(pack)
        forward_first = gather_slow(pack_forward(expand_weight[0], reduce_weight[0]))
        mod_events, normed_events = [], []
    opened = open_attention(first)
    packs = []
    held = opened
    for l in range(1, LAYERS):
        forward = pack_forward(*after((expand_weight[l], reduce_weight[l]), held))
        attention = pack_attention(*after((joint_weight[l], project_weight[l]), forward))
        packs.append((attention, forward))
        held = attention

    stamps = jnp.zeros((planes, crops), jnp.int32)
    for step in range(planes):
        row = from_plane(timesteps[0], step) if step else timesteps[0]
        stamps = jnp.where(
            (jnp.arange(planes) == (plane - step) % planes)[:, None], row[None, :], stamps
        )
    stamps = stamps.reshape(planes * crops)
    embedded = jax.nn.silu(step_embed(stamps, D)).astype(BF16)
    condition = lax.dynamic_slice_in_dim(embedded, plane * height, height, axis=1)
    part = jnp.stack([dot(condition, modulation_weight[l]) for l in range(LAYERS)], axis=1)
    before = jnp.concatenate([jnp.zeros_like(part[:1]), part[:-1]])
    part = jnp.stack([before, part], axis=1)
    part = after(lax.all_to_all(part, EVERY, 0, 0, tiled=True), mod_events)
    part = jnp.sum(part.reshape((planes, seq) + part.shape[1:]), axis=0)
    mods = jnp.transpose(part, (2, 1, 0, 3)).reshape(LAYERS, 2, 6, D)

    bounds = jnp.cumsum(lengths[0])
    span = 2 * block + AFTER
    places = (group * TP - 1) * block + jnp.arange((TP + 1) * block + AFTER, dtype=jnp.int32)
    inside = (places >= 0) & (places < seq * block)
    segment = jnp.where(inside, segment_of(places, bounds), -1)
    segk = jnp.stack(
        [lax.dynamic_slice_in_dim(segment, (member ^ j) * block, span) for j in range(TP)]
    )[:, None, :]
    segq = segk[:, 0, block : 2 * block].reshape(TP * block, 1)
    own = segment_of(mine * block + jnp.arange(block, dtype=jnp.int32), bounds)[:, None]
    sides = [(own == mine - 1).astype(F32), ((own == mine) & (own < crops)).astype(F32)]
    living = (own < crops).astype(F32)
    onehot = (segq == jnp.arange(crops, dtype=jnp.int32)[None, :]).astype(BF16)
    blocks = jnp.stack([group * TP + (member ^ j) for j in range(TP)])
    firsts = jnp.repeat(blocks, block)[:, None]
    slot_sides = jnp.concatenate([segq == firsts - 1, (segq == firsts) & (segq < crops)], axis=1)
    context = (sides, living, segq, segk, slot_sides.astype(F32))
    rows = FF // (planes * seq)
    units = member * groups + jnp.arange(groups, dtype=jnp.int32)
    starts = (FF // planes) * jnp.arange(planes, dtype=jnp.int32)[None, :] + rows * units[:, None]
    hidden_here = (starts[:, :, None] + jnp.arange(rows, dtype=jnp.int32)).reshape(LOCAL_FF)
    spread = (hidden_here // (FF // GROUPS))[None, :] == jnp.arange(GROUPS)[:, None]
    masks = []
    for l in range(LAYERS):
        heads_on = lax.dynamic_slice_in_dim(head_mask[0, l], member * LOCAL_HEADS, LOCAL_HEADS, 1)
        heads_on = jnp.pad(heads_on.astype(BF16), ((0, 0), (0, LANES - LOCAL_HEADS)))
        groups_on = dot(group_mask[0, l].astype(BF16), spread.astype(BF16))
        groups_on = jnp.pad(groups_on, ((1, 0), (0, 0)))
        active = jnp.stack(
            [lax.dynamic_slice_in_dim(groups_on, blocks[j], 2) for j in range(TP)]
        )
        keeping = skip_mask[0, l].astype(F32)[:, None] * living
        masks.append((dot(onehot, heads_on), active, keeping))

    stream = hidden_in[0].astype(F32)
    records, weights = [], []
    w_joint, project_columns = opened
    forward_slow = [gather_slow(forward) for _, forward in packs]
    for l in range(LAYERS):
        events, pieces, others = {}, [], []
        if l + 1 < LAYERS:
            attention, forward = packs[l]
            events["halos"], events["mixed"] = [forward], [attention]
            pieces = gather_planes(attention) if compact() else gather_slow(attention)
        if l == 0 and compact():
            first_others = [exchange(after(forward_first[0], w_joint), TP)]
            events["normed_one"] = normed_events
            events["far_one"] = [forward_first[1]]
            events["halos"] = events["halos"] + [forward_first[2]]
            events["mixed"] = events["mixed"] + [forward_first[3], first_others[0]]

        def hold(name, value, *more, events=events, l=l, pieces=pieces, others=others):
            if l == 0 and compact() and name == "halos":
                first_others.extend(exchange(after(p, value), TP) for p in forward_first[1:])
                events["branch"] = first_others[1:3]
            if l + 1 < LAYERS and name == "branch" and compact():
                events["branch"] = events.get("branch", []) + pieces[1:2]
            if l + 1 < LAYERS and name == "far_two":
                if compact():
                    events["far_two"] = pieces[2:]
                    for k in range(4):
                        others.append(exchange(after(pieces[k], *others[-1:]), TP))
                following.append(open_attention(pieces + others))
                events["feedout"] = following
            return after(value, *more, *events.get(name, []))

        def open_here(mine, l=l):
            if l == 0:
                return open_forward(forward_first + first_others if compact() else forward_first)
            return open_forward(forward_slow[l - 1])

        following = []
        stream, record, used = layer_forward(
            stream, mods[l], w_joint, project_columns, open_here, masks[l], context, hold
        )
        records.append(record)
        weights.append(used)
        if following:
            w_joint, project_columns = following[0]
    final_state = stream.astype(BF16)[None]
    adjoint = cotangent[0].astype(F32)
    grads, d_mods = [None] * LAYERS, [None] * LAYERS
    waiting = None
    for l in reversed(range(LAYERS)):
        state = {}

        def hold(name, value, *more, waiting=waiting, state=state):
            events = []
            if waiting is not None:
                above, pieces, forward_sum = waiting
                steps = ["far_feed", "d_normed_two", "d_branch", "d_mixed"]
                if compact() and name in steps:
                    step = steps.index(name)
                    state["sum"] = owner_sum(pieces, step, state.get("sum"))
                    events.append(state["sum"])
                if name == "d_branch":
                    state["forward"] = tuple(return_forward(forward_sum))
                    events.append(state["forward"])
                if name == "d_joint":
                    owned = state["sum"] if compact() else owner_sum_slow(pieces)
                    state["attention"] = return_attention(owned)
                    grads[above] = state["attention"] + state["forward"]
                    events.append(state["attention"])
            return after(value, *more, *events)

        adjoint, d_mods[l], pieces, forward_sum = layer_backward(
            adjoint, records[l], mods[l], weights[l], masks[l], context, l == 0, hold
        )
        waiting = (l, pieces, forward_sum)
    _, pieces, forward_sum = waiting
    if compact():
        owned = None
        for step in range(4):
            owned = owner_sum(pieces, step, owned)
    else:
        owned = owner_sum_slow(pieces)
    grads[0] = return_attention(owned) + tuple(return_forward(forward_sum))

    d_mod = jnp.stack(d_mods, axis=1)
    d_mod = d_mod[1] + shifted(d_mod[0], -1)
    d_mod = jnp.transpose(d_mod.reshape(LAYERS, seq, 6 * D // seq), (1, 0, 2))
    d_mod = jnp.broadcast_to(d_mod[None], (planes,) + d_mod.shape)
    d_mod = d_mod.reshape((planes * seq,) + d_mod.shape[2:])
    d_mod = lax.all_to_all(d_mod, EVERY, 0, 0, tiled=True)
    modulation_grad = jnp.stack(
        [
            lax.dot_general(
                condition.astype(F32),
                d_mod[:, l],
                (((0,), (0,)), ((), ())),
                precision=HIGH,
                preferred_element_type=F32,
            )
            for l in range(LAYERS)
        ]
    )
    joint_grad, project_grad, expand_grad, reduce_grad = [
        jnp.stack([grads[l][i] for l in range(LAYERS)]) for i in range(4)
    ]
    return (
        final_state,
        adjoint[None],
        modulation_grad,
        joint_grad,
        project_grad,
        expand_grad,
        reduce_grad,
    )


def solution(mesh):
    planes, seq = mesh.shape["dp"], mesh.shape["seq"]
    mesh = Mesh(mesh.devices.reshape(planes, seq // TP, TP), EVERY)
    in_specs = (
        P("dp", SEQ, None),
        P("dp", None),
        P("dp", None),
        P("dp", None, None, None),
        P("dp", None, None, None),
        P("dp", None, SEQ),
        P(None, "dp", SEQ),
        P(None, "dp", SEQ),
        P(None, "dp", SEQ),
        P(None, "dp", SEQ),
        P(None, "dp", SEQ),
        P("dp", SEQ, None),
    )
    out_specs = (
        P("dp", SEQ, None),
        P("dp", SEQ, None),
        P(None, "dp", SEQ),
        P(None, "dp", SEQ),
        P(None, "dp", SEQ),
        P(None, "dp", SEQ),
        P(None, "dp", SEQ),
    )
    return jax.shard_map(shards, mesh=mesh, in_specs=in_specs, out_specs=out_specs, check_vma=False)
```

```python
import functools
import math

import jax
import jax.numpy as jnp
import numpy as np
from jax import lax
from jax.experimental import pallas as pl
from jax.experimental.pallas import tpu as pltpu
from jax.sharding import Mesh
from jax.sharding import PartitionSpec as P

D = 1152
HEADS = 16
HEAD_DIM = 72
FF = 4608
GROUPS = 16
LAYERS = 2

TP = 4
LANES = 128
LOCAL_HEADS = HEADS // TP
LOCAL_FF = FF // TP
WIDTH = -(-LOCAL_HEADS * HEAD_DIM // LANES) * LANES
AFTER = 128
CHUNK = 256

SEQ = ("group", "member")
EVERY = ("dp", "group", "member")
OWNERS = ("dp", "group")

EPS = 1e-06
HIGH = lax.Precision.HIGHEST
NEGATIVE = -1e30
FACTOR = HEAD_DIM ** (-0.5)
F32 = jnp.float32
BF16 = jnp.bfloat16


def sizes():
    groups, planes = lax.axis_size("group"), lax.axis_size("dp")
    return groups * TP, groups, planes


def place():
    return lax.axis_index("group"), lax.axis_index("member")


def here():
    return jnp.stack([lax.axis_index("dp"), *place()])


def device_of(unit, groups):
    return (unit % groups) * TP + unit // groups


def unit_table(seq, groups):
    return np.array([(s % TP) * groups + s // TP for s in range(seq)])


def my_unit():
    _, groups, _ = sizes()
    group, member = place()
    return member * groups + group


def exchange(value, mask):
    seq, _, _ = sizes()
    return lax.ppermute(value, SEQ, [(i, i ^ mask) for i in range(seq)])


def shifted(value, steps):
    count, _, _ = sizes()
    return lax.ppermute(
        value, SEQ, [(i, i + steps) for i in range(count) if 0 <= i + steps < count]
    )


def from_plane(value, back):
    planes = lax.axis_size("dp")
    return lax.ppermute(value, "dp", [(d, (d + back) % planes) for d in range(planes)])


def after(value, *events):
    return lax.optimization_barrier((value,) + events)[0]


def dot(left, right):
    return jnp.dot(left, right, preferred_element_type=F32)


def through_rows(left, right):
    return lax.dot_general(left, right, (((0,), (0,)), ((), ())), preferred_element_type=F32)


def against_cols(left, right):
    return lax.dot_general(left, right, (((1,), (1,)), ((), ())), preferred_element_type=F32)


def near(mine):
    return [mine, exchange(mine, 1)]


def far(theirs):
    return [theirs, exchange(theirs, 1)]


def pair_sum(parts):
    return parts[0].astype(F32) + exchange(parts[1], 1).astype(F32)


def far_sum(pair):
    return exchange(pair.astype(BF16), 2).astype(F32)


def kinds_table(seq, groups):
    pairs, kinds = [], np.zeros((3, seq), np.int32)
    for r in range(3):
        targets = [device_of((3 * s + r) % seq, groups) for s in range(seq)]
        pairs.append(list(enumerate(targets)))
        for s in range(seq):
            kinds[r, targets[s]] = (3 * s + r) // seq
    return pairs, kinds


def my_kinds():
    seq, groups, _ = sizes()
    return jnp.asarray(kinds_table(seq, groups)[1])[:, lax.axis_index(SEQ)]


def deal_joint(joint):
    seq, groups, _ = sizes()
    pairs, _ = kinds_table(seq, groups)
    cols = joint.shape[2] // 3
    sent = [
        jnp.concatenate(
            [joint[l, :, r * cols : (r + 1) * cols] for l in range(LAYERS)], axis=1
        )
        for r in range(3)
    ]
    return [lax.ppermute(part, SEQ, pairs[r]) for r, part in enumerate(sent)]


def return_joint(parts):
    seq, groups, _ = sizes()
    pairs, _ = kinds_table(seq, groups)
    back = [lax.ppermute(part, SEQ, [(b, a) for a, b in pairs[r]]) for r, part in enumerate(parts)]
    return jnp.concatenate(back, axis=1).astype(F32)


def choose(which, options):
    first, second, third = options
    return jnp.where(which == 0, first, jnp.where(which == 1, second, third))


def pack_attention_any(got, projects):
    kinds = my_kinds()
    cols = projects[0].shape[1]
    packs = []
    for l, project in enumerate(projects):
        parts = [part[:, l * cols : (l + 1) * cols] for part in got]
        sent = [
            jnp.where(kinds[0] == k, parts[0], jnp.where(kinds[1] == k, parts[1], parts[2]))
            for k in range(3)
        ]
        packs.append(jnp.concatenate(sent + [project], axis=1))
    return packs


def open_attention_any(stack):
    _, groups, planes = sizes()
    height, cols = stack.shape[1], stack.shape[2] // 4
    stack = stack.reshape(planes, groups, height, 4, cols)
    kinds = jnp.transpose(stack, (3, 0, 2, 1, 4)).reshape(4, D, groups * cols)
    blank = jnp.zeros((D, WIDTH - groups * cols), BF16)
    joint = jnp.concatenate([part for k in range(3) for part in (kinds[k], blank)], axis=1)
    return joint, kinds[3].reshape(TP, D // TP, groups * cols)


def join_project_any(got):
    _, groups, _ = sizes()
    rows = got.reshape(TP, D // TP, groups, -1).transpose(1, 2, 0, 3).reshape(D // TP, D)
    return jnp.concatenate([rows, jnp.zeros((WIDTH - D // TP, D), BF16)], axis=0)


def split_project_any(grad):
    _, groups, _ = sizes()
    chunks = grad[: D // TP].reshape(D // TP, groups, TP, -1).transpose(2, 0, 1, 3)
    return chunks.reshape(TP, D // TP, -1)


def split_attention_any(g_joint, got):
    _, groups, planes = sizes()
    cols = D // TP // groups
    parts = [g_joint[:, k * WIDTH : k * WIDTH + groups * cols] for k in range(3)]
    parts = jnp.stack(parts + [got.reshape(D, groups * cols)])
    parts = parts.reshape(4, planes, D // planes, groups, cols).transpose(1, 3, 2, 0, 4)
    return parts.reshape(planes * groups, D // planes, 4 * cols)


def unpack_attention_any(owned):
    kinds = my_kinds()
    cols = owned.shape[1] // 4
    own = [owned[:, k * cols : (k + 1) * cols] for k in range(4)]
    return [choose(kinds[r], own[:3]).astype(BF16) for r in range(3)] + [own[3].astype(F32)]


def pack_forward_any(expand, reduce):
    seq, groups, planes = sizes()
    cols, rows = expand.shape[1] // planes, reduce.shape[0] // seq
    chunks = []
    for unit in unit_table(seq, groups):
        q = unit % planes
        chunks += [expand[:, q * cols : (q + 1) * cols], reduce[unit * rows : (unit + 1) * rows]]
    chunks = jnp.concatenate([chunk.reshape(-1, cols) for chunk in chunks], axis=0)
    return chunks.reshape(seq, -1, cols)


def unpack_forward_any(got):
    seq, _, planes = sizes()
    ways, cols = seq // planes, got.shape[2]
    height, width = D // planes, got.shape[2] * planes
    mine = got.reshape((planes, ways) + got.shape[1:])
    mine = lax.dynamic_index_in_dim(mine, my_unit() // planes, 1, keepdims=False)
    expand = jnp.concatenate([mine[d, :height] for d in range(planes)], axis=1)
    reduce = got[:, height:].reshape(seq, cols, D // seq)
    reduce = jnp.concatenate([reduce[s] for s in range(seq)], axis=1)
    blocks = [reduce[:, k * width : (k + 1) * width] for k in range(D // width)]
    return jnp.concatenate([expand] + blocks, axis=0)


def open_forward_any(stack):
    _, groups, planes = sizes()
    height, width = D // planes, stack.shape[2]
    rows = width // planes
    stack = stack.reshape((planes, groups) + stack.shape[1:])
    expand = jnp.transpose(stack[:, :, :height], (0, 2, 1, 3)).reshape(D, groups * width)
    reduce = stack[:, :, height:].reshape(planes, groups, D // width, rows, width)
    reduce = jnp.transpose(reduce, (1, 0, 3, 2, 4)).reshape(groups * planes * rows, D)
    return expand, reduce


def split_forward_any(g_expand, g_reduce):
    _, groups, planes = sizes()
    height, width = D // planes, LOCAL_FF // groups
    rows = width // planes
    expand = g_expand.reshape(planes, height, groups, width).transpose(0, 2, 1, 3)
    reduce = g_reduce.reshape(groups, planes, rows, D // width, width).transpose(1, 0, 3, 2, 4)
    reduce = reduce.reshape(planes, groups, rows * D // width, width)
    stack = jnp.concatenate([expand, reduce], axis=2)
    return stack.reshape((planes * groups,) + stack.shape[2:])


def pack_return_any(owned):
    seq, _, planes = sizes()
    ways, height, width = seq // planes, D // planes, owned.shape[1]
    rows, cols = width // planes, width // planes
    blocks = owned[height:].reshape(D // width, rows, width)
    reduce = jnp.concatenate([blocks[k] for k in range(D // width)], axis=1)
    chunks = []
    for s in range(seq):
        d = s // ways
        chunks.append(owned[:height, d * cols : (d + 1) * cols])
        chunks.append(reduce[:, s * (D // seq) : (s + 1) * (D // seq)].reshape(-1, cols))
    return jnp.concatenate(chunks, axis=0).reshape(seq, -1, cols)


def unpack_return_any(got):
    seq, groups, planes = sizes()
    ways, cols, height = seq // planes, got.shape[2], D // planes
    got = jnp.swapaxes(got.reshape((groups, TP) + got.shape[1:]), 0, 1).reshape(got.shape)
    first = planes * (lax.axis_index(SEQ) % ways)
    mine = lax.dynamic_slice_in_dim(got[:, :height], first, planes)
    expand = jnp.concatenate([mine[q] for q in range(planes)], axis=1)
    return expand.astype(F32), got[:, height:].reshape(-1, D // seq).astype(F32)


def compact():
    seq, groups, planes = sizes()
    return groups == 2 and planes == 4 and D // seq % 16 == 0


def rearrange(body, arrays, outs, name):
    return pl.pallas_call(
        body,
        in_specs=[pl.BlockSpec(memory_space=pltpu.SMEM)]
        + [pl.BlockSpec(memory_space=pltpu.VMEM)] * len(arrays),
        out_specs=[pl.BlockSpec(memory_space=pltpu.VMEM)] * len(outs),
        out_shape=[jax.ShapeDtypeStruct(shape, dtype) for shape, dtype in outs],
        compiler_params=pltpu.CompilerParams(vmem_limit_bytes=48 * 1024 * 1024),
        cost_estimate=pl.CostEstimate(
            flops=0,
            bytes_accessed=sum(math.prod(shape) * 4 for shape, _ in outs),
            transcendentals=0,
        ),
        name=name,
    )(here(), *arrays)


def side_by_side(parts):
    return jnp.concatenate(parts, axis=1)


def kind_sent(me_ref, r):
    unit = me_ref[2] * 2 + me_ref[1]
    source = (3 * (unit + 8 - r)) % 8
    return (3 * source + r) // 8


def pack_attention_kernel(me_ref, a_ref, b_ref, c_ref, *refs):
    cols = refs[0].shape[1]
    first, second = kind_sent(me_ref, 0), kind_sent(me_ref, 1)
    for l in range(LAYERS):
        project_ref, out_ref = refs[l], refs[LAYERS + l]
        at = slice(l * cols, (l + 1) * cols)
        for half in range(2):
            rows = slice(half * cols, (half + 1) * cols)
            a, b, c = a_ref[rows, at], b_ref[rows, at], c_ref[rows, at]
            parts = [jnp.where(first == k, a, jnp.where(second == k, b, c)) for k in range(3)]
            out_ref[:, half * 4 * cols : (half + 1) * 4 * cols] = side_by_side(
                parts + [project_ref[rows]]
            )


def by_plane(me_ref, refs):
    if len(refs) == 1:
        return [(d, refs[0][2 * d], refs[0][2 * d + 1]) for d in range(4)]
    got = []
    for step in range(4):
        own, other = refs[step][...], refs[4 + step][...]
        first = jnp.where(me_ref[1] == 0, own, other)
        second = jnp.where(me_ref[1] == 0, other, own)
        got.append(((me_ref[0] + 4 - step) % 4, first, second))
    return got


def rows_at(start, count):
    if isinstance(start, int):
        return slice(start, start + count)
    return pl.ds(pl.multiple_of(start, 16), count)


def open_attention_kernel(me_ref, *refs):
    *refs, joint_ref, project_ref = refs
    cols = refs[0].shape[-2]
    blank = jnp.zeros((cols, WIDTH - 2 * cols), BF16)
    for plane, first, second in by_plane(me_ref, refs):
        for half in range(2):
            pieces = [
                [piece[:, (4 * half + k) * cols : (4 * half + k + 1) * cols] for k in range(4)]
                for piece in (first, second)
            ]
            parts = []
            for kind in range(3):
                parts += [pieces[0][kind], pieces[1][kind], blank]
            joint_ref[rows_at(plane * 2 * cols + half * cols, cols)] = side_by_side(parts)
            project_ref[plane, half * cols : (half + 1) * cols] = side_by_side(
                [pieces[0][3], pieces[1][3]]
            )


def join_project_kernel(me_ref, got_ref, out_ref):
    cols = got_ref.shape[2] // 2
    rows = got_ref.shape[1]
    out_ref[:rows] = side_by_side(
        [got_ref[t][:, g * cols : (g + 1) * cols] for g in range(2) for t in range(4)]
    )
    out_ref[rows:] = jnp.zeros((out_ref.shape[0] - rows, out_ref.shape[1]), BF16)


def split_project_kernel(me_ref, grad_ref, out_ref):
    rows, cols = out_ref.shape[1], out_ref.shape[2] // 2
    for t in range(4):
        out_ref[t] = side_by_side(
            [grad_ref[:rows, (g * 4 + t) * cols : (g * 4 + t + 1) * cols] for g in range(2)]
        )


def pack_forward_kernel(me_ref, expand_ref, reduce_ref, out_ref):
    cols = reduce_ref.shape[1]
    for s, unit in enumerate(unit_table(8, 2)):
        at = slice(unit % 4 * cols, (unit % 4 + 1) * cols)
        out_ref[s] = side_by_side(
            [
                expand_ref[:cols, at],
                expand_ref[cols:, at],
                reduce_ref[unit * cols : (unit + 1) * cols],
            ]
        )


def unpack_forward_kernel(me_ref, got_ref, out_ref):
    cols = got_ref.shape[1]
    unit = me_ref[2] * 2 + me_ref[1]
    for half in range(2):
        parts = []
        for d in range(4):
            parts.append(got_ref[2 * d + unit // 4][:, half * cols : (half + 1) * cols])
        for s in range(4):
            parts.append(got_ref[4 * half + s][:, 2 * cols :])
        out_ref[half * cols : (half + 1) * cols] = side_by_side(parts)


def open_forward_kernel(me_ref, *refs):
    *refs, expand_ref, reduce_ref = refs
    height = refs[0].shape[-2]
    rows, width = height // 2, D // 2
    for plane, first, second in by_plane(me_ref, refs):
        expand_ref[rows_at(plane * height, height)] = side_by_side(
            [first[:, :width], second[:, :width]]
        )
        for group, piece in enumerate((first, second)):
            reduce_ref[rows_at(group * width + plane * rows, rows)] = side_by_side(
                [piece[:rows, width:], piece[rows:, width:]]
            )


def put_pieces(me_ref, outs, step, pair):
    if len(outs) == 1:
        outs[0][2 * step], outs[0][2 * step + 1] = pair
    else:
        outs[step][...] = jnp.where(me_ref[1] == 0, pair[0], pair[1])
        outs[4 + step][...] = jnp.where(me_ref[1] == 0, pair[1], pair[0])


def split_forward_kernel(me_ref, expand_ref, reduce_ref, *outs):
    height = outs[0].shape[-2]
    rows, width = height // 2, D // 2
    for step in range(4):
        plane = step if len(outs) == 1 else (me_ref[0] + 3 - step) % 4
        expand = expand_ref[rows_at(plane * height, height)]
        pair = []
        for group in range(2):
            reduce = reduce_ref[rows_at(group * width + plane * rows, rows)]
            part = expand[:, group * width : (group + 1) * width]
            upper = side_by_side([part[:rows], reduce[:, :width]])
            lower = side_by_side([part[rows:], reduce[:, width:]])
            pair.append(jnp.concatenate([upper, lower], axis=0))
        put_pieces(me_ref, outs, step, pair)


def pack_return_kernel(me_ref, whole_ref, out_ref):
    cols = out_ref.shape[1]
    for s in range(8):
        at = slice(s // 2 * cols, (s // 2 + 1) * cols)
        right = slice((4 + s % 4) * cols, (5 + s % 4) * cols)
        out_ref[s] = side_by_side(
            [
                whole_ref[:cols, at],
                whole_ref[cols:, at],
                whole_ref[s // 4 * cols : (s // 4 + 1) * cols, right],
            ]
        )


def unpack_return_kernel(me_ref, got_ref, expand_ref, reduce_ref):
    cols = got_ref.shape[1]
    for half in range(2):
        parts = []
        for q in range(4):
            device = q % 2 * 4 + 2 * (me_ref[2] % 2) + q // 2
            parts.append(got_ref[device][:, half * cols : (half + 1) * cols])
        expand_ref[half * cols : (half + 1) * cols] = side_by_side(parts).astype(F32)
    for s, unit in enumerate(unit_table(8, 2)):
        reduce_ref[unit * cols : (unit + 1) * cols] = got_ref[s][:, 2 * cols :].astype(F32)


def split_attention_kernel(me_ref, joint_ref, project_ref, *outs):
    cols = outs[0].shape[-2]
    for step in range(4):
        plane = step if len(outs) == 1 else (me_ref[0] + 3 - step) % 4
        parts = [[], []]
        for half in range(2):
            rows = joint_ref[rows_at(plane * 2 * cols + half * cols, cols)]
            project = project_ref[plane, half * cols : (half + 1) * cols]
            for group in range(2):
                for kind in range(3):
                    at = kind * WIDTH + group * cols
                    parts[group].append(rows[:, at : at + cols])
                parts[group].append(project[:, group * cols : (group + 1) * cols])
        put_pieces(me_ref, outs, step, [side_by_side(part) for part in parts])


def unpack_attention_kernel(me_ref, whole_ref, a_ref, b_ref, c_ref, project_ref):
    cols = whole_ref.shape[0]
    for half in range(2):
        rows = slice(half * cols, (half + 1) * cols)
        parts = []
        for k in range(4):
            at = (half * 4 + k) * cols
            parts.append(whole_ref[:, at : at + cols])
        for r, ref in enumerate((a_ref, b_ref, c_ref)):
            ref[rows] = choose(kind_sent(me_ref, r), parts[:3]).astype(BF16)
        project_ref[rows] = parts[3].astype(F32)


def pack_attention(joint, project):
    got = deal_joint(joint)
    projects = [project[l] for l in range(LAYERS)]
    if not compact():
        return pack_attention_any(got, projects)
    cols = project.shape[2]
    outs = [((cols, 8 * cols), BF16)] * LAYERS
    return rearrange(pack_attention_kernel, [*got, *projects], outs, "pack_attention")


def pack_forward(expand, reduce, *events):
    cols = reduce.shape[1]
    if compact():
        outs = [((8, cols, 3 * cols), BF16)]
        (chunks,) = rearrange(pack_forward_kernel, [expand, reduce], outs, "pack_forward")
    else:
        chunks = pack_forward_any(expand, reduce)
    got = after(lax.all_to_all(chunks, SEQ, 0, 0, tiled=True), *events)
    if not compact():
        return unpack_forward_any(got)
    return rearrange(
        unpack_forward_kernel, [got], [((2 * cols, 8 * cols), BF16)], "unpack_forward"
    )[0]


def gather_slow(pack):
    return [lax.all_gather(pack, OWNERS, axis=0, tiled=False)]


def gather_planes(pack):
    return [pack] + [from_plane(pack, back) for back in range(1, 4)]


def open_attention(pieces):
    if not compact():
        return open_attention_any(pieces[0])
    cols = D // 8
    outs = [((D, 3 * WIDTH), BF16), ((TP, 2 * cols, 2 * cols), BF16)]
    return rearrange(open_attention_kernel, pieces, outs, "open_attention")


def project_matrix(columns):
    got = lax.all_to_all(columns, "member", 0, 0, tiled=True)
    if not compact():
        return join_project_any(got)
    return rearrange(join_project_kernel, [got], [((WIDTH, D), BF16)], "join_project")[0]


def open_forward(pieces):
    if not compact():
        return open_forward_any(pieces[0])
    outs = [((D, D), BF16), ((D, D), BF16)]
    return rearrange(open_forward_kernel, pieces, outs, "open_forward")


def piece_outs(shape, fast):
    return [(shape, BF16)] * 8 if fast else [((8,) + shape, BF16)]


def split_project(g_project):
    if compact():
        outs = [((TP, D // TP, D // TP), BF16)]
        (chunks,) = rearrange(split_project_kernel, [g_project], outs, "split_project")
    else:
        chunks = split_project_any(g_project)
    return lax.all_to_all(chunks, "member", 0, 0, tiled=True)


def split_attention(g_joint, project, fast):
    if not compact():
        return [split_attention_any(g_joint, project)]
    outs = piece_outs((D // 8, D), fast)
    return rearrange(split_attention_kernel, [g_joint, project], outs, "split_attention")


def split_forward(g_expand, g_reduce, fast):
    if not compact():
        return [split_forward_any(g_expand, g_reduce)]
    outs = piece_outs((D // 4, D), fast)
    return rearrange(split_forward_kernel, [g_expand, g_reduce], outs, "split_forward")


def owner_sum(pieces, step, carried, *events):
    own, other = pieces[step], after(pieces[4 + step], *events)
    total = own.astype(F32) + exchange(other, TP).astype(F32)
    if step:
        total = total + from_plane(carried, 1).astype(F32)
    return total.astype(BF16)


def owner_sum_slow(pieces):
    return lax.psum_scatter(pieces[0], OWNERS, scatter_dimension=0, tiled=False)


def return_attention(owned):
    if compact():
        cols = D // 8
        outs = [((2 * cols, cols), BF16)] * 3 + [((2 * cols, cols), F32)]
        *parts, project = rearrange(unpack_attention_kernel, [owned], outs, "unpack_attention")
    else:
        *parts, project = unpack_attention_any(owned)
    return return_joint(parts), project


def return_forward(owned):
    cols = D // 8
    if compact():
        outs = [((8, cols, 3 * cols), BF16)]
        (chunks,) = rearrange(pack_return_kernel, [owned], outs, "pack_return")
    else:
        chunks = pack_return_any(owned)
    got = lax.all_to_all(chunks, SEQ, 0, 0, tiled=True)
    if not compact():
        return unpack_return_any(got)
    outs = [((2 * cols, 4 * cols), F32), ((8 * cols, cols), F32)]
    return rearrange(unpack_return_kernel, [got], outs, "unpack_return")


def half_call(body, half, chunks, matrices, tokens, into, partial, name):
    count = chunks[0].shape[0]

    def whole(array):
        return pl.BlockSpec(array.shape, lambda i: (0,) * array.ndim)

    def slot(shape):
        return pl.BlockSpec(shape, lambda i: (2 * half + i,) + (0,) * (len(shape) - 1))

    kept = [array for _, array in into if array is not None]
    operands = [*chunks, *matrices, *tokens]
    specs = [whole(array) for array in (*chunks, *matrices)]
    specs += [slot((array.shape[0] // TP,) + array.shape[1:]) for array in tokens]
    out_specs = [slot((count, width)) for width, _ in into]
    shapes = [jax.ShapeDtypeStruct((TP * count, width), BF16) for width, _ in into]
    if partial:
        out_specs += [pl.BlockSpec((count, D), lambda i: (0, 0))] * 2
        shapes += [jax.ShapeDtypeStruct((count, D), BF16)] * 2
    aliases = {len(operands) + k: k for k in range(len(kept))}
    work = sum(2 * 2 * count * math.prod(matrix.shape) for matrix in matrices)

    def kernel(a_ref, b_ref, *refs):
        n = len(matrices) + len(tokens)
        mine = pl.program_id(0) == 0
        rows = jnp.where(mine, a_ref[...], b_ref[...])
        body(rows, mine, refs[:n], refs[n + len(kept) :])

    return pl.pallas_call(
        kernel,
        grid=(2,),
        in_specs=specs + [pl.BlockSpec(memory_space=pl.ANY)] * len(kept),
        out_specs=out_specs,
        out_shape=shapes,
        input_output_aliases=aliases,
        compiler_params=kernel_params(),
        cost_estimate=pl.CostEstimate(
            flops=work, bytes_accessed=work // 512, transcendentals=2 * count * D
        ),
        name=name,
    )(*operands, *kept)


def slot_products(product, half, tokens, matrix, name, slots=TP):
    count = tokens.shape[0] // slots

    def kernel(rows_ref, matrix_ref, a_ref, b_ref):
        value = product(rows_ref[...], matrix_ref[...])
        put_partial(pl.program_id(0) == 0, value, a_ref, b_ref)

    return pl.pallas_call(
        kernel,
        grid=(2,),
        in_specs=[
            pl.BlockSpec((count, tokens.shape[1]), lambda i: (2 * half + i, 0)),
            pl.BlockSpec(matrix.shape, lambda i: (0, 0)),
        ],
        out_specs=[pl.BlockSpec((count, D), lambda i: (0, 0))] * 2,
        out_shape=[jax.ShapeDtypeStruct((count, D), BF16)] * 2,
        compiler_params=kernel_params(),
        cost_estimate=pl.CostEstimate(
            flops=4 * count * math.prod(matrix.shape),
            bytes_accessed=2 * math.prod(matrix.shape),
            transcendentals=0,
        ),
        name=name,
    )(tokens, matrix)


def put_partial(mine, value, a_ref, b_ref):
    value = value.astype(BF16)

    @pl.when(mine)
    def _():
        a_ref[...] = value

    @pl.when(jnp.logical_not(mine))
    def _():
        b_ref[...] = value


def chunks_of(width):
    return [slice(at, min(at + CHUNK, width)) for at in range(0, width, CHUNK)]


def joint_body(rows, mine, refs, outs):
    outs[0][...] = dot(rows, refs[0][...]).astype(BF16)


def forward_body(rows, mine, refs, outs):
    expand_ref, reduce_ref, sides_ref, active_ref = refs
    activated_ref, slope_ref, a_ref, b_ref = outs
    root = math.sqrt(2.0 / math.pi)
    before, now = sides_ref[:, 0:1], sides_ref[:, 1:2]
    for at in chunks_of(LOCAL_FF):
        pre = dot(rows, expand_ref[:, at])
        square = pre * pre
        curve = jnp.tanh(root * pre * (1.0 + 0.044715 * square))
        half = 0.5 + 0.5 * curve
        mask = before * active_ref[0, 0:1, at] + now * active_ref[0, 1:2, at]
        slope = half + pre * (half - half * half) * (2.0 * root * (1.0 + 0.134145 * square))
        activated_ref[:, at] = (pre * half * mask).astype(BF16)
        slope_ref[:, at] = (slope * mask).astype(BF16)
    put_partial(mine, dot(activated_ref[...], reduce_ref[...]), a_ref, b_ref)


def backward_body(rows, mine, refs, outs):
    expand_ref, reduce_ref, slope_ref = refs
    d_pre_ref, a_ref, b_ref = outs
    for at in chunks_of(LOCAL_FF):
        d_active = against_cols(rows, reduce_ref[at])
        d_pre_ref[:, at] = (d_active * slope_ref[:, at].astype(F32)).astype(BF16)
    put_partial(mine, against_cols(d_pre_ref[...], expand_ref[...]), a_ref, b_ref)


def head_tiles(head):
    low = head * HEAD_DIM // LANES * LANES
    high = -(-(head + 1) * HEAD_DIM // LANES) * LANES
    return low, high


def lanes_of(head, shape):
    low, high = head_tiles(head)
    lane = lax.broadcasted_iota(jnp.int32, shape, 1) + low
    return (lane >= head * HEAD_DIM) & (lane < (head + 1) * HEAD_DIM)


def key_tiles(refs, halos, block, base, low, high):
    before_ref, after_ref = halos
    prev_ref, here_ref, next_ref = refs
    prev = jnp.where(block == 0, before_ref[:, base + low : base + high], prev_ref[:, low:high])
    following = jnp.where(
        block == TP - 1, after_ref[:, base + low : base + high], next_ref[:, low:high]
    )
    return prev, here_ref[:, low:high], following


def attend_kernel(base, me_ref, q_ref, *refs):
    keys, values, halos = refs[0:3], refs[3:6], refs[6:8]
    segq_ref, segk_ref, head_ref, mixed_ref, lse_ref = refs[8:]
    block = (base + pl.program_id(0)) ^ me_ref[2]
    count = q_ref.shape[0]
    allowed = segq_ref[...] == segk_ref[0]
    tiles = [jnp.zeros((count, LANES), F32) for _ in range(WIDTH // LANES)]
    total = jnp.zeros((count, LANES), F32)
    lane = lax.broadcasted_iota(jnp.int32, (count, LANES), 1)
    for head in range(LOCAL_HEADS):
        low, high = head_tiles(head)
        mine = lanes_of(head, (count, high - low))
        query = jnp.where(mine, q_ref[:, low:high], 0)
        key = key_tiles(keys, halos, block, 0, low, high)
        scores = jnp.concatenate([against_cols(query, part) for part in key], axis=1) * FACTOR
        scores = jnp.where(allowed, scores, NEGATIVE)
        highest = jnp.max(scores, axis=-1, keepdims=True)
        weights = jnp.exp(scores - highest)
        sums = jnp.sum(weights, axis=-1, keepdims=True)
        probs = (weights / sums).astype(BF16)
        out, at = 0.0, 0
        for part in key_tiles(values, halos, block, WIDTH, low, high):
            out = out + dot(probs[:, at : at + part.shape[0]], part)
            at += part.shape[0]
        out = jnp.where(mine, out, 0.0) * head_ref[:, head : head + 1]
        for k in range(low // LANES, high // LANES):
            at = k * LANES - low
            tiles[k] = tiles[k] + out[:, at : at + LANES]
        total = jnp.where(lane == head, highest + jnp.log(sums), total)
    for k, tile in enumerate(tiles):
        mixed_ref[:, k * LANES : (k + 1) * LANES] = tile.astype(BF16)
    lse_ref[...] = total


def attend_back_kernel(me_ref, q_ref, *refs):
    keys, values, halos = refs[0:3], refs[3:6], refs[6:8]
    grad_ref, mixed_ref, lse_ref, segq_ref, segk_ref, head_ref = refs[8:14]
    d_joint_ref, d_before_ref, d_after_ref, sum_ref = refs[14:]
    step = pl.program_id(0)
    block = step ^ me_ref[2]
    count = q_ref.shape[0]

    @pl.when(step == 0)
    def _():
        sum_ref[...] = jnp.zeros_like(sum_ref)

    prev = jnp.where(block == 0, TP, jnp.maximum(block - 1, 0) ^ me_ref[2])
    following = jnp.where(block == TP - 1, TP + 1, jnp.minimum(block + 1, TP - 1) ^ me_ref[2])
    windows = [
        (pl.ds(pl.multiple_of(prev * count, count), count), 0),
        (pl.ds(pl.multiple_of(step * count, count), count), count),
        (pl.ds(pl.multiple_of(following * count, count), AFTER), 2 * count),
    ]
    rows = pl.ds(pl.multiple_of(step * count, count), count)
    allowed = segq_ref[...] == segk_ref[0]
    tiles = [jnp.zeros((count, LANES), F32) for _ in range(WIDTH // LANES)]
    for head in range(LOCAL_HEADS):
        low, high = head_tiles(head)
        mine = lanes_of(head, (count, high - low))
        query = jnp.where(mine, q_ref[:, low:high], 0)
        key = key_tiles(keys, halos, block, 0, low, high)
        value = key_tiles(values, halos, block, WIDTH, low, high)
        active = head_ref[:, head : head + 1]
        grad = jnp.where(mine, grad_ref[:, low:high].astype(F32) * active, 0.0)
        balance = jnp.sum(grad * mixed_ref[:, low:high].astype(F32), axis=-1, keepdims=True)
        grad = grad.astype(BF16)
        scores = jnp.concatenate([against_cols(query, part) for part in key], axis=1) * FACTOR
        probs = jnp.where(allowed, jnp.exp(scores - lse_ref[:, head : head + 1]), 0.0)
        d_probs = jnp.concatenate([against_cols(grad, part) for part in value], axis=1)
        d_scores = (probs * (d_probs - balance)).astype(BF16)
        probs = probs.astype(BF16)
        d_query = 0.0
        for (window, at), part in zip(windows, key):
            piece = d_scores[:, at : at + part.shape[0]]
            d_query = d_query + dot(piece, part)
            sum_ref[window, low:high] += through_rows(piece, query) * FACTOR
            sum_ref[window, WIDTH + low : WIDTH + high] += through_rows(
                probs[:, at : at + part.shape[0]], grad
            )
        d_query = jnp.where(mine, d_query, 0.0)
        for k in range(low // LANES, high // LANES):
            at = k * LANES - low
            tiles[k] = tiles[k] + d_query[:, at : at + LANES]
    for k, tile in enumerate(tiles):
        d_joint_ref[rows, k * LANES : (k + 1) * LANES] = (tile * FACTOR).astype(BF16)

    @pl.when(step == pl.num_programs(0) - 1)
    def _():
        d_joint_ref[:, WIDTH:] = sum_ref[: TP * count].astype(BF16)
        d_before_ref[...] = sum_ref[TP * count : (TP + 1) * count].astype(BF16)
        d_after_ref[...] = sum_ref[(TP + 1) * count : (TP + 1) * count + AFTER].astype(BF16)


def kernel_params():
    return pltpu.CompilerParams(
        dimension_semantics=("arbitrary",), vmem_limit_bytes=48 * 1024 * 1024
    )


def block_specs(count, base=0):
    def rows(width):
        return pl.BlockSpec((count, width), lambda j, me: (base + j, 0))

    def whole(shape):
        return pl.BlockSpec(shape, lambda j, me: (0,) * len(shape))

    def around(kind):
        def before(j, me):
            return (jnp.maximum(((base + j) ^ me[2]) - 1, 0) ^ me[2], kind)

        def following(j, me):
            slot = jnp.minimum(((base + j) ^ me[2]) + 1, TP - 1) ^ me[2]
            return (slot * (count // AFTER), kind)

        return [
            pl.BlockSpec((count, WIDTH), before),
            pl.BlockSpec((count, WIDTH), lambda j, me: (base + j, kind)),
            pl.BlockSpec((AFTER, WIDTH), following),
        ]

    fixed = [rows(WIDTH)] + around(1) + around(2)
    return rows, whole, fixed + [whole((count, 2 * WIDTH)), whole((AFTER, 2 * WIDTH))]


def attend(joint, halos, segq, segk, heads, base, slots):
    span = segk.shape[2]
    count = joint.shape[0] // TP
    rows, whole, specs = block_specs(count, base)
    return pl.pallas_call(
        functools.partial(attend_kernel, base),
        grid_spec=pltpu.PrefetchScalarGridSpec(
            num_scalar_prefetch=1,
            grid=(slots,),
            in_specs=specs
            + [
                rows(1),
                pl.BlockSpec((1, 1, span), lambda j, me: (base + j, 0, 0)),
                rows(LANES),
            ],
            out_specs=[
                pl.BlockSpec((count, WIDTH), lambda j, me: (j, 0)),
                pl.BlockSpec((count, LANES), lambda j, me: (j, 0)),
            ],
        ),
        out_shape=[
            jax.ShapeDtypeStruct((slots * count, WIDTH), BF16),
            jax.ShapeDtypeStruct((slots * count, LANES), F32),
        ],
        compiler_params=kernel_params(),
        cost_estimate=pl.CostEstimate(
            flops=8 * slots * count * span * LANES * LOCAL_HEADS,
            bytes_accessed=slots * count * WIDTH * 8,
            transcendentals=slots * count * span * LOCAL_HEADS,
        ),
        name="attend",
    )(here(), *[joint] * 7, *halos, segq, segk, heads)


def attend_back(joint, halos, grad, mixed, log_total, segq, segk, heads):
    span = segk.shape[2]
    count = joint.shape[0] // TP
    rows, whole, specs = block_specs(count)
    shapes = [(TP * count, 3 * WIDTH), (count, 2 * WIDTH), (AFTER, 2 * WIDTH)]
    return pl.pallas_call(
        attend_back_kernel,
        grid_spec=pltpu.PrefetchScalarGridSpec(
            num_scalar_prefetch=1,
            grid=(TP,),
            in_specs=specs
            + [
                rows(WIDTH),
                rows(WIDTH),
                rows(LANES),
                rows(1),
                pl.BlockSpec((1, 1, span), lambda j, me: (j, 0, 0)),
                rows(LANES),
            ],
            out_specs=[whole(shape) for shape in shapes],
            scratch_shapes=[pltpu.VMEM(((TP + 2) * count, 2 * WIDTH), F32)],
        ),
        out_shape=[jax.ShapeDtypeStruct(shape, BF16) for shape in shapes],
        compiler_params=kernel_params(),
        cost_estimate=pl.CostEstimate(
            flops=20 * TP * count * span * LANES * LOCAL_HEADS,
            bytes_accessed=TP * count * WIDTH * 20,
            transcendentals=TP * count * span * LOCAL_HEADS,
        ),
        name="attend_back",
    )(here(), *[joint] * 7, *halos, grad, mixed, log_total, segq, segk, heads)


def halos_of(joint):
    _, groups, _ = sizes()
    count = joint.shape[0] // TP
    if groups == 1:
        return [jnp.zeros((rows, 2 * WIDTH), joint.dtype) for rows in (count, AFTER)]
    group, member = place()
    column = jnp.int32(WIDTH)
    last = ((member ^ (TP - 1)) * count, column)
    if groups == 2:
        first = (member * count, column)
        start = [jnp.where(group == 0, x, y) for x, y in zip(last, first)]
        got = exchange(lax.dynamic_slice(joint, start, (count, 2 * WIDTH)), TP)
        return [got, got]
    last = lax.dynamic_slice(joint, last, (count, 2 * WIDTH))
    first = lax.dynamic_slice(joint, (member * count, column), (AFTER, 2 * WIDTH))
    return [shifted(last, TP), shifted(first, -TP)]


def halos_back(d_joint, d_before, d_after):
    _, groups, _ = sizes()
    if groups == 1:
        return d_joint
    group, member = place()
    count = d_joint.shape[0] // TP
    last, first = (member ^ (TP - 1)) * count, member * count
    if groups == 2:
        d_after = jnp.pad(d_after, ((0, count - AFTER), (0, 0)))
        got = exchange(jnp.where(group == 0, d_after, d_before), TP)
        pieces = [(got, jnp.where(group == 0, last, first))]
    else:
        pieces = [(shifted(d_before, -TP), last), (shifted(d_after, TP), first)]
    for piece, at in pieces:
        start = (at, jnp.int32(WIDTH))
        sums = lax.dynamic_slice(d_joint, start, piece.shape)
        sums = (sums.astype(F32) + piece.astype(F32)).astype(BF16)
        d_joint = lax.dynamic_update_slice(d_joint, sums, start)
    return d_joint


def normed(stream):
    center = stream - jnp.mean(stream, axis=-1, keepdims=True)
    scale = lax.rsqrt(jnp.mean(center * center, axis=-1, keepdims=True) + EPS)
    return center * scale, scale


def norm_back(grad, unit, scale):
    mean = jnp.mean(grad, axis=-1, keepdims=True)
    slope = jnp.mean(grad * unit, axis=-1, keepdims=True)
    return scale * (grad - mean - unit * slope)


def per_token(vectors, sides):
    return sides[0] * vectors[0][None, :] + sides[1] * vectors[1][None, :]


def per_crop(value, sides):
    return jnp.stack([jnp.sum(value * sides[0], axis=0), jnp.sum(value * sides[1], axis=0)])


def step_embed(stamps, breadth):
    halfway = breadth // 2
    frequency = jnp.exp(-math.log(10000.0) * jnp.arange(halfway, dtype=F32) / halfway)
    angles = stamps.astype(F32)[..., None] * frequency
    return jnp.concatenate([jnp.cos(angles), jnp.sin(angles)], axis=-1)


def segment_of(places, bounds):
    return jnp.sum((places[:, None] >= bounds[None, :]).astype(jnp.int32), axis=-1)


def layer_forward(
    stream, mod, w_joint, project_columns, open_reduce, masks, context, hold, split
):
    head_tok, active, keeping = masks
    sides, living, segq, segk, slot_sides = context
    offset_one, stretch_one, gate_one, offset_two, stretch_two, gate_two = [
        per_token(mod[:, i], sides) for i in range(6)
    ]
    count = stream.shape[0]
    unit_one, _ = normed(stream)
    mine = (unit_one * (1.0 + stretch_one) + offset_one).astype(BF16)
    mine = hold("normed_one", mine)
    theirs, ours = exchange(mine, 2), near(mine)
    (joint,) = half_call(
        joint_body, 0, ours, [w_joint], [], [(3 * WIDTH, None)], False, "joint_near"
    )
    theirs = far(hold("far_one", theirs, joint))
    (joint,) = half_call(
        joint_body, 1, theirs, [w_joint], [], [(3 * WIDTH, joint)], False, "joint_far"
    )
    normed_one = ours + theirs
    halos = halos_of(joint)
    w_project = project_matrix(after(project_columns, joint))
    halos = hold("halos", halos)
    if split:
        far_rows, total_far = attend(joint, halos, segq, segk, head_tok, 2, 2)
        away = pair_sum(slot_products(dot, 0, far_rows, w_project, "branch_far", 2))
        held = after(halos, away)
        near_rows, total_near = attend(joint, held, segq, segk, head_tok, 0, 2)
        near_rows = hold("mixed", near_rows)
        close = pair_sum(slot_products(dot, 0, near_rows, w_project, "branch_near", 2))
        mixed = jnp.concatenate([near_rows, far_rows], axis=0)
        log_total = jnp.concatenate([total_near, total_far], axis=0)
    else:
        mixed, log_total = attend(joint, halos, segq, segk, head_tok, 0, TP)
        mixed = hold("mixed", mixed)
        away = pair_sum(slot_products(dot, 1, mixed, w_project, "branch_far"))
        close = pair_sum(slot_products(dot, 0, after(mixed, away), w_project, "branch_near"))
    branch = after(hold("branch", far_sum(away)), close) + close
    middle = stream + gate_one * branch * living
    unit_two, _ = normed(middle)
    mine = (unit_two * (1.0 + stretch_two) + offset_two).astype(BF16)
    theirs, ours = exchange(mine, 2), near(mine)
    w_expand, w_reduce = open_reduce(mine)
    matrices, tokens = [w_expand, w_reduce], [slot_sides, active]
    activated, slope, *parts = half_call(
        forward_body, 0, ours, matrices, tokens, [(LOCAL_FF, None)] * 2, True, "forward_near"
    )
    close = pair_sum(parts)
    theirs = far(hold("far_two", theirs, activated))
    activated, slope, *parts = half_call(
        forward_body,
        1,
        theirs,
        matrices,
        tokens,
        [(LOCAL_FF, activated), (LOCAL_FF, slope)],
        True,
        "forward_far",
    )
    away = pair_sum(parts)
    feedout = hold("feedout", far_sum(away), away) + close
    result = middle + gate_two * feedout * keeping
    record = (
        stream,
        normed_one,
        joint,
        halos,
        mixed,
        log_total,
        branch,
        middle,
        ours + theirs,
        slope,
        activated,
        feedout,
    )
    return result, record, (w_joint, w_project, w_expand, w_reduce)


def layer_backward(adjoint, record, mod, weights, masks, context, last, hold):
    (
        stream,
        normed_one,
        joint,
        halos,
        mixed,
        log_total,
        branch,
        middle,
        normed_two,
        slope,
        activated,
        feedout,
    ) = record
    w_joint, w_project, w_expand, w_reduce = weights
    head_tok, active, keeping = masks
    sides, living, segq, segk, slot_sides = context
    offset_one, stretch_one, gate_one, offset_two, stretch_two, gate_two = [
        per_token(mod[:, i], sides) for i in range(6)
    ]
    count = stream.shape[0]
    fast = compact()
    mine = (adjoint * gate_two * keeping).astype(BF16)
    theirs, ours = exchange(mine, 2), near(mine)
    matrices = [w_expand, w_reduce]
    d_pre, *parts = half_call(
        backward_body, 0, ours, matrices, [slope], [(LOCAL_FF, None)], True, "backward_near"
    )
    close = pair_sum(parts)
    theirs = far(hold("far_feed", theirs, d_pre))
    d_pre, *parts = half_call(
        backward_body, 1, theirs, matrices, [slope], [(LOCAL_FF, d_pre)], True, "backward_far"
    )
    away = pair_sum(parts)
    d_feed = jnp.concatenate(ours + theirs, axis=0)
    g_reduce = through_rows(activated, after(d_feed, away)).astype(BF16)
    d_gate_two = per_crop(after(adjoint, away) * feedout * keeping, sides)
    unit_two, scale_two = normed(middle)
    d_normed_two = hold("d_normed_two", far_sum(away), g_reduce, d_gate_two) + close
    d_middle = adjoint + norm_back(d_normed_two * (1.0 + stretch_two), unit_two, scale_two)
    mine = (d_middle * gate_one * living).astype(BF16)
    theirs, ours = exchange(mine, 2), near(mine)
    rows = after(jnp.concatenate(normed_two, axis=0), ours)
    g_expand = through_rows(rows, d_pre).astype(BF16)
    forward_pieces = split_forward(g_expand, g_reduce, False)
    d_offset_two = per_crop(after(d_normed_two, mine), sides)
    d_stretch_two = per_crop(after(d_normed_two, mine) * unit_two, sides)
    theirs = hold("d_branch", theirs, forward_pieces, d_offset_two, d_stretch_two)
    forward_sum = owner_sum_slow(forward_pieces)
    d_branch = jnp.concatenate(ours + far(theirs), axis=0)
    d_mixed = against_cols(d_branch, w_project).astype(BF16)
    g_project = split_project(through_rows(mixed, d_branch).astype(BF16))
    d_mixed = hold("d_mixed", d_mixed)
    d_joint = halos_back(
        *attend_back(joint, halos, d_mixed, mixed, log_total, segq, segk, head_tok)
    )
    d_joint = hold("d_joint", d_joint)

    def normed_parts(rows, half):
        return slot_products(against_cols, half, rows, w_joint, "d_normed")

    if last:
        g_joint = through_rows(jnp.concatenate(normed_one, axis=0), d_joint).astype(BF16)
        attention_pieces = split_attention(g_joint, g_project, fast)
        away = pair_sum(normed_parts(after(d_joint, attention_pieces), 1))
    else:
        away = pair_sum(normed_parts(d_joint, 1))
        rows = after(jnp.concatenate(normed_one, axis=0), away)
        g_joint = through_rows(rows, d_joint).astype(BF16)
        attention_pieces = split_attention(g_joint, g_project, fast)
    close = pair_sum(normed_parts(after(d_joint, away), 0))
    d_normed_one = after(far_sum(away), close, attention_pieces) + close
    unit_one, scale_one = normed(stream)
    d_stream = d_middle + norm_back(d_normed_one * (1.0 + stretch_one), unit_one, scale_one)
    d_gate_one = per_crop(d_middle * branch * living, sides)
    d_offset_one = per_crop(d_normed_one, sides)
    d_stretch_one = per_crop(d_normed_one * unit_one, sides)
    d_mod = jnp.stack(
        [d_offset_one, d_stretch_one, d_gate_one, d_offset_two, d_stretch_two, d_gate_two], axis=1
    )
    return d_stream, d_mod, attention_pieces, forward_sum


def shards(
    hidden_in,
    lengths,
    timesteps,
    head_mask,
    group_mask,
    skip_mask,
    modulation_weight,
    joint_weight,
    project_weight,
    expand_weight,
    reduce_weight,
    cotangent,
):
    seq, groups, planes = sizes()
    block = hidden_in.shape[1]
    crops = lengths.shape[1]
    mine = lax.axis_index(SEQ)
    plane = lax.axis_index("dp")
    group, member = place()
    height = D // planes

    attention_packs = pack_attention(joint_weight, project_weight)
    if compact():
        first = gather_planes(attention_packs[0])
        held = after((expand_weight[0], reduce_weight[0]), attention_packs[0])
        forward_first = gather_planes(pack_forward(*held, first))
        for k in range(4):
            first.append(exchange(after(first[k], first[-1]) if k else first[0], TP))
        mod_events, normed_events = [first[1], first[4]], [forward_first[0], first[5]]
    else:
        first = gather_slow(attention_packs[0])
        forward_first = gather_slow(pack_forward(expand_weight[0], reduce_weight[0]))
        mod_events, normed_events = [], []
    w_joint, project_columns = open_attention(first)

    stamps = jnp.zeros((planes, crops), jnp.int32)
    for step in range(planes):
        row = from_plane(timesteps[0], step) if step else timesteps[0]
        stamps = jnp.where(
            (jnp.arange(planes) == (plane - step) % planes)[:, None], row[None, :], stamps
        )
    stamps = stamps.reshape(planes * crops)
    embedded = jax.nn.silu(step_embed(stamps, D)).astype(BF16)
    condition = lax.dynamic_slice_in_dim(embedded, plane * height, height, axis=1)
    part = jnp.stack([dot(condition, modulation_weight[l]) for l in range(LAYERS)], axis=1)
    before = jnp.concatenate([jnp.zeros_like(part[:1]), part[:-1]])
    part = jnp.stack([before, part], axis=1)
    part = after(lax.all_to_all(part, EVERY, 0, 0, tiled=True), mod_events)
    part = jnp.sum(part.reshape((planes, seq) + part.shape[1:]), axis=0)
    mods = jnp.transpose(part, (2, 1, 0, 3)).reshape(LAYERS, 2, 6, D)

    bounds = jnp.cumsum(lengths[0])
    span = 2 * block + AFTER
    places = (group * TP - 1) * block + jnp.arange((TP + 1) * block + AFTER, dtype=jnp.int32)
    inside = (places >= 0) & (places < seq * block)
    segment = jnp.where(inside, segment_of(places, bounds), -1)
    segk = jnp.stack(
        [lax.dynamic_slice_in_dim(segment, (member ^ j) * block, span) for j in range(TP)]
    )[:, None, :]
    segq = segk[:, 0, block : 2 * block].reshape(TP * block, 1)
    own = segment_of(mine * block + jnp.arange(block, dtype=jnp.int32), bounds)[:, None]
    sides = [(own == mine - 1).astype(F32), ((own == mine) & (own < crops)).astype(F32)]
    living = (own < crops).astype(F32)
    onehot = (segq == jnp.arange(crops, dtype=jnp.int32)[None, :]).astype(BF16)
    blocks = jnp.stack([group * TP + (member ^ j) for j in range(TP)])
    firsts = jnp.repeat(blocks, block)[:, None]
    slot_sides = jnp.concatenate([segq == firsts - 1, (segq == firsts) & (segq < crops)], axis=1)
    context = (sides, living, segq, segk, slot_sides.astype(F32))
    rows = FF // (planes * seq)
    units = member * groups + jnp.arange(groups, dtype=jnp.int32)
    starts = (FF // planes) * jnp.arange(planes, dtype=jnp.int32)[None, :] + rows * units[:, None]
    hidden_here = (starts[:, :, None] + jnp.arange(rows, dtype=jnp.int32)).reshape(LOCAL_FF)
    spread = (hidden_here // (FF // GROUPS))[None, :] == jnp.arange(GROUPS)[:, None]
    masks = []
    for l in range(LAYERS):
        heads_on = lax.dynamic_slice_in_dim(head_mask[0, l], member * LOCAL_HEADS, LOCAL_HEADS, 1)
        heads_on = jnp.pad(heads_on.astype(BF16), ((0, 0), (0, LANES - LOCAL_HEADS)))
        groups_on = dot(group_mask[0, l].astype(BF16), spread.astype(BF16))
        groups_on = jnp.pad(groups_on, ((1, 0), (0, 0)))
        active = jnp.stack(
            [lax.dynamic_slice_in_dim(groups_on, blocks[j], 2) for j in range(TP)]
        )
        keeping = skip_mask[0, l].astype(F32)[:, None] * living
        masks.append((dot(onehot, heads_on), active, keeping))

    stream = hidden_in[0].astype(F32)
    records, weights = [], []
    forward_slow = []
    for l in range(LAYERS):
        events, pieces = {}, []
        if l + 1 < LAYERS:
            pack = after(attention_packs[l + 1], w_joint)
            pieces = gather_planes(pack) if compact() else gather_slow(pack)
        if l == 0 and compact():
            first_others = [exchange(after(forward_first[0], w_joint), TP)]
            events["normed_one"] = normed_events
            events["far_one"] = [forward_first[1]]
            events["halos"] = [forward_first[2]]
            events["mixed"] = [forward_first[3], first_others[0]]

        def hold(name, value, *more, events=events, l=l, pieces=pieces):
            if l == 0 and compact() and name == "halos":
                first_others.extend(exchange(after(p, value), TP) for p in forward_first[1:])
                events["branch"] = first_others[1:3]
            if l + 1 < LAYERS:
                if name == "halos":
                    held = after((expand_weight[l + 1], reduce_weight[l + 1]), value)
                    forward = pack_forward(*held)
                    forward_slow.append(gather_slow(forward))
                    events["mixed"] = events.get("mixed", []) + [forward]
                if name == "branch" and compact():
                    events["branch"] = events.get("branch", []) + pieces[1:2]
                    pieces.extend([exchange(piece, TP) for piece in pieces])
                    events["far_two"] = pieces[2:6]
                if name == "far_two":
                    following.append(open_attention(pieces))
                    events["feedout"] = following
            return after(value, *more, *events.get(name, []))

        def open_here(mine, l=l):
            if l == 0:
                return open_forward(forward_first + first_others if compact() else forward_first)
            return open_forward(forward_slow[l - 1])

        following = []
        stream, record, used = layer_forward(
            stream, mods[l], w_joint, project_columns, open_here, masks[l], context, hold, l > 0
        )
        records.append(record)
        weights.append(used)
        if following:
            w_joint, project_columns = following[0]
    final_state = stream.astype(BF16)[None]
    adjoint = cotangent[0].astype(F32)
    grads, d_mods = [None] * LAYERS, [None] * LAYERS
    waiting = None
    for l in reversed(range(LAYERS)):
        state = {}

        def hold(name, value, *more, waiting=waiting, state=state):
            events = []
            if waiting is not None:
                above, pieces, forward_sum = waiting
                steps = ["far_feed", "d_normed_two", "d_branch", "d_mixed"]
                if compact() and name in steps:
                    step = steps.index(name)
                    state["sum"] = owner_sum(pieces, step, state.get("sum"))
                    events.append(state["sum"])
                if name == "d_branch":
                    state["forward"] = tuple(return_forward(forward_sum))
                    events.append(state["forward"])
                if name == "d_joint":
                    owned = state["sum"] if compact() else owner_sum_slow(pieces)
                    state["attention"] = return_attention(owned)
                    grads[above] = state["attention"] + state["forward"]
                    events.append(state["attention"])
            return after(value, *more, *events)

        adjoint, d_mods[l], pieces, forward_sum = layer_backward(
            adjoint, records[l], mods[l], weights[l], masks[l], context, l == 0, hold
        )
        waiting = (l, pieces, forward_sum)
    _, pieces, forward_sum = waiting
    if compact():
        owned = None
        for step in range(4):
            owned = owner_sum(pieces, step, owned)
    else:
        owned = owner_sum_slow(pieces)
    grads[0] = return_attention(owned) + tuple(return_forward(forward_sum))

    d_mod = jnp.stack(d_mods, axis=1)
    d_mod = d_mod[1] + shifted(d_mod[0], -1)
    d_mod = jnp.transpose(d_mod.reshape(LAYERS, seq, 6 * D // seq), (1, 0, 2))
    d_mod = jnp.broadcast_to(d_mod[None], (planes,) + d_mod.shape)
    d_mod = d_mod.reshape((planes * seq,) + d_mod.shape[2:])
    d_mod = lax.all_to_all(d_mod, EVERY, 0, 0, tiled=True)
    modulation_grad = jnp.stack(
        [
            lax.dot_general(
                condition.astype(F32),
                d_mod[:, l],
                (((0,), (0,)), ((), ())),
                precision=HIGH,
                preferred_element_type=F32,
            )
            for l in range(LAYERS)
        ]
    )
    joint_grad, project_grad, expand_grad, reduce_grad = [
        jnp.stack([grads[l][i] for l in range(LAYERS)]) for i in range(4)
    ]
    return (
        final_state,
        adjoint[None],
        modulation_grad,
        joint_grad,
        project_grad,
        expand_grad,
        reduce_grad,
    )


def solution(mesh):
    planes, seq = mesh.shape["dp"], mesh.shape["seq"]
    mesh = Mesh(mesh.devices.reshape(planes, seq // TP, TP), EVERY)
    in_specs = (
        P("dp", SEQ, None),
        P("dp", None),
        P("dp", None),
        P("dp", None, None, None),
        P("dp", None, None, None),
        P("dp", None, SEQ),
        P(None, "dp", SEQ),
        P(None, "dp", SEQ),
        P(None, "dp", SEQ),
        P(None, "dp", SEQ),
        P(None, "dp", SEQ),
        P("dp", SEQ, None),
    )
    out_specs = (
        P("dp", SEQ, None),
        P("dp", SEQ, None),
        P(None, "dp", SEQ),
        P(None, "dp", SEQ),
        P(None, "dp", SEQ),
        P(None, "dp", SEQ),
        P(None, "dp", SEQ),
    )
    return jax.shard_map(shards, mesh=mesh, in_specs=in_specs, out_specs=out_specs, check_vma=False)
```

```python
import functools
import math

import jax
import jax.numpy as jnp
import numpy as np
from jax import lax
from jax.experimental import pallas as pl
from jax.experimental.pallas import tpu as pltpu
from jax.sharding import Mesh
from jax.sharding import PartitionSpec as P

D = 1152
HEADS = 16
HEAD_DIM = 72
FF = 4608
GROUPS = 16
LAYERS = 2

TP = 4
LANES = 128
LOCAL_HEADS = HEADS // TP
LOCAL_FF = FF // TP
WIDTH = -(-LOCAL_HEADS * HEAD_DIM // LANES) * LANES
AFTER = 128
CHUNK = 256

SEQ = ("group", "member")
EVERY = ("dp", "group", "member")
OWNERS = ("dp", "group")

EPS = 1e-06
HIGH = lax.Precision.HIGHEST
NEGATIVE = -1e30
FACTOR = HEAD_DIM ** (-0.5)
F32 = jnp.float32
BF16 = jnp.bfloat16


def sizes():
    groups, planes = lax.axis_size("group"), lax.axis_size("dp")
    return groups * TP, groups, planes


def place():
    return lax.axis_index("group"), lax.axis_index("member")


def here():
    return jnp.stack([lax.axis_index("dp"), *place()])


def device_of(unit, groups):
    return (unit % groups) * TP + unit // groups


def unit_table(seq, groups):
    return np.array([(s % TP) * groups + s // TP for s in range(seq)])


def my_unit():
    _, groups, _ = sizes()
    group, member = place()
    return member * groups + group


def exchange(value, mask):
    seq, _, _ = sizes()
    return lax.ppermute(value, SEQ, [(i, i ^ mask) for i in range(seq)])


def shifted(value, steps):
    count, _, _ = sizes()
    return lax.ppermute(
        value, SEQ, [(i, i + steps) for i in range(count) if 0 <= i + steps < count]
    )


def from_plane(value, back):
    planes = lax.axis_size("dp")
    return lax.ppermute(value, "dp", [(d, (d + back) % planes) for d in range(planes)])


def after(value, *events):
    return lax.optimization_barrier((value,) + events)[0]


def dot(left, right):
    return jnp.dot(left, right, preferred_element_type=F32)


def through_rows(left, right):
    return lax.dot_general(left, right, (((0,), (0,)), ((), ())), preferred_element_type=F32)


def against_cols(left, right):
    return lax.dot_general(left, right, (((1,), (1,)), ((), ())), preferred_element_type=F32)


def near(mine):
    return [mine, exchange(mine, 1)]


def far(theirs):
    return [theirs, exchange(theirs, 1)]


def pair_sum(parts):
    return parts[0].astype(F32) + exchange(parts[1], 1).astype(F32)


def far_sum(pair):
    return exchange(pair.astype(BF16), 2).astype(F32)


def kinds_table(seq, groups):
    pairs, kinds = [], np.zeros((3, seq), np.int32)
    for r in range(3):
        targets = [device_of((3 * s + r) % seq, groups) for s in range(seq)]
        pairs.append(list(enumerate(targets)))
        for s in range(seq):
            kinds[r, targets[s]] = (3 * s + r) // seq
    return pairs, kinds


def my_kinds():
    seq, groups, _ = sizes()
    return jnp.asarray(kinds_table(seq, groups)[1])[:, lax.axis_index(SEQ)]


def deal_joint(joint):
    seq, groups, _ = sizes()
    pairs, _ = kinds_table(seq, groups)
    cols = joint.shape[2] // 3
    sent = [
        jnp.concatenate(
            [joint[l, :, r * cols : (r + 1) * cols] for l in range(LAYERS)], axis=1
        )
        for r in range(3)
    ]
    return [lax.ppermute(part, SEQ, pairs[r]) for r, part in enumerate(sent)]


def return_joint(parts):
    seq, groups, _ = sizes()
    pairs, _ = kinds_table(seq, groups)
    back = [lax.ppermute(part, SEQ, [(b, a) for a, b in pairs[r]]) for r, part in enumerate(parts)]
    return jnp.concatenate(back, axis=1).astype(F32)


def choose(which, options):
    first, second, third = options
    return jnp.where(which == 0, first, jnp.where(which == 1, second, third))


def pack_attention_any(got, projects):
    kinds = my_kinds()
    cols = projects[0].shape[1]
    packs = []
    for l, project in enumerate(projects):
        parts = [part[:, l * cols : (l + 1) * cols] for part in got]
        sent = [
            jnp.where(kinds[0] == k, parts[0], jnp.where(kinds[1] == k, parts[1], parts[2]))
            for k in range(3)
        ]
        packs.append(jnp.concatenate(sent + [project], axis=1))
    return packs


def open_attention_any(stack):
    _, groups, planes = sizes()
    height, cols = stack.shape[1], stack.shape[2] // 4
    stack = stack.reshape(planes, groups, height, 4, cols)
    kinds = jnp.transpose(stack, (3, 0, 2, 1, 4)).reshape(4, D, groups * cols)
    blank = jnp.zeros((D, WIDTH - groups * cols), BF16)
    joint = jnp.concatenate([part for k in range(3) for part in (kinds[k], blank)], axis=1)
    return joint, kinds[3].reshape(TP, D // TP, groups * cols)


def join_project_any(got):
    _, groups, _ = sizes()
    rows = got.reshape(TP, D // TP, groups, -1).transpose(1, 2, 0, 3).reshape(D // TP, D)
    return jnp.concatenate([rows, jnp.zeros((WIDTH - D // TP, D), BF16)], axis=0)


def split_project_any(grad):
    _, groups, _ = sizes()
    chunks = grad[: D // TP].reshape(D // TP, groups, TP, -1).transpose(2, 0, 1, 3)
    return chunks.reshape(TP, D // TP, -1)


def split_attention_any(g_joint, got):
    _, groups, planes = sizes()
    cols = D // TP // groups
    parts = [g_joint[:, k * WIDTH : k * WIDTH + groups * cols] for k in range(3)]
    parts = jnp.stack(parts + [got.reshape(D, groups * cols)])
    parts = parts.reshape(4, planes, D // planes, groups, cols).transpose(1, 3, 2, 0, 4)
    return parts.reshape(planes * groups, D // planes, 4 * cols)


def unpack_attention_any(owned):
    kinds = my_kinds()
    cols = owned.shape[1] // 4
    own = [owned[:, k * cols : (k + 1) * cols] for k in range(4)]
    return [choose(kinds[r], own[:3]).astype(BF16) for r in range(3)] + [own[3].astype(F32)]


def pack_forward_any(expand, reduce):
    seq, groups, planes = sizes()
    cols, rows = expand.shape[1] // planes, reduce.shape[0] // seq
    chunks = []
    for unit in unit_table(seq, groups):
        q = unit % planes
        chunks += [expand[:, q * cols : (q + 1) * cols], reduce[unit * rows : (unit + 1) * rows]]
    chunks = jnp.concatenate([chunk.reshape(-1, cols) for chunk in chunks], axis=0)
    return chunks.reshape(seq, -1, cols)


def unpack_forward_any(got):
    seq, _, planes = sizes()
    ways, cols = seq // planes, got.shape[2]
    height, width = D // planes, got.shape[2] * planes
    mine = got.reshape((planes, ways) + got.shape[1:])
    mine = lax.dynamic_index_in_dim(mine, my_unit() // planes, 1, keepdims=False)
    expand = jnp.concatenate([mine[d, :height] for d in range(planes)], axis=1)
    reduce = got[:, height:].reshape(seq, cols, D // seq)
    reduce = jnp.concatenate([reduce[s] for s in range(seq)], axis=1)
    blocks = [reduce[:, k * width : (k + 1) * width] for k in range(D // width)]
    return jnp.concatenate([expand] + blocks, axis=0)


def open_forward_any(stack):
    _, groups, planes = sizes()
    height, width = D // planes, stack.shape[2]
    rows = width // planes
    stack = stack.reshape((planes, groups) + stack.shape[1:])
    expand = jnp.transpose(stack[:, :, :height], (0, 2, 1, 3)).reshape(D, groups * width)
    reduce = stack[:, :, height:].reshape(planes, groups, D // width, rows, width)
    reduce = jnp.transpose(reduce, (1, 0, 3, 2, 4)).reshape(groups * planes * rows, D)
    return expand, reduce


def split_forward_any(g_expand, g_reduce):
    _, groups, planes = sizes()
    height, width = D // planes, LOCAL_FF // groups
    rows = width // planes
    expand = g_expand.reshape(planes, height, groups, width).transpose(0, 2, 1, 3)
    reduce = g_reduce.reshape(groups, planes, rows, D // width, width).transpose(1, 0, 3, 2, 4)
    reduce = reduce.reshape(planes, groups, rows * D // width, width)
    stack = jnp.concatenate([expand, reduce], axis=2)
    return stack.reshape((planes * groups,) + stack.shape[2:])


def pack_return_any(owned):
    seq, _, planes = sizes()
    ways, height, width = seq // planes, D // planes, owned.shape[1]
    rows, cols = width // planes, width // planes
    blocks = owned[height:].reshape(D // width, rows, width)
    reduce = jnp.concatenate([blocks[k] for k in range(D // width)], axis=1)
    chunks = []
    for s in range(seq):
        d = s // ways
        chunks.append(owned[:height, d * cols : (d + 1) * cols])
        chunks.append(reduce[:, s * (D // seq) : (s + 1) * (D // seq)].reshape(-1, cols))
    return jnp.concatenate(chunks, axis=0).reshape(seq, -1, cols)


def unpack_return_any(got):
    seq, groups, planes = sizes()
    ways, cols, height = seq // planes, got.shape[2], D // planes
    got = jnp.swapaxes(got.reshape((groups, TP) + got.shape[1:]), 0, 1).reshape(got.shape)
    first = planes * (lax.axis_index(SEQ) % ways)
    mine = lax.dynamic_slice_in_dim(got[:, :height], first, planes)
    expand = jnp.concatenate([mine[q] for q in range(planes)], axis=1)
    return expand.astype(F32), got[:, height:].reshape(-1, D // seq).astype(F32)


def compact():
    seq, groups, planes = sizes()
    return groups == 2 and planes == 4 and D // seq % 16 == 0


def rearrange(body, arrays, outs, name):
    return pl.pallas_call(
        body,
        in_specs=[pl.BlockSpec(memory_space=pltpu.SMEM)]
        + [pl.BlockSpec(memory_space=pltpu.VMEM)] * len(arrays),
        out_specs=[pl.BlockSpec(memory_space=pltpu.VMEM)] * len(outs),
        out_shape=[jax.ShapeDtypeStruct(shape, dtype) for shape, dtype in outs],
        compiler_params=pltpu.CompilerParams(vmem_limit_bytes=48 * 1024 * 1024),
        cost_estimate=pl.CostEstimate(
            flops=0,
            bytes_accessed=sum(math.prod(shape) * 4 for shape, _ in outs),
            transcendentals=0,
        ),
        name=name,
    )(here(), *arrays)


def side_by_side(parts):
    return jnp.concatenate(parts, axis=1)


def kind_sent(me_ref, r):
    unit = me_ref[2] * 2 + me_ref[1]
    source = (3 * (unit + 8 - r)) % 8
    return (3 * source + r) // 8


def pack_attention_kernel(me_ref, a_ref, b_ref, c_ref, *refs):
    cols = refs[0].shape[1]
    first, second = kind_sent(me_ref, 0), kind_sent(me_ref, 1)
    for l in range(LAYERS):
        project_ref, out_ref = refs[l], refs[LAYERS + l]
        at = slice(l * cols, (l + 1) * cols)
        for half in range(2):
            rows = slice(half * cols, (half + 1) * cols)
            a, b, c = a_ref[rows, at], b_ref[rows, at], c_ref[rows, at]
            parts = [jnp.where(first == k, a, jnp.where(second == k, b, c)) for k in range(3)]
            out_ref[:, half * 4 * cols : (half + 1) * 4 * cols] = side_by_side(
                parts + [project_ref[rows]]
            )


def by_plane(me_ref, refs):
    if len(refs) == 1:
        return [(d, refs[0][2 * d], refs[0][2 * d + 1]) for d in range(4)]
    got = []
    for step in range(4):
        own, other = refs[step][...], refs[4 + step][...]
        first = jnp.where(me_ref[1] == 0, own, other)
        second = jnp.where(me_ref[1] == 0, other, own)
        got.append(((me_ref[0] + 4 - step) % 4, first, second))
    return got


def rows_at(start, count):
    if isinstance(start, int):
        return slice(start, start + count)
    return pl.ds(pl.multiple_of(start, 16), count)


def open_attention_kernel(me_ref, *refs):
    *refs, joint_ref, project_ref = refs
    cols = refs[0].shape[-2]
    blank = jnp.zeros((cols, WIDTH - 2 * cols), BF16)
    for plane, first, second in by_plane(me_ref, refs):
        for half in range(2):
            pieces = [
                [piece[:, (4 * half + k) * cols : (4 * half + k + 1) * cols] for k in range(4)]
                for piece in (first, second)
            ]
            parts = []
            for kind in range(3):
                parts += [pieces[0][kind], pieces[1][kind], blank]
            joint_ref[rows_at(plane * 2 * cols + half * cols, cols)] = side_by_side(parts)
            project_ref[plane, half * cols : (half + 1) * cols] = side_by_side(
                [pieces[0][3], pieces[1][3]]
            )


def join_project_kernel(me_ref, got_ref, out_ref):
    cols = got_ref.shape[2] // 2
    rows = got_ref.shape[1]
    out_ref[:rows] = side_by_side(
        [got_ref[t][:, g * cols : (g + 1) * cols] for g in range(2) for t in range(4)]
    )
    out_ref[rows:] = jnp.zeros((out_ref.shape[0] - rows, out_ref.shape[1]), BF16)


def split_project_kernel(me_ref, grad_ref, out_ref):
    rows, cols = out_ref.shape[1], out_ref.shape[2] // 2
    for t in range(4):
        out_ref[t] = side_by_side(
            [grad_ref[:rows, (g * 4 + t) * cols : (g * 4 + t + 1) * cols] for g in range(2)]
        )


def pack_forward_kernel(me_ref, expand_ref, reduce_ref, out_ref):
    cols = reduce_ref.shape[1]
    for s, unit in enumerate(unit_table(8, 2)):
        at = slice(unit % 4 * cols, (unit % 4 + 1) * cols)
        out_ref[s] = side_by_side(
            [
                expand_ref[:cols, at],
                expand_ref[cols:, at],
                reduce_ref[unit * cols : (unit + 1) * cols],
            ]
        )


def unpack_forward_kernel(me_ref, got_ref, out_ref):
    cols = got_ref.shape[1]
    unit = me_ref[2] * 2 + me_ref[1]
    for half in range(2):
        parts = []
        for d in range(4):
            parts.append(got_ref[2 * d + unit // 4][:, half * cols : (half + 1) * cols])
        for s in range(4):
            parts.append(got_ref[4 * half + s][:, 2 * cols :])
        out_ref[half * cols : (half + 1) * cols] = side_by_side(parts)


def open_forward_kernel(me_ref, *refs):
    *refs, expand_ref, reduce_ref = refs
    height = refs[0].shape[-2]
    rows, width = height // 2, D // 2
    for plane, first, second in by_plane(me_ref, refs):
        expand_ref[rows_at(plane * height, height)] = side_by_side(
            [first[:, :width], second[:, :width]]
        )
        for group, piece in enumerate((first, second)):
            reduce_ref[rows_at(group * width + plane * rows, rows)] = side_by_side(
                [piece[:rows, width:], piece[rows:, width:]]
            )


def put_pieces(me_ref, outs, step, pair):
    if len(outs) == 1:
        outs[0][2 * step], outs[0][2 * step + 1] = pair
    else:
        outs[step][...] = jnp.where(me_ref[1] == 0, pair[0], pair[1])
        outs[4 + step][...] = jnp.where(me_ref[1] == 0, pair[1], pair[0])


def split_forward_kernel(me_ref, expand_ref, reduce_ref, *outs):
    height = outs[0].shape[-2]
    rows, width = height // 2, D // 2
    for step in range(4):
        plane = step if len(outs) == 1 else (me_ref[0] + 3 - step) % 4
        expand = expand_ref[rows_at(plane * height, height)]
        pair = []
        for group in range(2):
            reduce = reduce_ref[rows_at(group * width + plane * rows, rows)]
            part = expand[:, group * width : (group + 1) * width]
            upper = side_by_side([part[:rows], reduce[:, :width]])
            lower = side_by_side([part[rows:], reduce[:, width:]])
            pair.append(jnp.concatenate([upper, lower], axis=0))
        put_pieces(me_ref, outs, step, pair)


def pack_return_kernel(me_ref, whole_ref, out_ref):
    cols = out_ref.shape[1]
    for s in range(8):
        at = slice(s // 2 * cols, (s // 2 + 1) * cols)
        right = slice((4 + s % 4) * cols, (5 + s % 4) * cols)
        out_ref[s] = side_by_side(
            [
                whole_ref[:cols, at],
                whole_ref[cols:, at],
                whole_ref[s // 4 * cols : (s // 4 + 1) * cols, right],
            ]
        )


def unpack_return_kernel(me_ref, got_ref, expand_ref, reduce_ref):
    cols = got_ref.shape[1]
    for half in range(2):
        parts = []
        for q in range(4):
            device = q % 2 * 4 + 2 * (me_ref[2] % 2) + q // 2
            parts.append(got_ref[device][:, half * cols : (half + 1) * cols])
        expand_ref[half * cols : (half + 1) * cols] = side_by_side(parts).astype(F32)
    for s, unit in enumerate(unit_table(8, 2)):
        part = got_ref[s][:, 2 * cols :].astype(F32)
        reduce_ref[:, unit * cols : (unit + 1) * cols] = part.T


def split_attention_kernel(me_ref, joint_ref, project_ref, *outs):
    cols = outs[0].shape[-2]
    for step in range(4):
        plane = step if len(outs) == 1 else (me_ref[0] + 3 - step) % 4
        parts = [[], []]
        for half in range(2):
            rows = joint_ref[rows_at(plane * 2 * cols + half * cols, cols)]
            project = project_ref[plane, half * cols : (half + 1) * cols]
            for group in range(2):
                for kind in range(3):
                    at = kind * WIDTH + group * cols
                    parts[group].append(rows[:, at : at + cols])
                parts[group].append(project[:, group * cols : (group + 1) * cols])
        put_pieces(me_ref, outs, step, [side_by_side(part) for part in parts])


def unpack_attention_kernel(me_ref, whole_ref, a_ref, b_ref, c_ref, project_ref):
    cols = whole_ref.shape[0]
    for half in range(2):
        rows = slice(half * cols, (half + 1) * cols)
        parts = []
        for k in range(4):
            at = (half * 4 + k) * cols
            parts.append(whole_ref[:, at : at + cols])
        for r, ref in enumerate((a_ref, b_ref, c_ref)):
            ref[rows] = choose(kind_sent(me_ref, r), parts[:3]).astype(BF16)
        project_ref[rows] = parts[3].astype(F32)


def pack_attention(joint, project):
    got = deal_joint(joint)
    projects = [project[l] for l in range(LAYERS)]
    if not compact():
        return pack_attention_any(got, projects)
    cols = project.shape[2]
    outs = [((cols, 8 * cols), BF16)] * LAYERS
    return rearrange(pack_attention_kernel, [*got, *projects], outs, "pack_attention")


def pack_forward(expand, reduce, *events):
    cols = reduce.shape[1]
    if compact():
        outs = [((8, cols, 3 * cols), BF16)]
        (chunks,) = rearrange(pack_forward_kernel, [expand, reduce], outs, "pack_forward")
    else:
        chunks = pack_forward_any(expand, reduce)
    got = after(lax.all_to_all(chunks, SEQ, 0, 0, tiled=True), *events)
    if not compact():
        return unpack_forward_any(got)
    return rearrange(
        unpack_forward_kernel, [got], [((2 * cols, 8 * cols), BF16)], "unpack_forward"
    )[0]


def gather_slow(pack):
    return [lax.all_gather(pack, OWNERS, axis=0, tiled=False)]


def gather_planes(pack):
    return [pack] + [from_plane(pack, back) for back in range(1, 4)]


def open_attention(pieces):
    if not compact():
        return open_attention_any(pieces[0])
    cols = D // 8
    outs = [((D, 3 * WIDTH), BF16), ((TP, 2 * cols, 2 * cols), BF16)]
    return rearrange(open_attention_kernel, pieces, outs, "open_attention")


def project_matrix(columns):
    got = lax.all_to_all(columns, "member", 0, 0, tiled=True)
    if not compact():
        return join_project_any(got)
    return rearrange(join_project_kernel, [got], [((WIDTH, D), BF16)], "join_project")[0]


def open_forward(pieces):
    if not compact():
        return open_forward_any(pieces[0])
    outs = [((D, D), BF16), ((D, D), BF16)]
    return rearrange(open_forward_kernel, pieces, outs, "open_forward")


def piece_outs(shape, fast):
    return [(shape, BF16)] * 8 if fast else [((8,) + shape, BF16)]


def split_project(g_project):
    if compact():
        outs = [((TP, D // TP, D // TP), BF16)]
        (chunks,) = rearrange(split_project_kernel, [g_project], outs, "split_project")
    else:
        chunks = split_project_any(g_project)
    return lax.all_to_all(chunks, "member", 0, 0, tiled=True)


def split_attention(g_joint, project, fast):
    if not compact():
        return [split_attention_any(g_joint, project)]
    outs = piece_outs((D // 8, D), fast)
    return rearrange(split_attention_kernel, [g_joint, project], outs, "split_attention")


def split_forward(g_expand, g_reduce, fast):
    if not compact():
        return [split_forward_any(g_expand, g_reduce)]
    outs = piece_outs((D // 4, D), fast)
    return rearrange(split_forward_kernel, [g_expand, g_reduce], outs, "split_forward")


def owner_sum(pieces, step, carried, *events):
    own, other = pieces[step], after(pieces[4 + step], *events)
    total = own.astype(F32) + exchange(other, TP).astype(F32)
    if step:
        total = total + from_plane(carried, 1).astype(F32)
    return total.astype(BF16)


def owner_sum_slow(pieces):
    return lax.psum_scatter(pieces[0], OWNERS, scatter_dimension=0, tiled=False)


def return_attention(owned):
    if compact():
        cols = D // 8
        outs = [((2 * cols, cols), BF16)] * 3 + [((2 * cols, cols), F32)]
        *parts, project = rearrange(unpack_attention_kernel, [owned], outs, "unpack_attention")
    else:
        *parts, project = unpack_attention_any(owned)
    return return_joint(parts), project


def return_forward(owned):
    cols = D // 8
    if compact():
        outs = [((8, cols, 3 * cols), BF16)]
        (chunks,) = rearrange(pack_return_kernel, [owned], outs, "pack_return")
    else:
        chunks = pack_return_any(owned)
    got = lax.all_to_all(chunks, SEQ, 0, 0, tiled=True)
    if not compact():
        return unpack_return_any(got)
    outs = [((2 * cols, 4 * cols), F32), ((cols, 8 * cols), F32)]
    expand, reduce = rearrange(unpack_return_kernel, [got], outs, "unpack_return")
    return expand, reduce.T


def half_call(body, half, chunks, matrices, tokens, into, partial, name):
    count = chunks[0].shape[0]

    def whole(array):
        return pl.BlockSpec(array.shape, lambda i: (0,) * array.ndim)

    def slot(shape):
        return pl.BlockSpec(shape, lambda i: (2 * half + i,) + (0,) * (len(shape) - 1))

    kept = [array for _, array in into if array is not None]
    operands = [*chunks, *matrices, *tokens]
    specs = [whole(array) for array in (*chunks, *matrices)]
    specs += [slot((array.shape[0] // TP,) + array.shape[1:]) for array in tokens]
    out_specs = [slot((count, width)) for width, _ in into]
    shapes = [jax.ShapeDtypeStruct((TP * count, width), BF16) for width, _ in into]
    if partial:
        out_specs += [pl.BlockSpec((count, D), lambda i: (0, 0))] * 2
        shapes += [jax.ShapeDtypeStruct((count, D), BF16)] * 2
    aliases = {len(operands) + k: k for k in range(len(kept))}
    work = sum(2 * 2 * count * math.prod(matrix.shape) for matrix in matrices)

    def kernel(a_ref, b_ref, *refs):
        n = len(matrices) + len(tokens)
        mine = pl.program_id(0) == 0
        rows = jnp.where(mine, a_ref[...], b_ref[...])
        body(rows, mine, refs[:n], refs[n + len(kept) :])

    return pl.pallas_call(
        kernel,
        grid=(2,),
        in_specs=specs + [pl.BlockSpec(memory_space=pl.ANY)] * len(kept),
        out_specs=out_specs,
        out_shape=shapes,
        input_output_aliases=aliases,
        compiler_params=kernel_params(),
        cost_estimate=pl.CostEstimate(
            flops=work, bytes_accessed=work // 512, transcendentals=2 * count * D
        ),
        name=name,
    )(*operands, *kept)


def slot_products(product, half, tokens, matrix, name, slots=TP):
    count = tokens.shape[0] // slots

    def kernel(rows_ref, matrix_ref, a_ref, b_ref):
        value = product(rows_ref[...], matrix_ref[...])
        put_partial(pl.program_id(0) == 0, value, a_ref, b_ref)

    return pl.pallas_call(
        kernel,
        grid=(2,),
        in_specs=[
            pl.BlockSpec((count, tokens.shape[1]), lambda i: (2 * half + i, 0)),
            pl.BlockSpec(matrix.shape, lambda i: (0, 0)),
        ],
        out_specs=[pl.BlockSpec((count, D), lambda i: (0, 0))] * 2,
        out_shape=[jax.ShapeDtypeStruct((count, D), BF16)] * 2,
        compiler_params=kernel_params(),
        cost_estimate=pl.CostEstimate(
            flops=4 * count * math.prod(matrix.shape),
            bytes_accessed=2 * math.prod(matrix.shape),
            transcendentals=0,
        ),
        name=name,
    )(tokens, matrix)


def put_partial(mine, value, a_ref, b_ref):
    value = value.astype(BF16)

    @pl.when(mine)
    def _():
        a_ref[...] = value

    @pl.when(jnp.logical_not(mine))
    def _():
        b_ref[...] = value


def chunks_of(width):
    return [slice(at, min(at + CHUNK, width)) for at in range(0, width, CHUNK)]


def joint_body(rows, mine, refs, outs):
    outs[0][...] = dot(rows, refs[0][...]).astype(BF16)


def forward_body(rows, mine, refs, outs):
    expand_ref, reduce_ref, sides_ref, active_ref = refs
    activated_ref, slope_ref, a_ref, b_ref = outs
    root = math.sqrt(2.0 / math.pi)
    before, now = sides_ref[:, 0:1], sides_ref[:, 1:2]
    for at in chunks_of(LOCAL_FF):
        pre = dot(rows, expand_ref[:, at])
        square = pre * pre
        curve = jnp.tanh(root * pre * (1.0 + 0.044715 * square))
        half = 0.5 + 0.5 * curve
        mask = before * active_ref[0, 0:1, at] + now * active_ref[0, 1:2, at]
        slope = half + pre * (half - half * half) * (2.0 * root * (1.0 + 0.134145 * square))
        activated_ref[:, at] = (pre * half * mask).astype(BF16)
        slope_ref[:, at] = (slope * mask).astype(BF16)
    put_partial(mine, dot(activated_ref[...], reduce_ref[...]), a_ref, b_ref)


def backward_body(rows, mine, refs, outs):
    expand_ref, reduce_ref, slope_ref = refs
    d_pre_ref, a_ref, b_ref = outs
    for at in chunks_of(LOCAL_FF):
        d_active = against_cols(rows, reduce_ref[at])
        d_pre_ref[:, at] = (d_active * slope_ref[:, at].astype(F32)).astype(BF16)
    put_partial(mine, against_cols(d_pre_ref[...], expand_ref[...]), a_ref, b_ref)


def head_tiles(head):
    low = head * HEAD_DIM // LANES * LANES
    high = -(-(head + 1) * HEAD_DIM // LANES) * LANES
    return low, high


def lanes_of(head, shape):
    low, high = head_tiles(head)
    lane = lax.broadcasted_iota(jnp.int32, shape, 1) + low
    return (lane >= head * HEAD_DIM) & (lane < (head + 1) * HEAD_DIM)


def key_tiles(refs, halos, block, base, low, high):
    before_ref, after_ref = halos
    prev_ref, here_ref, next_ref = refs
    prev = jnp.where(block == 0, before_ref[:, base + low : base + high], prev_ref[:, low:high])
    following = jnp.where(
        block == TP - 1, after_ref[:, base + low : base + high], next_ref[:, low:high]
    )
    return prev, here_ref[:, low:high], following


def attend_kernel(base, me_ref, q_ref, *refs):
    keys, values, halos = refs[0:3], refs[3:6], refs[6:8]
    segq_ref, segk_ref, head_ref, mixed_ref, lse_ref = refs[8:]
    block = (base + pl.program_id(0)) ^ me_ref[2]
    count = q_ref.shape[0]
    allowed = segq_ref[...] == segk_ref[0]
    tiles = [jnp.zeros((count, LANES), F32) for _ in range(WIDTH // LANES)]
    total = jnp.zeros((count, LANES), F32)
    lane = lax.broadcasted_iota(jnp.int32, (count, LANES), 1)
    for head in range(LOCAL_HEADS):
        low, high = head_tiles(head)
        mine = lanes_of(head, (count, high - low))
        query = jnp.where(mine, q_ref[:, low:high], 0)
        key = key_tiles(keys, halos, block, 0, low, high)
        scores = jnp.concatenate([against_cols(query, part) for part in key], axis=1) * FACTOR
        scores = jnp.where(allowed, scores, NEGATIVE)
        highest = jnp.max(scores, axis=-1, keepdims=True)
        weights = jnp.exp(scores - highest)
        sums = jnp.sum(weights, axis=-1, keepdims=True)
        probs = (weights / sums).astype(BF16)
        out, at = 0.0, 0
        for part in key_tiles(values, halos, block, WIDTH, low, high):
            out = out + dot(probs[:, at : at + part.shape[0]], part)
            at += part.shape[0]
        out = jnp.where(mine, out, 0.0) * head_ref[:, head : head + 1]
        for k in range(low // LANES, high // LANES):
            at = k * LANES - low
            tiles[k] = tiles[k] + out[:, at : at + LANES]
        total = jnp.where(lane == head, highest + jnp.log(sums), total)
    for k, tile in enumerate(tiles):
        mixed_ref[:, k * LANES : (k + 1) * LANES] = tile.astype(BF16)
    lse_ref[...] = total


def attend_back_kernel(me_ref, q_ref, *refs):
    keys, values, halos = refs[0:3], refs[3:6], refs[6:8]
    grad_ref, mixed_ref, lse_ref, segq_ref, segk_ref, head_ref = refs[8:14]
    d_joint_ref, d_before_ref, d_after_ref, sum_ref = refs[14:]
    step = pl.program_id(0)
    block = step ^ me_ref[2]
    count = q_ref.shape[0]

    @pl.when(step == 0)
    def _():
        sum_ref[...] = jnp.zeros_like(sum_ref)

    prev = jnp.where(block == 0, TP, jnp.maximum(block - 1, 0) ^ me_ref[2])
    following = jnp.where(block == TP - 1, TP + 1, jnp.minimum(block + 1, TP - 1) ^ me_ref[2])
    windows = [
        (pl.ds(pl.multiple_of(prev * count, count), count), 0),
        (pl.ds(pl.multiple_of(step * count, count), count), count),
        (pl.ds(pl.multiple_of(following * count, count), AFTER), 2 * count),
    ]
    rows = pl.ds(pl.multiple_of(step * count, count), count)
    allowed = segq_ref[...] == segk_ref[0]
    tiles = [jnp.zeros((count, LANES), F32) for _ in range(WIDTH // LANES)]
    for head in range(LOCAL_HEADS):
        low, high = head_tiles(head)
        mine = lanes_of(head, (count, high - low))
        query = jnp.where(mine, q_ref[:, low:high], 0)
        key = key_tiles(keys, halos, block, 0, low, high)
        value = key_tiles(values, halos, block, WIDTH, low, high)
        active = head_ref[:, head : head + 1]
        grad = jnp.where(mine, grad_ref[:, low:high].astype(F32) * active, 0.0)
        balance = jnp.sum(grad * mixed_ref[:, low:high].astype(F32), axis=-1, keepdims=True)
        grad = grad.astype(BF16)
        scores = jnp.concatenate([against_cols(query, part) for part in key], axis=1) * FACTOR
        probs = jnp.where(allowed, jnp.exp(scores - lse_ref[:, head : head + 1]), 0.0)
        d_probs = jnp.concatenate([against_cols(grad, part) for part in value], axis=1)
        d_scores = (probs * (d_probs - balance)).astype(BF16)
        probs = probs.astype(BF16)
        d_query = 0.0
        for (window, at), part in zip(windows, key):
            piece = d_scores[:, at : at + part.shape[0]]
            d_query = d_query + dot(piece, part)
            sum_ref[window, low:high] += through_rows(piece, query) * FACTOR
            sum_ref[window, WIDTH + low : WIDTH + high] += through_rows(
                probs[:, at : at + part.shape[0]], grad
            )
        d_query = jnp.where(mine, d_query, 0.0)
        for k in range(low // LANES, high // LANES):
            at = k * LANES - low
            tiles[k] = tiles[k] + d_query[:, at : at + LANES]
    for k, tile in enumerate(tiles):
        d_joint_ref[rows, k * LANES : (k + 1) * LANES] = (tile * FACTOR).astype(BF16)

    @pl.when(step == pl.num_programs(0) - 1)
    def _():
        d_joint_ref[:, WIDTH:] = sum_ref[: TP * count].astype(BF16)
        d_before_ref[...] = sum_ref[TP * count : (TP + 1) * count].astype(BF16)
        d_after_ref[...] = sum_ref[(TP + 1) * count : (TP + 1) * count + AFTER].astype(BF16)


def kernel_params():
    return pltpu.CompilerParams(
        dimension_semantics=("arbitrary",), vmem_limit_bytes=48 * 1024 * 1024
    )


def block_specs(count, base=0):
    def rows(width):
        return pl.BlockSpec((count, width), lambda j, me: (base + j, 0))

    def whole(shape):
        return pl.BlockSpec(shape, lambda j, me: (0,) * len(shape))

    def around(kind):
        def before(j, me):
            return (jnp.maximum(((base + j) ^ me[2]) - 1, 0) ^ me[2], kind)

        def following(j, me):
            slot = jnp.minimum(((base + j) ^ me[2]) + 1, TP - 1) ^ me[2]
            return (slot * (count // AFTER), kind)

        return [
            pl.BlockSpec((count, WIDTH), before),
            pl.BlockSpec((count, WIDTH), lambda j, me: (base + j, kind)),
            pl.BlockSpec((AFTER, WIDTH), following),
        ]

    fixed = [rows(WIDTH)] + around(1) + around(2)
    return rows, whole, fixed + [whole((count, 2 * WIDTH)), whole((AFTER, 2 * WIDTH))]


def attend(joint, halos, segq, segk, heads, base, slots):
    span = segk.shape[2]
    count = joint.shape[0] // TP
    rows, whole, specs = block_specs(count, base)
    return pl.pallas_call(
        functools.partial(attend_kernel, base),
        grid_spec=pltpu.PrefetchScalarGridSpec(
            num_scalar_prefetch=1,
            grid=(slots,),
            in_specs=specs
            + [
                rows(1),
                pl.BlockSpec((1, 1, span), lambda j, me: (base + j, 0, 0)),
                rows(LANES),
            ],
            out_specs=[
                pl.BlockSpec((count, WIDTH), lambda j, me: (j, 0)),
                pl.BlockSpec((count, LANES), lambda j, me: (j, 0)),
            ],
        ),
        out_shape=[
            jax.ShapeDtypeStruct((slots * count, WIDTH), BF16),
            jax.ShapeDtypeStruct((slots * count, LANES), F32),
        ],
        compiler_params=kernel_params(),
        cost_estimate=pl.CostEstimate(
            flops=8 * slots * count * span * LANES * LOCAL_HEADS,
            bytes_accessed=slots * count * WIDTH * 8,
            transcendentals=slots * count * span * LOCAL_HEADS,
        ),
        name="attend",
    )(here(), *[joint] * 7, *halos, segq, segk, heads)


def attend_back(joint, halos, grad, mixed, log_total, segq, segk, heads):
    span = segk.shape[2]
    count = joint.shape[0] // TP
    rows, whole, specs = block_specs(count)
    shapes = [(TP * count, 3 * WIDTH), (count, 2 * WIDTH), (AFTER, 2 * WIDTH)]
    return pl.pallas_call(
        attend_back_kernel,
        grid_spec=pltpu.PrefetchScalarGridSpec(
            num_scalar_prefetch=1,
            grid=(TP,),
            in_specs=specs
            + [
                rows(WIDTH),
                rows(WIDTH),
                rows(LANES),
                rows(1),
                pl.BlockSpec((1, 1, span), lambda j, me: (j, 0, 0)),
                rows(LANES),
            ],
            out_specs=[whole(shape) for shape in shapes],
            scratch_shapes=[pltpu.VMEM(((TP + 2) * count, 2 * WIDTH), F32)],
        ),
        out_shape=[jax.ShapeDtypeStruct(shape, BF16) for shape in shapes],
        compiler_params=kernel_params(),
        cost_estimate=pl.CostEstimate(
            flops=20 * TP * count * span * LANES * LOCAL_HEADS,
            bytes_accessed=TP * count * WIDTH * 20,
            transcendentals=TP * count * span * LOCAL_HEADS,
        ),
        name="attend_back",
    )(here(), *[joint] * 7, *halos, grad, mixed, log_total, segq, segk, heads)


def halos_of(joint):
    _, groups, _ = sizes()
    count = joint.shape[0] // TP
    if groups == 1:
        return [jnp.zeros((rows, 2 * WIDTH), joint.dtype) for rows in (count, AFTER)]
    group, member = place()
    column = jnp.int32(WIDTH)
    last = ((member ^ (TP - 1)) * count, column)
    if groups == 2:
        first = (member * count, column)
        start = [jnp.where(group == 0, x, y) for x, y in zip(last, first)]
        got = exchange(lax.dynamic_slice(joint, start, (count, 2 * WIDTH)), TP)
        return [got, got]
    last = lax.dynamic_slice(joint, last, (count, 2 * WIDTH))
    first = lax.dynamic_slice(joint, (member * count, column), (AFTER, 2 * WIDTH))
    return [shifted(last, TP), shifted(first, -TP)]


def halos_back(d_joint, d_before, d_after):
    _, groups, _ = sizes()
    if groups == 1:
        return d_joint
    group, member = place()
    count = d_joint.shape[0] // TP
    last, first = (member ^ (TP - 1)) * count, member * count
    if groups == 2:
        d_after = jnp.pad(d_after, ((0, count - AFTER), (0, 0)))
        got = exchange(jnp.where(group == 0, d_after, d_before), TP)
        pieces = [(got, jnp.where(group == 0, last, first))]
    else:
        pieces = [(shifted(d_before, -TP), last), (shifted(d_after, TP), first)]
    for piece, at in pieces:
        start = (at, jnp.int32(WIDTH))
        sums = lax.dynamic_slice(d_joint, start, piece.shape)
        sums = (sums.astype(F32) + piece.astype(F32)).astype(BF16)
        d_joint = lax.dynamic_update_slice(d_joint, sums, start)
    return d_joint


def normed(stream):
    center = stream - jnp.mean(stream, axis=-1, keepdims=True)
    scale = lax.rsqrt(jnp.mean(center * center, axis=-1, keepdims=True) + EPS)
    return center * scale, scale


def norm_back(grad, unit, scale):
    mean = jnp.mean(grad, axis=-1, keepdims=True)
    slope = jnp.mean(grad * unit, axis=-1, keepdims=True)
    return scale * (grad - mean - unit * slope)


def per_token(vectors, sides):
    return sides[0] * vectors[0][None, :] + sides[1] * vectors[1][None, :]


def per_crop(value, sides):
    return jnp.stack([jnp.sum(value * sides[0], axis=0), jnp.sum(value * sides[1], axis=0)])


def step_embed(stamps, breadth):
    halfway = breadth // 2
    frequency = jnp.exp(-math.log(10000.0) * jnp.arange(halfway, dtype=F32) / halfway)
    angles = stamps.astype(F32)[..., None] * frequency
    return jnp.concatenate([jnp.cos(angles), jnp.sin(angles)], axis=-1)


def segment_of(places, bounds):
    return jnp.sum((places[:, None] >= bounds[None, :]).astype(jnp.int32), axis=-1)


def layer_forward(
    stream, mod, w_joint, project_columns, open_reduce, masks, context, hold, split
):
    head_tok, active, keeping = masks
    sides, living, segq, segk, slot_sides = context
    offset_one, stretch_one, gate_one, offset_two, stretch_two, gate_two = [
        per_token(mod[:, i], sides) for i in range(6)
    ]
    count = stream.shape[0]
    unit_one, _ = normed(stream)
    mine = (unit_one * (1.0 + stretch_one) + offset_one).astype(BF16)
    mine = hold("normed_one", mine)
    theirs, ours = exchange(mine, 2), near(mine)
    (joint,) = half_call(
        joint_body, 0, ours, [w_joint], [], [(3 * WIDTH, None)], False, "joint_near"
    )
    theirs = far(hold("far_one", theirs, joint))
    (joint,) = half_call(
        joint_body, 1, theirs, [w_joint], [], [(3 * WIDTH, joint)], False, "joint_far"
    )
    normed_one = ours + theirs
    halos = halos_of(joint)
    w_project = project_matrix(after(project_columns, joint))
    halos = hold("halos", halos)
    if split:
        far_rows, total_far = attend(joint, halos, segq, segk, head_tok, 2, 2)
        away = pair_sum(slot_products(dot, 0, far_rows, w_project, "branch_far", 2))
        held = after(halos, away)
        near_rows, total_near = attend(joint, held, segq, segk, head_tok, 0, 2)
        near_rows = hold("mixed", near_rows)
        close = pair_sum(slot_products(dot, 0, near_rows, w_project, "branch_near", 2))
        mixed = jnp.concatenate([near_rows, far_rows], axis=0)
        log_total = jnp.concatenate([total_near, total_far], axis=0)
    else:
        mixed, log_total = attend(joint, halos, segq, segk, head_tok, 0, TP)
        mixed = hold("mixed", mixed)
        away = pair_sum(slot_products(dot, 1, mixed, w_project, "branch_far"))
        close = pair_sum(slot_products(dot, 0, after(mixed, away), w_project, "branch_near"))
    branch = after(hold("branch", far_sum(away)), close) + close
    middle = stream + gate_one * branch * living
    unit_two, _ = normed(middle)
    mine = (unit_two * (1.0 + stretch_two) + offset_two).astype(BF16)
    theirs, ours = exchange(mine, 2), near(mine)
    w_expand, w_reduce = open_reduce(mine)
    matrices, tokens = [w_expand, w_reduce], [slot_sides, active]
    activated, slope, *parts = half_call(
        forward_body, 0, ours, matrices, tokens, [(LOCAL_FF, None)] * 2, True, "forward_near"
    )
    close = pair_sum(parts)
    theirs = far(hold("far_two", theirs, activated))
    activated, slope, *parts = half_call(
        forward_body,
        1,
        theirs,
        matrices,
        tokens,
        [(LOCAL_FF, activated), (LOCAL_FF, slope)],
        True,
        "forward_far",
    )
    away = pair_sum(parts)
    feedout = hold("feedout", far_sum(away), away) + close
    result = middle + gate_two * feedout * keeping
    record = (
        stream,
        normed_one,
        joint,
        halos,
        mixed,
        log_total,
        branch,
        middle,
        ours + theirs,
        slope,
        activated,
        feedout,
    )
    return result, record, (w_joint, w_project, w_expand, w_reduce)


def layer_backward(adjoint, record, mod, weights, masks, context, last, hold):
    (
        stream,
        normed_one,
        joint,
        halos,
        mixed,
        log_total,
        branch,
        middle,
        normed_two,
        slope,
        activated,
        feedout,
    ) = record
    w_joint, w_project, w_expand, w_reduce = weights
    head_tok, active, keeping = masks
    sides, living, segq, segk, slot_sides = context
    offset_one, stretch_one, gate_one, offset_two, stretch_two, gate_two = [
        per_token(mod[:, i], sides) for i in range(6)
    ]
    count = stream.shape[0]
    fast = compact()
    mine = (adjoint * gate_two * keeping).astype(BF16)
    theirs, ours = exchange(mine, 2), near(mine)
    matrices = [w_expand, w_reduce]
    d_pre, *parts = half_call(
        backward_body, 0, ours, matrices, [slope], [(LOCAL_FF, None)], True, "backward_near"
    )
    close = pair_sum(parts)
    theirs = far(hold("far_feed", theirs, d_pre))
    d_pre, *parts = half_call(
        backward_body, 1, theirs, matrices, [slope], [(LOCAL_FF, d_pre)], True, "backward_far"
    )
    away = pair_sum(parts)
    d_feed = jnp.concatenate(ours + theirs, axis=0)
    g_reduce = through_rows(activated, after(d_feed, away)).astype(BF16)
    d_gate_two = per_crop(after(adjoint, away) * feedout * keeping, sides)
    unit_two, scale_two = normed(middle)
    d_normed_two = hold("d_normed_two", far_sum(away), g_reduce, d_gate_two) + close
    d_middle = adjoint + norm_back(d_normed_two * (1.0 + stretch_two), unit_two, scale_two)
    mine = (d_middle * gate_one * living).astype(BF16)
    theirs, ours = exchange(mine, 2), near(mine)
    rows = after(jnp.concatenate(normed_two, axis=0), ours)
    g_expand = through_rows(rows, d_pre).astype(BF16)
    forward_pieces = split_forward(g_expand, g_reduce, False)
    d_offset_two = per_crop(after(d_normed_two, mine), sides)
    d_stretch_two = per_crop(after(d_normed_two, mine) * unit_two, sides)
    theirs = hold("d_branch", theirs, forward_pieces, d_offset_two, d_stretch_two)
    forward_sum = owner_sum_slow(forward_pieces)
    d_branch = jnp.concatenate(ours + far(theirs), axis=0)
    d_mixed = against_cols(d_branch, w_project).astype(BF16)
    g_project = split_project(through_rows(mixed, d_branch).astype(BF16))
    d_mixed = hold("d_mixed", d_mixed)
    d_joint = halos_back(
        *attend_back(joint, halos, d_mixed, mixed, log_total, segq, segk, head_tok)
    )
    d_joint = hold("d_joint", d_joint)

    def normed_parts(rows, half):
        return slot_products(against_cols, half, rows, w_joint, "d_normed")

    if last:
        g_joint = through_rows(jnp.concatenate(normed_one, axis=0), d_joint).astype(BF16)
        attention_pieces = split_attention(g_joint, g_project, fast)
        away = pair_sum(normed_parts(after(d_joint, attention_pieces), 1))
    else:
        away = pair_sum(normed_parts(d_joint, 1))
        rows = after(jnp.concatenate(normed_one, axis=0), away)
        g_joint = through_rows(rows, d_joint).astype(BF16)
        attention_pieces = split_attention(g_joint, g_project, fast)
    close = pair_sum(normed_parts(after(d_joint, away), 0))
    d_normed_one = after(far_sum(away), close, attention_pieces) + close
    unit_one, scale_one = normed(stream)
    d_stream = d_middle + norm_back(d_normed_one * (1.0 + stretch_one), unit_one, scale_one)
    d_gate_one = per_crop(d_middle * branch * living, sides)
    d_offset_one = per_crop(d_normed_one, sides)
    d_stretch_one = per_crop(d_normed_one * unit_one, sides)
    d_mod = jnp.stack(
        [d_offset_one, d_stretch_one, d_gate_one, d_offset_two, d_stretch_two, d_gate_two], axis=1
    )
    return d_stream, d_mod, attention_pieces, forward_sum


def shards(
    hidden_in,
    lengths,
    timesteps,
    head_mask,
    group_mask,
    skip_mask,
    modulation_weight,
    joint_weight,
    project_weight,
    expand_weight,
    reduce_weight,
    cotangent,
):
    seq, groups, planes = sizes()
    block = hidden_in.shape[1]
    crops = lengths.shape[1]
    mine = lax.axis_index(SEQ)
    plane = lax.axis_index("dp")
    group, member = place()
    height = D // planes

    attention_packs = pack_attention(joint_weight, project_weight)
    if compact():
        first = gather_planes(attention_packs[0])
        held = after((expand_weight[0], reduce_weight[0]), attention_packs[0])
        forward_first = gather_planes(pack_forward(*held, first))
        for k in range(4):
            first.append(exchange(after(first[k], first[-1]) if k else first[0], TP))
        mod_events, normed_events = [first[1], first[4]], [forward_first[0], first[5]]
    else:
        first = gather_slow(attention_packs[0])
        forward_first = gather_slow(pack_forward(expand_weight[0], reduce_weight[0]))
        mod_events, normed_events = [], []
    w_joint, project_columns = open_attention(first)

    stamps = jnp.zeros((planes, crops), jnp.int32)
    for step in range(planes):
        row = from_plane(timesteps[0], step) if step else timesteps[0]
        stamps = jnp.where(
            (jnp.arange(planes) == (plane - step) % planes)[:, None], row[None, :], stamps
        )
    stamps = stamps.reshape(planes * crops)
    embedded = jax.nn.silu(step_embed(stamps, D)).astype(BF16)
    condition = lax.dynamic_slice_in_dim(embedded, plane * height, height, axis=1)
    part = jnp.stack([dot(condition, modulation_weight[l]) for l in range(LAYERS)], axis=1)
    before = jnp.concatenate([jnp.zeros_like(part[:1]), part[:-1]])
    part = jnp.stack([before, part], axis=1)
    part = after(lax.all_to_all(part, EVERY, 0, 0, tiled=True), mod_events)
    part = jnp.sum(part.reshape((planes, seq) + part.shape[1:]), axis=0)
    mods = jnp.transpose(part, (2, 1, 0, 3)).reshape(LAYERS, 2, 6, D)

    bounds = jnp.cumsum(lengths[0])
    span = 2 * block + AFTER
    places = (group * TP - 1) * block + jnp.arange((TP + 1) * block + AFTER, dtype=jnp.int32)
    inside = (places >= 0) & (places < seq * block)
    segment = jnp.where(inside, segment_of(places, bounds), -1)
    segk = jnp.stack(
        [lax.dynamic_slice_in_dim(segment, (member ^ j) * block, span) for j in range(TP)]
    )[:, None, :]
    segq = segk[:, 0, block : 2 * block].reshape(TP * block, 1)
    own = segment_of(mine * block + jnp.arange(block, dtype=jnp.int32), bounds)[:, None]
    sides = [(own == mine - 1).astype(F32), ((own == mine) & (own < crops)).astype(F32)]
    living = (own < crops).astype(F32)
    onehot = (segq == jnp.arange(crops, dtype=jnp.int32)[None, :]).astype(BF16)
    blocks = jnp.stack([group * TP + (member ^ j) for j in range(TP)])
    firsts = jnp.repeat(blocks, block)[:, None]
    slot_sides = jnp.concatenate([segq == firsts - 1, (segq == firsts) & (segq < crops)], axis=1)
    context = (sides, living, segq, segk, slot_sides.astype(F32))
    rows = FF // (planes * seq)
    units = member * groups + jnp.arange(groups, dtype=jnp.int32)
    starts = (FF // planes) * jnp.arange(planes, dtype=jnp.int32)[None, :] + rows * units[:, None]
    hidden_here = (starts[:, :, None] + jnp.arange(rows, dtype=jnp.int32)).reshape(LOCAL_FF)
    spread = (hidden_here // (FF // GROUPS))[None, :] == jnp.arange(GROUPS)[:, None]
    masks = []
    for l in range(LAYERS):
        heads_on = lax.dynamic_slice_in_dim(head_mask[0, l], member * LOCAL_HEADS, LOCAL_HEADS, 1)
        heads_on = jnp.pad(heads_on.astype(BF16), ((0, 0), (0, LANES - LOCAL_HEADS)))
        groups_on = dot(group_mask[0, l].astype(BF16), spread.astype(BF16))
        groups_on = jnp.pad(groups_on, ((1, 0), (0, 0)))
        active = jnp.stack(
            [lax.dynamic_slice_in_dim(groups_on, blocks[j], 2) for j in range(TP)]
        )
        keeping = skip_mask[0, l].astype(F32)[:, None] * living
        masks.append((dot(onehot, heads_on), active, keeping))

    stream = hidden_in[0].astype(F32)
    records, weights = [], []
    forward_slow = []
    for l in range(LAYERS):
        events, pieces = {}, []
        if l + 1 < LAYERS:
            pack = after(attention_packs[l + 1], w_joint)
            pieces = gather_planes(pack) if compact() else gather_slow(pack)
        if l == 0 and compact():
            first_others = [exchange(after(forward_first[0], w_joint), TP)]
            events["normed_one"] = normed_events
            events["far_one"] = [forward_first[1]]
            events["halos"] = [forward_first[2]]
            events["mixed"] = [forward_first[3], first_others[0]]

        def hold(name, value, *more, events=events, l=l, pieces=pieces):
            if l == 0 and compact() and name == "halos":
                first_others.extend(exchange(after(p, value), TP) for p in forward_first[1:])
                events["branch"] = first_others[1:3]
            if l + 1 < LAYERS:
                if name == "halos":
                    held = after((expand_weight[l + 1], reduce_weight[l + 1]), value)
                    forward = pack_forward(*held)
                    forward_slow.append(gather_slow(forward))
                    events["mixed"] = events.get("mixed", []) + [forward]
                if name == "branch" and compact():
                    events["branch"] = events.get("branch", []) + pieces[1:2]
                    pieces.extend([exchange(piece, TP) for piece in pieces])
                    events["far_two"] = pieces[2:6]
                if name == "far_two":
                    following.append(open_attention(pieces))
                    events["feedout"] = following
            return after(value, *more, *events.get(name, []))

        def open_here(mine, l=l):
            if l == 0:
                return open_forward(forward_first + first_others if compact() else forward_first)
            return open_forward(forward_slow[l - 1])

        following = []
        stream, record, used = layer_forward(
            stream, mods[l], w_joint, project_columns, open_here, masks[l], context, hold, l > 0
        )
        records.append(record)
        weights.append(used)
        if following:
            w_joint, project_columns = following[0]
    final_state = stream.astype(BF16)[None]
    adjoint = cotangent[0].astype(F32)
    grads, d_mods = [None] * LAYERS, [None] * LAYERS
    waiting = None
    for l in reversed(range(LAYERS)):
        state = {}

        def hold(name, value, *more, waiting=waiting, state=state):
            events = []
            if waiting is not None:
                above, pieces, forward_sum = waiting
                steps = ["far_feed", "d_normed_two", "d_branch", "d_mixed"]
                if compact() and name in steps:
                    step = steps.index(name)
                    state["sum"] = owner_sum(pieces, step, state.get("sum"))
                    events.append(state["sum"])
                if name == "d_branch":
                    state["forward"] = tuple(return_forward(forward_sum))
                    events.append(state["forward"])
                if name == "d_joint":
                    owned = state["sum"] if compact() else owner_sum_slow(pieces)
                    state["attention"] = return_attention(owned)
                    grads[above] = state["attention"] + state["forward"]
                    events.append(state["attention"])
            return after(value, *more, *events)

        adjoint, d_mods[l], pieces, forward_sum = layer_backward(
            adjoint, records[l], mods[l], weights[l], masks[l], context, l == 0, hold
        )
        waiting = (l, pieces, forward_sum)
    _, pieces, forward_sum = waiting
    if compact():
        owned = None
        for step in range(4):
            owned = owner_sum(pieces, step, owned)
    else:
        owned = owner_sum_slow(pieces)
    grads[0] = return_attention(owned) + tuple(return_forward(forward_sum))

    d_mod = jnp.stack(d_mods, axis=1)
    d_mod = d_mod[1] + shifted(d_mod[0], -1)
    d_mod = jnp.transpose(d_mod.reshape(LAYERS, seq, 6 * D // seq), (1, 0, 2))
    d_mod = jnp.broadcast_to(d_mod[None], (planes,) + d_mod.shape)
    d_mod = d_mod.reshape((planes * seq,) + d_mod.shape[2:])
    d_mod = lax.all_to_all(d_mod, EVERY, 0, 0, tiled=True)
    modulation_grad = jnp.stack(
        [
            lax.dot_general(
                condition.astype(F32),
                d_mod[:, l],
                (((0,), (0,)), ((), ())),
                precision=HIGH,
                preferred_element_type=F32,
            )
            for l in range(LAYERS)
        ]
    )
    joint_grad, project_grad, expand_grad, reduce_grad = [
        jnp.stack([grads[l][i] for l in range(LAYERS)]) for i in range(4)
    ]
    return (
        final_state,
        adjoint[None],
        modulation_grad,
        joint_grad,
        project_grad,
        expand_grad,
        reduce_grad,
    )


def solution(mesh):
    planes, seq = mesh.shape["dp"], mesh.shape["seq"]
    mesh = Mesh(mesh.devices.reshape(planes, seq // TP, TP), EVERY)
    in_specs = (
        P("dp", SEQ, None),
        P("dp", None),
        P("dp", None),
        P("dp", None, None, None),
        P("dp", None, None, None),
        P("dp", None, SEQ),
        P(None, "dp", SEQ),
        P(None, "dp", SEQ),
        P(None, "dp", SEQ),
        P(None, "dp", SEQ),
        P(None, "dp", SEQ),
        P("dp", SEQ, None),
    )
    out_specs = (
        P("dp", SEQ, None),
        P("dp", SEQ, None),
        P(None, "dp", SEQ),
        P(None, "dp", SEQ),
        P(None, "dp", SEQ),
        P(None, "dp", SEQ),
        P(None, "dp", SEQ),
    )
    return jax.shard_map(shards, mesh=mesh, in_specs=in_specs, out_specs=out_specs, check_vma=False)
```
